512 devices in a mesh: sub: 64 (over y, z), grp: 8 (over x, core).
Axes of the slice: x: 4, y: 4, z: 16, core: 2. Of those that a mesh axis runs over, the one named last changes fastest.
Arguments:
- schur_inverse: bfloat16 [64, 8, 1024, 1024], P('sub', 'grp'), may hold values from -1 to 4, as said below
- schur: bfloat16 [64, 8, 1024, 1024], P('sub', 'grp'), may hold values from -1 to 4, as said below
- coarse_basis: float32 [64, 8, 8, 1024], P('sub', 'grp'), may hold values from -0.6 to 0.6
- corner_index: int32 [64, 8, 8], P('sub', 'grp'), may hold values from 0 to 255
- coarse_inverse: float32 [256, 256], replicated, may hold values from -1 to 4, as said below
- neighbor_map: int32 [64, 8, 512], P('sub', 'grp'), may hold values from 0 to 511, each once within a row
- load: float32 [64, 8, 1024, 32], P('sub', 'grp'), may hold values from -6 to 6
- previous: bfloat16 [64, 8, 1024, 256], P('sub', 'grp'), may hold values from -7 to 7
- mass: float32 [64, 8, 1024], P('sub', 'grp'), may hold values from 0.5 to 2
Outputs:
- new_block: float32 [64, 8, 1024, 32], P('sub', 'grp')
- multipliers: float32 [64, 8, 512, 32], P('sub', 'grp')
- coefficients: float32 [256, 32], replicated
- factor: float32 [32, 32], replicated
The draws below stay inside these ranges and needn't reach their ends.
Inputs may be any that keep to these rules, and one draw needn't show every extreme that they name: `corner_index`: each subdomain's 8 corners name coarse dofs. `neighbor_map`: each row is a permutation of the 512 multiplier numbers. `schur_inverse`: each block is symmetric positive definite. `schur`: each block is symmetric positive definite. `coarse_inverse`: symmetric positive definite.
All inputs are finite; a program needn't handle non-finite values.
Results may differ from the reference program's by a relative error of at most 0.005.
Values sent between devices are 32-bit elements; how exact they have to be, the bound alone decides.
No kernel may reach another device: no remote copies, remote signals or barrier semaphores. Data moves between devices by JAX's collectives and lax.ppermute only.
A program may use at most 64 MiB of HBM per device.

```python
import math
import jax
import jax.numpy as jnp
from jax import lax

BD = 1024
K = 32
NCL = 8
NCG = 256
ITERS = 3
NPREV = 8
FACE = 512
ROWS = 524288
N_SUB = 64
N_GRP = 8


def spd_blocks(key, shape, order, low, high):
    key_diag, key_off = jax.random.split(key)
    diagonal = jax.random.uniform(key_diag, shape[:-1], jnp.float32, low, high)
    spread = 0.8 / math.sqrt(order)
    offdiag = jax.random.uniform(key_off, shape, jnp.float32, -spread, spread)
    symmetric = (offdiag + jnp.swapaxes(offdiag, -1, -2)) * 0.7071
    rows = lax.broadcasted_iota(jnp.int32, shape, len(shape) - 2)
    cols = lax.broadcasted_iota(jnp.int32, shape, len(shape) - 1)
    identity = (rows == cols).astype(jnp.float32)
    return symmetric * (1.0 - identity) + identity * diagonal[..., None]


def shared_base(key):
    return jax.random.truncated_normal(key, -4.0, 4.0, (N_SUB, N_GRP, BD, K), jnp.float32)


def draw_schur_inverse(key, part):
    key = jax.random.fold_in(key, 1)
    blocks = spd_blocks(key, (N_SUB, N_GRP, BD, BD), BD, 1.5, 3.0)
    return blocks.astype(jnp.bfloat16)


def draw_schur(key, part):
    key = jax.random.fold_in(key, 2)
    blocks = spd_blocks(key, (N_SUB, N_GRP, BD, BD), BD, 1.5, 3.0)
    return blocks.astype(jnp.bfloat16)


def draw_coarse_inverse(key, part):
    key = jax.random.fold_in(key, 3)
    return spd_blocks(key, (NCG, NCG), NCG, 1.2, 2.5)


def draw_load(key, part):
    base = shared_base(key)
    key = jax.random.fold_in(key, 4)
    noise = jax.random.truncated_normal(key, -4.0, 4.0, base.shape, jnp.float32)
    return base + 0.5 * noise


def draw_previous(key, part):
    base = shared_base(key)
    key = jax.random.fold_in(key, 5)
    shape = (N_SUB, N_GRP, BD, NPREV * K)
    noise = jax.random.truncated_normal(key, -4.0, 4.0, shape, jnp.float32)
    common = 0.7
    return (common * jnp.tile(base, (1, 1, 1, NPREV)) + noise).astype(jnp.bfloat16)


def set_ends(values, key, smallest, high):
    extent = values.shape
    place = [jax.random.randint(jax.random.fold_in(key, axis), (), 0, extent[axis]) for axis in range(len(extent))]
    values = values.at[tuple(place)].set(smallest)
    longest = extent.index(max(extent))
    place[longest] = (place[longest] + 1) % extent[longest]
    return values.at[tuple(place)].set(high)


def block_levels(own_key, extent, cuts, smallest, top_value):
    def one(dim, blocks):
        heights = jax.random.uniform(jax.random.fold_in(jax.random.fold_in(own_key, 6), dim), (blocks,), jnp.float32, smallest / len(cuts), top_value / len(cuts))
        return jnp.repeat(jnp.exp(heights), extent[dim] // blocks).reshape((-1,) + (1,) * (len(extent) - dim - 1))

    loudness = one(*cuts[0])
    for cut in cuts[1:]:
        loudness = loudness * one(*cut)
    return loudness


def gaussian(stream_key, extent, deviation, most, shards=(), held_as=jnp.bfloat16):
    values = deviation * jax.random.normal(stream_key, extent, jnp.float32)
    if shards:
        values = values * block_levels(stream_key, extent, shards, -0.22, 0.18)
    return jnp.clip(values, -most, most).astype(held_as)


def setup_inputs(seed: int = 0) -> dict:
    key_list = jax.random.split(jax.random.key(seed), 10)
    return {
        "schur_inverse": draw_schur_inverse(jax.random.fold_in(key_list[9], 71), 0),
        "schur": draw_schur(jax.random.fold_in(key_list[9], 71), 0),
        "coarse_basis": gaussian(key_list[2], (N_SUB, N_GRP, NCL, BD), 0.1, 0.6, ((0, 64), (1, 8)), jnp.float32),
        "corner_index": set_ends(jax.random.randint(key_list[3], (N_SUB, N_GRP, NCL), 0, NCG), jax.random.fold_in(key_list[3], 1), 0, NCG - 1).astype(jnp.int32),
        "coarse_inverse": draw_coarse_inverse(jax.random.fold_in(key_list[9], 71), 0),
        "neighbor_map": jax.vmap(lambda own: jax.random.permutation(own, FACE))(jax.random.split(key_list[5], N_SUB * N_GRP)).reshape((N_SUB, N_GRP, FACE)).astype(jnp.int32),
        "load": draw_load(jax.random.fold_in(key_list[9], 71), 0),
        "previous": draw_previous(jax.random.fold_in(key_list[9], 71), 0),
        "mass": jnp.clip(jnp.exp(math.log(2.0) - 1.3862944 * jax.random.uniform(key_list[8], (N_SUB, N_GRP, BD), jnp.float32) ** block_levels(key_list[8], (N_SUB, N_GRP, BD), ((0, 64), (1, 8)), -0.2, 0.2)), 0.5, 2.0),
    }


HI = lax.Precision.HIGHEST

def local_products(blocks, vectors):
    flat_blocks = blocks.reshape((-1,) + blocks.shape[2:])
    flat_vectors = vectors.reshape((-1,) + vectors.shape[2:])
    result = lax.map(lambda pair: jnp.dot(pair[0].astype(jnp.float32), pair[1].astype(jnp.float32), preferred_element_type=jnp.float32), (flat_blocks, flat_vectors))
    return result.reshape(vectors.shape[:2] + result.shape[1:])

def jump_transpose(lam, neighbor_map):
    before = jnp.concatenate([jnp.zeros_like(lam[:1]), lam[:-1]], axis=0)
    left_face = -jnp.take_along_axis(before, neighbor_map[..., None], axis=2)
    return jnp.concatenate([left_face, lam], axis=2)

def jump(field, neighbor_map):
    face = neighbor_map.shape[2]
    inverse_map = jnp.argsort(neighbor_map, axis=-1).astype(jnp.int32)
    send = jnp.take_along_axis(field[:, :, :face], inverse_map[..., None], axis=2)
    after = jnp.concatenate([send[1:], jnp.zeros_like(send[:1])], axis=0)
    active = (jnp.arange(field.shape[0]) < field.shape[0] - 1).astype(jnp.float32)[:, None, None, None]
    return (field[:, :, face:] - after) * active

def apply_inverse(t, schur_inverse, coarse_basis, corner_index, coarse_inverse):
    local = local_products(schur_inverse, t.astype(jnp.bfloat16))
    corner_terms = jnp.einsum('sgcr,sgrk->sgck', coarse_basis, t, precision=HI)
    coarse_rhs = jax.ops.segment_sum(corner_terms.reshape(-1, t.shape[-1]), corner_index.reshape(-1), num_segments=coarse_inverse.shape[0])
    coarse = jnp.dot(coarse_inverse, coarse_rhs, precision=HI)
    return local + jnp.einsum('sgcr,sgck->sgrk', coarse_basis, coarse[corner_index], precision=HI)

def reference(schur_inverse, schur, coarse_basis, corner_index, coarse_inverse, neighbor_map, load, previous, mass):

    def solve(t):
        return apply_inverse(t, schur_inverse, coarse_basis, corner_index, coarse_inverse)

    def dual(p):
        return jump(solve(jump_transpose(p, neighbor_map)), neighbor_map)

    def precondition(r):
        spread = 0.5 * jump_transpose(r, neighbor_map)
        return 0.5 * jump(local_products(schur, spread.astype(jnp.bfloat16)), neighbor_map)

    def column_dot(a, b):
        return jnp.sum(a * b, axis=(0, 1, 2))
    rhs = jump(solve(load), neighbor_map)
    lam = jnp.zeros_like(rhs)
    resid = rhs
    precond = precondition(resid)
    direction = precond
    rz = column_dot(resid, precond)
    for step in range(ITERS):
        image = dual(direction)
        alpha = rz / column_dot(direction, image)
        lam = lam + alpha * direction
        resid = resid - alpha * image
        if step + 1 < ITERS:
            precond = precondition(resid)
            rz_next = column_dot(resid, precond)
            direction = precond + rz_next / rz * direction
            rz = rz_next
    primal = solve(load - jump_transpose(lam, neighbor_map))
    weights = mass[..., None] / ROWS
    basis = previous.astype(jnp.float32)
    first = jnp.einsum('sgrc,sgrk->ck', basis, weights * primal, precision=HI)
    projected = primal - jnp.einsum('sgrc,ck->sgrk', basis, first, precision=HI)
    second = jnp.einsum('sgrc,sgrk->ck', basis, weights * projected, precision=HI)
    coefficients = first + second
    final = primal - jnp.einsum('sgrc,ck->sgrk', basis, coefficients, precision=HI)
    gram_block = jnp.einsum('sgrc,sgrk->ck', final, weights * final, precision=HI)
    lower = jnp.linalg.cholesky(gram_block)
    flat = final.reshape(-1, final.shape[-1])
    solved = lax.linalg.triangular_solve(lower, flat, left_side=False, lower=True, transpose_a=True)
    return (solved.reshape(final.shape), lam, coefficients, lower)
```

```python
import jax
import jax.numpy as jnp
import numpy as np
from jax import lax
from jax.experimental import pallas as pl
from jax.experimental.pallas import tpu as pltpu
from jax.sharding import Mesh, PartitionSpec as P

HI = lax.Precision.HIGHEST
F32 = jnp.float32
BF16 = jnp.bfloat16
RED = ("y", "x", "c")
LEVELS = 6
LANE = 128


def nn(a, b):
    return jnp.dot(a, b, precision=HI, preferred_element_type=F32)


def nt(a, b):
    return lax.dot_general(
        a, b, (((1,), (1,)), ((), ())), precision=HI, preferred_element_type=F32
    )


def lane_sum(a):
    return jnp.sum(a, axis=1, keepdims=True)


def call(kernel, outs, scratch=()):
    return pl.pallas_call(
        kernel,
        out_shape=outs,
        scratch_shapes=list(scratch),
        compiler_params=pltpu.CompilerParams(vmem_limit_bytes=48 * 1024 * 1024),
    )


def split_dot(t, mat):
    high = t.astype(BF16).astype(F32)
    both = jnp.concatenate([high, t - high], axis=0).astype(BF16)
    wide = jnp.dot(both, mat, preferred_element_type=F32)
    rows = t.shape[0]
    return wide[:rows] + wide[rows:]


def to_order(nm_col, face):
    return (nm_col == lax.broadcasted_iota(jnp.int32, (face, face), 1)).astype(F32)


def from_order(nm_row, face):
    return (nm_row == lax.broadcasted_iota(jnp.int32, (face, face), 0)).astype(F32)


def start_kernel(inv_ref, load_ref, basis_ref, nm_ref, corner_ref, sl_ref, sr_ref, cl_ref):
    face = nm_ref.shape[0]
    cols = load_ref.shape[1]
    corners = basis_ref.shape[0]
    rows = cols + corners
    load = jnp.transpose(load_ref[...])
    basis = basis_ref[...]
    order = to_order(nm_ref[...], face)
    wide = split_dot(load, inv_ref[...])
    left = nn(jnp.concatenate([wide[:, :face], basis[:, :face]], axis=0), order)
    sl_ref[0:rows, :] = left
    sr_ref[0:cols, :] = wide[:, face:]
    sr_ref[cols:rows, :] = basis[:, face:]
    for ref in (sl_ref, sr_ref):
        ref[rows : rows + 8, :] = jnp.zeros((8, face), F32)
        ref[rows : rows + 1, 0:corners] = corner_ref[...].astype(F32)
    cl_ref[...] = nt(load, basis)


def order_kernel(inv_ref, schur_ref, prev_ref, nm_col_ref, nm_row_ref, mass_ref,
                 inv_out, schur_out, prev_out, mass_out, *, total):
    face = nm_col_ref.shape[0]
    order32 = to_order(nm_col_ref[...], face)
    order = order32.astype(BF16)
    back = from_order(nm_row_ref[...], face).astype(BF16)
    for src, dst in ((inv_ref, inv_out), (schur_ref, schur_out)):
        dst[:, face:] = src[:, face:]
        dst[:, :face] = jnp.dot(src[:, :face], order, preferred_element_type=F32).astype(BF16)
        dst[:face, :] = jnp.dot(back, dst[:face, :], preferred_element_type=F32).astype(BF16)
    prev_out[face:, :] = prev_ref[face:, :]
    prev_out[:face, :] = jnp.dot(back, prev_ref[:face, :], preferred_element_type=F32).astype(BF16)
    mass = mass_ref[...] / total
    mass_out[:, face:] = mass[:, face:]
    mass_out[:, :face] = nn(jnp.broadcast_to(mass[:, :face], (8, face)), order32)[0:1]


def step_kernel(sl_ref, sr_ref, nl_ref, pr_ref, mask_ref, mat_ref, t_ref, ol_ref, or_ref,
                *, cols, width, scale):
    face = sl_ref.shape[1]
    new = width + 16
    rows = cols + new
    old = cols + width
    for lanes, own, other, shift in (
        (slice(0, face), sl_ref, pr_ref, 0),
        (slice(face, 2 * face), sr_ref, nl_ref, 16),
    ):
        keep = mask_ref[0:1, lanes]
        t_ref[0:cols, lanes] = (own[0:cols, :] - other[0:cols, :]) * keep
        edge = jnp.zeros((8, face), F32)
        mine = jnp.concatenate([edge, own[cols:old, :], edge], axis=0)
        blank = jnp.zeros((16, face), F32)
        theirs = other[cols:old, :]
        theirs = jnp.concatenate([theirs, blank] if shift == 0 else [blank, theirs], axis=0)
        t_ref[cols:rows, lanes] = (mine - theirs) * keep
    v = split_dot(t_ref[...], mat_ref[...])
    if scale != 1.0:
        v = v * scale
    ids = jnp.concatenate(
        [
            pr_ref[old : old + 8, 0:8],
            sl_ref[old : old + 8, 0:width],
            nl_ref[old : old + 8, width - 8 : width],
        ],
        axis=1,
    )
    for ref, lanes in ((ol_ref, slice(0, face)), (or_ref, slice(face, 2 * face))):
        ref[0:rows, :] = v[:, lanes]
        ref[rows : rows + 8, :] = jnp.zeros((8, face), F32)
        ref[rows : rows + 8, 0:new] = ids


def one_hot(ids, count):
    dof = lax.broadcasted_iota(jnp.int32, (count, ids.shape[1]), 0).astype(F32)
    return (ids == dof).astype(F32)


def pack(ref, at, matrix):
    half = matrix.shape[0] // 2
    ref[at : at + half, :] = matrix[:half, :half]
    ref[at + half : at + 2 * half, :] = matrix[half:, :half]
    ref[at + 2 * half : at + 3 * half, :] = matrix[half:, half:]


def unpack(ref, at):
    half = LANE
    a = ref[at : at + half, :]
    b = ref[at + half : at + 2 * half, :]
    c = ref[at + 2 * half : at + 3 * half, :]
    return jnp.concatenate(
        [jnp.concatenate([a, jnp.transpose(b)], axis=1), jnp.concatenate([b, c], axis=1)], axis=0
    )


def moment_kernel(sl0_ref, cl_ref, gram_ref, *refs, cols, count):
    out = refs[-1]
    half = count // 2
    tri = 3 * half

    def put(at, block):
        out[at : at + cols, :] = block[:, :half]
        out[at + cols : at + 2 * cols, :] = block[:, half:]

    base = 4 * tri
    own = sl0_ref.shape[0] - cols - 8
    put(base, nt(cl_ref[...], one_hot(sl0_ref[cols + own : cols + own + 1, 0:own], count)))
    sums = []
    for k in range(3):
        t_ref, l_ref, r_ref = refs[3 * k : 3 * k + 3]
        rows, double = t_ref.shape
        face = double // 2
        width = rows - cols
        spot = one_hot(l_ref[rows : rows + 1, 0:width], count)
        tl, tr = t_ref[cols:rows, :face], t_ref[cols:rows, face:]
        inner = nt(tl, l_ref[cols:rows, :]) + nt(tr, r_ref[cols:rows, :])
        pack(out, k * tri, nt(nn(spot, inner), spot))
        cross = nt(l_ref[0:cols, :], tl) + nt(r_ref[0:cols, :], tr)
        put(base + 2 * cols * (k + 1), nt(cross, spot))
        sums.append(
            lane_sum(t_ref[0:cols, :face] * l_ref[0:cols, :])
            + lane_sum(t_ref[0:cols, face:] * r_ref[0:cols, :])
        )
    pack(out, 3 * tri, gram_ref[...])
    at = base + 8 * cols
    out[at:, :] = jnp.zeros((out.shape[0] - at, LANE), F32)
    lane = lax.broadcasted_iota(jnp.int32, (cols, LANE), 1)
    block = jnp.zeros((cols, LANE), F32)
    for k in range(3):
        block = jnp.where(lane == k, sums[k], block)
    out[at : at + cols, :] = block


def combine_kernel(sums_ref, coarse_ref, ids_ref, mass_ref, prev_ref, *refs, cols, count):
    half = count // 2
    tri = 3 * half
    base = 4 * tri
    sl0, sr0 = refs[0:2]
    level = [None] + [refs[2 + 3 * k : 5 + 3 * k] for k in range(LEVELS)]
    out_ref, field_ref, dual_ref, scal_ref = refs[2 + 3 * LEVELS :]
    face = sl0.shape[1]

    def get(at):
        return jnp.concatenate([sums_ref[at : at + cols, :], sums_ref[at + cols : at + 2 * cols, :]], axis=1)

    m0, m1, m2 = (unpack(sums_ref, k * tri) for k in range(3))
    coarse = coarse_ref[...]
    c_load, w0x, w1x, w2x = (get(base + 2 * cols * k) for k in range(4))
    at = base + 8 * cols
    s0, s1, s2 = (sums_ref[at : at + cols, k : k + 1] for k in range(3))
    g0 = nn(c_load, coarse)
    m0g0, m1g0, m2g0 = nn(g0, m0), nn(g0, m1), nn(g0, m2)
    c0 = w0x + m0g0
    g1 = nn(c0, coarse)
    m0g1, m1g1 = nn(g1, m0), nn(g1, m1)
    rz0 = s0 + lane_sum(2.0 * w0x * g0 + g0 * m0g0)
    del0 = s1 + lane_sum(2.0 * w1x * g0 + g0 * m1g0 + c0 * g1)
    nu0 = s2 + lane_sum(2.0 * w2x * g0 + g0 * m2g0 + 2.0 * w1x * g1 + 2.0 * g1 * m1g0 + g1 * m0g1)
    al0 = rz0 / del0
    be1 = (rz0 - 2.0 * al0 * del0 + al0 * al0 * nu0) / rz0
    cz1 = c0 - al0 * (w1x + m1g0 + m0g1)
    gz1 = nn(cz1, coarse)
    cm = (
        (1.0 + be1) * (w1x + m1g0)
        - al0 * (m1g1 + w2x + m2g0)
        + nn(gz1, m0)
        + be1 * m0g1
    )
    gm = nn(cm, coarse)
    spot = one_hot(ids_ref[0:1, :], count)
    local = nn(jnp.concatenate([g0, g1, gz1, gm], axis=0), spot)

    def coef(k, n):
        width = 8 * (2 * k + 1)
        first = 8 * (LEVELS - k)
        return local[: n * cols, first : first + width]

    def spread(k, ref, n, lanes):
        width = 8 * (2 * k + 1)
        wide = nn(coef(k, n), ref[cols : cols + width, lanes])
        return [wide[i * cols : (i + 1) * cols] for i in range(n)]

    def fields(b2, b4, b6, lanes):
        x2, x4, x6 = (b[0:cols, lanes] for b in (b2, b4, b6))
        p20, p21, p2z = spread(2, b2, 3, lanes)
        p40, p41 = spread(4, b4, 2, lanes)
        (p60,) = spread(6, b6, 1, lanes)
        z0 = x2 + p20
        n0 = x4 + p40 + p21
        z1 = z0 - al0 * n0
        n1 = x4 + p40 - al0 * (x6 + p60 + p41) + p2z
        return z0, z1, n1 + be1 * n0

    left, right, whole = slice(0, face), slice(face, 2 * face), slice(0, face)
    t1, t2, t3, t4, t5, t6 = (level[k][0] for k in range(1, 7))
    z0, z1, m = fields(t2, t4, t6, right)
    _, _, m_left = fields(t2, t4, t6, left)
    p10, p11, p1z = spread(1, t1, 3, right)
    p30, p31 = spread(3, t3, 2, right)
    (p50,) = spread(5, t5, 1, right)
    x1, x3, x5 = (ref[0:cols, right] for ref in (t1, t3, t5))
    d = x1 + p10
    w0 = x3 + p30 + p11
    w1 = x3 + p30 - al0 * (x5 + p50 + p31) + p1z
    r1 = d - al0 * w0
    q1 = w1 + be1 * w0
    p1 = z1 + be1 * z0
    for side, (own, pos, lanes) in enumerate(((sl0, 1, left), (sr0, 2, right))):
        u = fields(level[2][pos], level[4][pos], level[6][pos], whole)
        corner = spread(0, own, 4, whole)
        field_ref[0:cols, lanes] = own[0:cols, :] + corner[0]
        for i in range(3):
            field_ref[(i + 1) * cols : (i + 2) * cols, lanes] = u[i] + corner[i + 1]
        mu = lane_sum((m if side else m_left) * u[2])
        mm = mu if side == 0 else mm + mu
    for i, item in enumerate((z0, z1, m)):
        dual_ref[i * cols : (i + 1) * cols, :] = item
    moments = (
        lane_sum(r1 * z1), lane_sum(r1 * m), lane_sum(q1 * z1), lane_sum(q1 * m),
        lane_sum(r1 * p1), lane_sum(p1 * q1), lane_sum(z1 * w1), lane_sum(m * w1), mm,
    )
    lane = lax.broadcasted_iota(jnp.int32, (cols, LANE), 1)
    block = jnp.zeros((cols, LANE), F32)
    for k, item in enumerate(moments):
        block = jnp.where(lane == k, item, block)
    field = field_ref[...]
    scaled = field * mass_ref[...]
    tq = nn(scaled, prev_ref[...].astype(F32))
    out_ref[0 : 4 * cols, :] = tq[:, :half]
    out_ref[4 * cols : 8 * cols, :] = tq[:, half:]
    out_ref[8 * cols : 12 * cols, :] = nt(scaled, field)
    out_ref[12 * cols : 13 * cols, :] = block
    out_ref[13 * cols :, :] = jnp.zeros((out_ref.shape[0] - 13 * cols, LANE), F32)
    block = jnp.zeros((cols, LANE), F32)
    for k, item in enumerate((al0, be1, lane_sum(cm * gm))):
        block = jnp.where(lane == k, item, block)
    scal_ref[...] = block


def final_kernel(sums_ref, early_ref, scal_ref, field_ref, dual_ref, prev_ref, nm_ref,
                 block_ref, multi_ref, coef_ref, factor_ref, *, cols, count):
    half = count // 2
    tri = 3 * half
    face = dual_ref.shape[1]
    at = 12 * cols
    r1z1, r1m, q1z1, q1m, r1p1, p1q1, z1w1, mw1, mm = (
        sums_ref[at : at + cols, k : k + 1] for k in range(9)
    )
    al0, be1, extra = (scal_ref[:, k : k + 1] for k in range(3))
    mfm = mm + extra
    al1 = r1p1 / p1q1
    z2q1 = q1z1 - al1 * q1m
    be2 = -z2q1 / p1q1
    rz2 = r1z1 - al1 * (r1m + q1z1) + al1 * al1 * q1m
    z2fz2 = z1w1 - 2.0 * al1 * mw1 + al1 * al1 * mfm
    al2 = rz2 / (z2fz2 + 2.0 * be2 * z2q1 + be2 * be2 * p1q1)
    along = al1 + al2 * be2
    parts = (al0 + along * be1, along + al2, -al1 * al2)
    multi = sum(y * dual_ref[i * cols : (i + 1) * cols, :] for i, y in enumerate(parts))
    multi_ref[...] = jnp.transpose(multi)
    weights = [jnp.ones((cols, 1), F32)] + [-y for y in parts]
    primal = sum(y * field_ref[i * cols : (i + 1) * cols, :] for i, y in enumerate(weights))
    g1 = sum(
        y
        * jnp.concatenate(
            [sums_ref[i * cols : (i + 1) * cols, :], sums_ref[(4 + i) * cols : (5 + i) * cols, :]],
            axis=1,
        )
        for i, y in enumerate(weights)
    )
    row = lax.broadcasted_iota(jnp.int32, (cols, cols), 0)
    col = lax.broadcasted_iota(jnp.int32, (cols, cols), 1)
    eye = (row == col).astype(F32)
    across = [jnp.sum(y * eye, axis=0, keepdims=True) for y in weights]
    gram = jnp.zeros((cols, cols), F32)
    for i in range(4):
        for j in range(4):
            tile = sums_ref[(8 + i) * cols : (9 + i) * cols, j * cols : (j + 1) * cols]
            gram = gram + weights[i] * tile * across[j]
    basis = unpack(early_ref, 3 * tri)
    c = 2.0 * g1 - nn(g1, basis)
    coef_ref[...] = jnp.transpose(c)
    gram = gram - nt(c, g1) - nt(g1, c) + nt(nn(c, basis), c)
    gram = 0.5 * (gram + jnp.transpose(gram))
    final = primal - nt(c, prev_ref[...].astype(F32))
    work = jnp.concatenate([gram, eye], axis=1)
    index = lax.broadcasted_iota(jnp.int32, (cols, 1), 0)
    pivots = jnp.zeros((cols, 1), F32)
    for k in range(cols):
        pivot = work[k : k + 1, k : k + 1]
        pivots = jnp.where(index == k, pivot, pivots)
        times = jnp.where(index > k, work[:, k : k + 1], 0.0) / pivot
        work = work - times * work[k : k + 1, :]
    work = work / jnp.sqrt(pivots)
    factor_ref[...] = jnp.transpose(jnp.where(row <= col, work[:, :cols], 0.0))
    solved = nn(work[:, cols:], final)
    left = nn(solved[:, :face], from_order(nm_ref[...], face))
    block_ref[:face, :] = jnp.transpose(left)
    block_ref[face:, :] = jnp.transpose(solved[:, face:])


def over_all(rows, n_red, n_z):
    part = rows.shape[0] // n_red
    mine = lax.all_to_all(rows.reshape(n_red, part, LANE), RED, 0, 0, tiled=True)
    mine = jnp.sum(mine, axis=0)
    peers = lax.all_to_all(jnp.broadcast_to(mine[None], (n_z, part, LANE)), "z", 0, 0, tiled=True)
    mine = jnp.sum(peers, axis=0)
    full = lax.all_to_all(jnp.broadcast_to(mine[None], (n_red, part, LANE)), RED, 0, 0, tiled=True)
    return full.reshape(n_red * part, LANE)


def up(count, unit):
    return -(-count // unit) * unit


def solution(mesh):
    n_sub, n_grp = mesh.shape["sub"], mesh.shape["grp"]
    n_y = min(4, n_sub)
    n_z = n_sub // n_y
    n_c = 2
    n_x = n_grp // n_c
    fine = Mesh(np.asarray(mesh.devices).reshape(n_y, n_z, n_x, n_c), ("y", "z", "x", "c"))
    n_red = n_y * n_x * n_c
    along = ("y", "z")
    ahead = [(i, i + 1) for i in range(n_sub - 1)]
    behind = [(i + 1, i) for i in range(n_sub - 1)]

    def on_device(schur_inverse, schur, coarse_basis, corner_index, coarse_inverse, neighbor_map,
                  load, previous, mass):
        inverse_block, schur_block, basis = schur_inverse[0, 0], schur[0, 0], coarse_basis[0, 0]
        corners, nm = corner_index[0, 0], neighbor_map[0, 0]
        rhs, earlier, weights = load[0, 0], previous[0, 0], mass[0, 0]
        rows, cols = rhs.shape
        face = nm.shape[0]
        count = coarse_inverse.shape[0]
        total = rows * n_sub * n_grp
        own = corners.shape[0]
        position = lax.axis_index(along)
        nm_row, nm_col = nm[None, :], nm[:, None]
        side = jnp.arange(2 * face) < face
        mask = jnp.where(side, position > 0, position < n_sub - 1).astype(F32)[None, :]
        mask = jnp.broadcast_to(mask, (8, 2 * face))

        def shape(*dims):
            return jax.ShapeDtypeStruct(dims, F32)

        sl, sr, cl = call(
            start_kernel, (shape(cols + own + 8, face), shape(cols + own + 8, face), shape(cols, own))
        )(inverse_block, rhs, basis, nm_col, corners[None, :])
        inv_p, schur_p, prev_p, mass_p = call(
            lambda *refs: order_kernel(*refs, total=total),
            (
                jax.ShapeDtypeStruct((rows, rows), BF16),
                jax.ShapeDtypeStruct((rows, rows), BF16),
                jax.ShapeDtypeStruct(earlier.shape, BF16),
                shape(1, rows),
            ),
        )(inverse_block, schur_block, earlier, nm_col, nm_row, weights[None, :])
        wide = earlier.astype(F32)
        gram = jnp.dot(wide.T, (weights / total)[:, None] * wide, precision=HI)

        chain = [sl, sr]
        width = own
        for k in range(1, LEVELS + 1):
            nl = lax.ppermute(sl, along, behind)
            pr = lax.ppermute(sr, along, ahead)
            odd = k % 2 == 1
            out = cols + width + 16
            t, sl, sr = call(
                lambda *refs, width=width, odd=odd: step_kernel(
                    *refs, cols=cols, width=width, scale=0.25 if odd else 1.0
                ),
                (shape(out, 2 * face), shape(out + 8, face), shape(out + 8, face)),
            )(sl, sr, nl, pr, mask, schur_p if odd else inv_p)
            chain += [t, sl, sr]
            width += 16
            if k == 3:
                size = up(6 * count + 9 * cols, 8 * n_red)
                first = call(
                    lambda *refs: moment_kernel(*refs, cols=cols, count=count), shape(size, LANE)
                )(chain[0], cl, gram, *chain[2:11])
                first = over_all(first, n_red, n_z)
        ids = sl[cols + width : cols + width + 8, :LANE]
        size = up(13 * cols, 8 * n_red)
        second, field, dual, scal = call(
            lambda *refs: combine_kernel(*refs, cols=cols, count=count),
            (shape(size, LANE), shape(4 * cols, rows), shape(3 * cols, face), shape(cols, LANE)),
        )(first, coarse_inverse, ids, mass_p, prev_p, *chain)
        second = over_all(second, n_red, n_z)
        block, multi, coefficients, factor = call(
            lambda *refs: final_kernel(*refs, cols=cols, count=count),
            (shape(rows, cols), shape(face, cols), shape(count, cols), shape(cols, cols)),
        )(second, first, scal, field, dual, prev_p, nm_row)
        return block[None, None], multi[None, None], coefficients, factor

    split = (along, ("x", "c"))
    return jax.shard_map(
        on_device,
        mesh=fine,
        in_specs=(
            P(*split, None, None),
            P(*split, None, None),
            P(*split, None, None),
            P(*split, None),
            P(),
            P(*split, None),
            P(*split, None, None),
            P(*split, None, None),
            P(*split, None),
        ),
        out_specs=(P(*split, None, None), P(*split, None, None), P(), P()),
        check_vma=False,
    )
```

```python
import jax
import jax.numpy as jnp
import numpy as np
from jax import lax
from jax.experimental import pallas as pl
from jax.experimental.pallas import tpu as pltpu
from jax.sharding import Mesh, PartitionSpec as P

HI = lax.Precision.HIGHEST
F32 = jnp.float32
BF16 = jnp.bfloat16
RED = ("y", "x", "c")
LEVELS = 6
LANE = 128


def nn(a, b):
    return jnp.dot(a, b, precision=HI, preferred_element_type=F32)


def nt(a, b):
    return lax.dot_general(
        a, b, (((1,), (1,)), ((), ())), precision=HI, preferred_element_type=F32
    )


def lane_sum(a):
    return jnp.sum(a, axis=1, keepdims=True)


def call(kernel, outs, scratch=()):
    return pl.pallas_call(
        kernel,
        out_shape=outs,
        scratch_shapes=list(scratch),
        compiler_params=pltpu.CompilerParams(vmem_limit_bytes=12 * 1024 * 1024),
    )


def split_dot(t, mat):
    high = t.astype(BF16).astype(F32)
    both = jnp.concatenate([high, t - high], axis=0).astype(BF16)
    wide = jnp.dot(both, mat, preferred_element_type=F32)
    rows = t.shape[0]
    return wide[:rows] + wide[rows:]


def to_order(nm_row, face):
    nm = jnp.transpose(jnp.broadcast_to(nm_row.astype(F32), (8, face)))[:, 0:1]
    return (nm == lax.broadcasted_iota(jnp.int32, (face, face), 1).astype(F32)).astype(F32)


def from_order(nm_row, face):
    return (nm_row == lax.broadcasted_iota(jnp.int32, (face, face), 0)).astype(F32)


def start_kernel(inv_hbm, load_hbm, basis_hbm, nm_hbm, corner_hbm, sl_ref, sr_ref, cl_ref,
                 inv_ref, load_ref, basis_ref, nm_ref, corner_ref, sems):
    pairs = (
        (nm_hbm, nm_ref), (load_hbm, load_ref), (basis_hbm, basis_ref), (corner_hbm, corner_ref),
        (inv_hbm, inv_ref),
    )
    copies = [pltpu.make_async_copy(src, dst, sems.at[i]) for i, (src, dst) in enumerate(pairs)]
    for copy in copies:
        copy.start()
    for copy in copies[:-1]:
        copy.wait()
    face = nm_ref.shape[1]
    cols = load_ref.shape[0]
    corners = basis_ref.shape[0]
    rows = cols + corners
    load = load_ref[...]
    basis = basis_ref[...]
    order = to_order(nm_ref[...], face)
    cl_ref[...] = nt(load, basis)
    for ref in (sl_ref, sr_ref):
        ref[rows : rows + 8, :] = jnp.zeros((8, face), F32)
        ref[rows : rows + 1, 0:corners] = corner_ref[...].astype(F32)
    sr_ref[cols:rows, :] = basis[:, face:]
    copies[-1].wait()
    wide = split_dot(load, inv_ref[...])
    sr_ref[0:cols, :] = wide[:, face:]
    sl_ref[0:rows, :] = nn(jnp.concatenate([wide[:, :face], basis[:, :face]], axis=0), order)


def matrix_kernel(src, nm_ref, dst):
    face = nm_ref.shape[1]
    order = to_order(nm_ref[...], face).astype(BF16)
    back = from_order(nm_ref[...], face).astype(BF16)
    dst[:, face:] = src[:, face:]
    dst[:, :face] = jnp.dot(src[:, :face], order, preferred_element_type=F32).astype(BF16)
    dst[:face, :] = jnp.dot(back, dst[:face, :], preferred_element_type=F32).astype(BF16)


def basis_kernel(prev_ref, nm_ref, mass_ref, prev_out, mass_out, gram_out, *, total):
    face = nm_ref.shape[1]
    back = from_order(nm_ref[...], face).astype(BF16)
    prev_out[face:, :] = prev_ref[face:, :]
    prev_out[:face, :] = jnp.dot(back, prev_ref[:face, :], preferred_element_type=F32).astype(BF16)
    mass = mass_ref[...] / total
    mass_out[:, face:] = mass[:, face:]
    left = jnp.broadcast_to(mass[:, :face], (8, face))
    mass_out[:, :face] = nn(left, to_order(nm_ref[...], face))[0:1]
    column = jnp.transpose(jnp.broadcast_to(mass, (8, mass.shape[1])))[:, 0:1]
    wide = prev_ref[...].astype(F32)
    gram_out[...] = lax.dot_general(
        wide * column, wide, (((0,), (0,)), ((), ())), precision=HI, preferred_element_type=F32
    )


def step_kernel(sl_ref, sr_ref, nl_ref, pr_ref, mask_ref, mat_ref, t_ref, ol_ref, or_ref,
                *, cols, width, scale):
    face = sl_ref.shape[1]
    new = width + 16
    rows = cols + new
    old = cols + width
    for lanes, own, other, shift in (
        (slice(0, face), sl_ref, pr_ref, 0),
        (slice(face, 2 * face), sr_ref, nl_ref, 16),
    ):
        keep = mask_ref[0:1, lanes]
        t_ref[0:cols, lanes] = (own[0:cols, :] - other[0:cols, :]) * keep
        edge = jnp.zeros((8, face), F32)
        mine = jnp.concatenate([edge, own[cols:old, :], edge], axis=0)
        blank = jnp.zeros((16, face), F32)
        theirs = other[cols:old, :]
        theirs = jnp.concatenate([theirs, blank] if shift == 0 else [blank, theirs], axis=0)
        t_ref[cols:rows, lanes] = (mine - theirs) * keep
    v = split_dot(t_ref[...], mat_ref[...])
    if scale != 1.0:
        v = v * scale
    ids = jnp.concatenate(
        [
            pr_ref[old : old + 8, 0:8],
            sl_ref[old : old + 8, 0:width],
            nl_ref[old : old + 8, width - 8 : width],
        ],
        axis=1,
    )
    for ref, lanes in ((ol_ref, slice(0, face)), (or_ref, slice(face, 2 * face))):
        ref[0:rows, :] = v[:, lanes]
        ref[rows : rows + 8, :] = jnp.zeros((8, face), F32)
        ref[rows : rows + 8, 0:new] = ids


def one_hot(ids, count):
    dof = lax.broadcasted_iota(jnp.int32, (count, ids.shape[1]), 0).astype(F32)
    return (ids == dof).astype(F32)


def lower(half):
    row = lax.broadcasted_iota(jnp.int32, (half, half), 0)
    col = lax.broadcasted_iota(jnp.int32, (half, half), 1)
    return row, col


def pack(ref, k, matrix, diagonals):
    half = LANE
    at = 2 * half * k
    row, col = lower(half)
    last = matrix[half:, half:]
    ref[at : at + half, :] = jnp.where(row >= col, matrix[:half, :half], last)
    ref[at + half : at + 2 * half, :] = matrix[half:, :half]
    ref[diagonals + k : diagonals + k + 1, :] = jnp.sum(
        jnp.where(row == col, last, 0.0), axis=0, keepdims=True
    )


def unpack(ref, k, diagonals):
    half = LANE
    at = 2 * half * k
    row, col = lower(half)
    shared = ref[at : at + half, :]
    flipped = jnp.transpose(shared)
    cross = ref[at + half : at + 2 * half, :]
    first = jnp.where(row >= col, shared, flipped)
    last = jnp.where(row < col, shared, flipped)
    last = jnp.where(row == col, ref[diagonals + k : diagonals + k + 1, :], last)
    return jnp.concatenate(
        [
            jnp.concatenate([first, jnp.transpose(cross)], axis=1),
            jnp.concatenate([cross, last], axis=1),
        ],
        axis=0,
    )


def moment_kernel(sl0_ref, cl_ref, gram_ref, *refs, cols, count):
    out = refs[-1]
    half = count // 2

    def put(at, block):
        out[at : at + cols, :] = block[:, :half]
        out[at + cols : at + 2 * cols, :] = block[:, half:]

    base = 8 * half
    at = base + 8 * cols
    diagonals = at + cols
    out[at:, :] = jnp.zeros((out.shape[0] - at, LANE), F32)
    own = sl0_ref.shape[0] - cols - 8
    put(base, nt(cl_ref[...], one_hot(sl0_ref[cols + own : cols + own + 1, 0:own], count)))
    sums = []
    for k in range(3):
        t_ref, l_ref, r_ref = refs[3 * k : 3 * k + 3]
        rows, double = t_ref.shape
        face = double // 2
        width = rows - cols
        spot = one_hot(l_ref[rows : rows + 1, 0:width], count)
        tl, tr = t_ref[cols:rows, :face], t_ref[cols:rows, face:]
        inner = nt(tl, l_ref[cols:rows, :]) + nt(tr, r_ref[cols:rows, :])
        pack(out, k, nt(nn(spot, inner), spot), diagonals)
        cross = nt(l_ref[0:cols, :], tl) + nt(r_ref[0:cols, :], tr)
        put(base + 2 * cols * (k + 1), nt(cross, spot))
        sums.append(
            lane_sum(t_ref[0:cols, :face] * l_ref[0:cols, :])
            + lane_sum(t_ref[0:cols, face:] * r_ref[0:cols, :])
        )
    pack(out, 3, gram_ref[...], diagonals)
    lane = lax.broadcasted_iota(jnp.int32, (cols, LANE), 1)
    block = jnp.zeros((cols, LANE), F32)
    for k in range(3):
        block = jnp.where(lane == k, sums[k], block)
    out[at : at + cols, :] = block


def combine_kernel(sums_ref, coarse_ref, mass_ref, prev_ref, *refs, cols, count):
    half = count // 2
    base = 8 * half
    diagonals = base + 9 * cols
    sl0, sr0 = refs[0:2]
    level = [None] + [refs[2 + 3 * k : 5 + 3 * k] for k in range(LEVELS)]
    out_ref, field_ref, dual_ref, scal_ref = refs[2 + 3 * LEVELS :]
    face = sl0.shape[1]

    def get(at):
        return jnp.concatenate([sums_ref[at : at + cols, :], sums_ref[at + cols : at + 2 * cols, :]], axis=1)

    m0, m1, m2 = (unpack(sums_ref, k, diagonals) for k in range(3))
    coarse = coarse_ref[...]
    c_load, w0x, w1x, w2x = (get(base + 2 * cols * k) for k in range(4))
    at = base + 8 * cols
    s0, s1, s2 = (sums_ref[at : at + cols, k : k + 1] for k in range(3))
    g0 = nn(c_load, coarse)
    m0g0, m1g0, m2g0 = nn(g0, m0), nn(g0, m1), nn(g0, m2)
    c0 = w0x + m0g0
    g1 = nn(c0, coarse)
    m0g1, m1g1 = nn(g1, m0), nn(g1, m1)
    rz0 = s0 + lane_sum(2.0 * w0x * g0 + g0 * m0g0)
    del0 = s1 + lane_sum(2.0 * w1x * g0 + g0 * m1g0 + c0 * g1)
    nu0 = s2 + lane_sum(2.0 * w2x * g0 + g0 * m2g0 + 2.0 * w1x * g1 + 2.0 * g1 * m1g0 + g1 * m0g1)
    al0 = rz0 / del0
    be1 = (rz0 - 2.0 * al0 * del0 + al0 * al0 * nu0) / rz0
    cz1 = c0 - al0 * (w1x + m1g0 + m0g1)
    gz1 = nn(cz1, coarse)
    cm = (
        (1.0 + be1) * (w1x + m1g0)
        - al0 * (m1g1 + w2x + m2g0)
        + nn(gz1, m0)
        + be1 * m0g1
    )
    gm = nn(cm, coarse)
    last = level[LEVELS][1]
    spot = one_hot(last[last.shape[0] - 8 : last.shape[0] - 7, 0:LANE], count)
    local = nn(jnp.concatenate([g0, g1, gz1, gm], axis=0), spot)

    def coef(k, n):
        width = 8 * (2 * k + 1)
        first = 8 * (LEVELS - k)
        return local[: n * cols, first : first + width]

    def spread(k, ref, n, lanes):
        width = 8 * (2 * k + 1)
        wide = nn(coef(k, n), ref[cols : cols + width, lanes])
        return [wide[i * cols : (i + 1) * cols] for i in range(n)]

    def fields(b2, b4, b6, lanes):
        x2, x4, x6 = (b[0:cols, lanes] for b in (b2, b4, b6))
        p20, p21, p2z = spread(2, b2, 3, lanes)
        p40, p41 = spread(4, b4, 2, lanes)
        (p60,) = spread(6, b6, 1, lanes)
        z0 = x2 + p20
        n0 = x4 + p40 + p21
        z1 = z0 - al0 * n0
        n1 = x4 + p40 - al0 * (x6 + p60 + p41) + p2z
        return z0, z1, n1 + be1 * n0

    left, right, whole = slice(0, face), slice(face, 2 * face), slice(0, face)
    t1, t2, t3, t4, t5, t6 = (level[k][0] for k in range(1, 7))
    z0, z1, m = fields(t2, t4, t6, right)
    _, _, m_left = fields(t2, t4, t6, left)
    p10, p11, p1z = spread(1, t1, 3, right)
    p30, p31 = spread(3, t3, 2, right)
    (p50,) = spread(5, t5, 1, right)
    x1, x3, x5 = (ref[0:cols, right] for ref in (t1, t3, t5))
    d = x1 + p10
    w0 = x3 + p30 + p11
    w1 = x3 + p30 - al0 * (x5 + p50 + p31) + p1z
    r1 = d - al0 * w0
    q1 = w1 + be1 * w0
    p1 = z1 + be1 * z0
    for side, (own, pos, lanes) in enumerate(((sl0, 1, left), (sr0, 2, right))):
        u = fields(level[2][pos], level[4][pos], level[6][pos], whole)
        corner = spread(0, own, 4, whole)
        field_ref[0:cols, lanes] = own[0:cols, :] + corner[0]
        for i in range(3):
            field_ref[(i + 1) * cols : (i + 2) * cols, lanes] = u[i] + corner[i + 1]
        mu = lane_sum((m if side else m_left) * u[2])
        mm = mu if side == 0 else mm + mu
    for i, item in enumerate((z0, z1, m)):
        dual_ref[i * cols : (i + 1) * cols, :] = item
    moments = (
        lane_sum(r1 * z1), lane_sum(r1 * m), lane_sum(q1 * z1), lane_sum(q1 * m),
        lane_sum(r1 * p1), lane_sum(p1 * q1), lane_sum(z1 * w1), lane_sum(m * w1), mm,
    )
    lane = lax.broadcasted_iota(jnp.int32, (cols, LANE), 1)
    block = jnp.zeros((cols, LANE), F32)
    for k, item in enumerate(moments):
        block = jnp.where(lane == k, item, block)
    field = field_ref[...]
    scaled = field * mass_ref[...]
    tq = nn(scaled, prev_ref[...].astype(F32))
    out_ref[0 : 4 * cols, :] = tq[:, :half]
    out_ref[4 * cols : 8 * cols, :] = tq[:, half:]
    out_ref[8 * cols : 12 * cols, :] = nt(scaled, field)
    out_ref[12 * cols : 13 * cols, :] = block
    out_ref[13 * cols :, :] = jnp.zeros((out_ref.shape[0] - 13 * cols, LANE), F32)
    block = jnp.zeros((cols, LANE), F32)
    for k, item in enumerate((al0, be1, lane_sum(cm * gm))):
        block = jnp.where(lane == k, item, block)
    scal_ref[...] = block


def final_kernel(sums_ref, early_ref, scal_ref, field_ref, dual_ref, prev_ref, nm_ref,
                 block_ref, multi_ref, coef_ref, factor_ref, *, cols, count):
    half = count // 2
    face = dual_ref.shape[1]
    at = 12 * cols
    r1z1, r1m, q1z1, q1m, r1p1, p1q1, z1w1, mw1, mm = (
        sums_ref[at : at + cols, k : k + 1] for k in range(9)
    )
    al0, be1, extra = (scal_ref[:, k : k + 1] for k in range(3))
    mfm = mm + extra
    al1 = r1p1 / p1q1
    z2q1 = q1z1 - al1 * q1m
    be2 = -z2q1 / p1q1
    rz2 = r1z1 - al1 * (r1m + q1z1) + al1 * al1 * q1m
    z2fz2 = z1w1 - 2.0 * al1 * mw1 + al1 * al1 * mfm
    al2 = rz2 / (z2fz2 + 2.0 * be2 * z2q1 + be2 * be2 * p1q1)
    along = al1 + al2 * be2
    parts = (al0 + along * be1, along + al2, -al1 * al2)
    multi = sum(y * dual_ref[i * cols : (i + 1) * cols, :] for i, y in enumerate(parts))
    multi_ref[...] = multi
    weights = [jnp.ones((cols, 1), F32)] + [-y for y in parts]
    primal = sum(y * field_ref[i * cols : (i + 1) * cols, :] for i, y in enumerate(weights))
    g1 = sum(
        y
        * jnp.concatenate(
            [sums_ref[i * cols : (i + 1) * cols, :], sums_ref[(4 + i) * cols : (5 + i) * cols, :]],
            axis=1,
        )
        for i, y in enumerate(weights)
    )
    row = lax.broadcasted_iota(jnp.int32, (cols, cols), 0)
    col = lax.broadcasted_iota(jnp.int32, (cols, cols), 1)
    eye = (row == col).astype(F32)
    across = [jnp.sum(y * eye, axis=0, keepdims=True) for y in weights]
    gram = jnp.zeros((cols, cols), F32)
    for i in range(4):
        for j in range(4):
            tile = sums_ref[(8 + i) * cols : (9 + i) * cols, j * cols : (j + 1) * cols]
            gram = gram + weights[i] * tile * across[j]
    basis = unpack(early_ref, 3, 8 * half + 9 * cols)
    c = 2.0 * g1 - nn(g1, basis)
    coef_ref[...] = c
    gram = gram - nt(c, g1) - nt(g1, c) + nt(nn(c, basis), c)
    gram = 0.5 * (gram + jnp.transpose(gram))
    final = primal - nt(c, prev_ref[...].astype(F32))
    work = jnp.concatenate([gram, eye], axis=1)
    index = lax.broadcasted_iota(jnp.int32, (cols, 1), 0)
    pivots = jnp.zeros((cols, 1), F32)
    for k in range(cols):
        pivot = work[k : k + 1, k : k + 1]
        pivots = jnp.where(index == k, pivot, pivots)
        times = jnp.where(index > k, work[:, k : k + 1], 0.0) / pivot
        work = work - times * work[k : k + 1, :]
    work = work / jnp.sqrt(pivots)
    factor_ref[...] = jnp.transpose(jnp.where(row <= col, work[:, :cols], 0.0))
    solved = nn(work[:, cols:], final)
    left = nn(solved[:, :face], from_order(nm_ref[...], face))
    block_ref[:, :face] = left
    block_ref[:, face:] = solved[:, face:]


def sum_kernel(parts_ref, out_ref):
    total = jnp.sum(parts_ref[...], axis=0)
    for i in range(out_ref.shape[0]):
        out_ref[i] = total


def swap(parts, axes):
    return lax.all_to_all(parts, axes, 0, 0, tiled=True)


def summed(parts, copies):
    return call(sum_kernel, jax.ShapeDtypeStruct((copies,) + parts.shape[1:], F32))(parts)


def over_all(rows, n_red, n_z):
    parts = swap(rows.reshape(n_red, rows.shape[0] // n_red, LANE), RED)
    parts = swap(summed(parts, n_z), "z")
    return swap(summed(parts, n_red), RED).reshape(rows.shape)


def up(count, unit):
    return -(-count // unit) * unit


def solution(mesh):
    n_sub, n_grp = mesh.shape["sub"], mesh.shape["grp"]
    n_y = min(4, n_sub)
    n_z = n_sub // n_y
    n_c = 2
    n_x = n_grp // n_c
    fine = Mesh(np.asarray(mesh.devices).reshape(n_y, n_z, n_x, n_c), ("y", "z", "x", "c"))
    n_red = n_y * n_x * n_c
    along = ("y", "z")
    ahead = [(i, i + 1) for i in range(n_sub - 1)]
    behind = [(i + 1, i) for i in range(n_sub - 1)]

    def on_device(schur_inverse, schur, coarse_basis, corner_index, coarse_inverse, neighbor_map,
                  load, previous, mass):
        inverse_block, schur_block, basis = schur_inverse[0, 0], schur[0, 0], coarse_basis[0, 0]
        corners, nm = corner_index[0, 0], neighbor_map[0, 0]
        rhs, earlier, weights = load[0, 0].T, previous[0, 0], mass[0, 0]
        cols, rows = rhs.shape
        face = nm.shape[0]
        count = coarse_inverse.shape[0]
        total = rows * n_sub * n_grp
        own = corners.shape[0]
        position = lax.axis_index(along)
        nm_row = nm[None, :]
        side = jnp.arange(2 * face) < face
        mask = jnp.where(side, position > 0, position < n_sub - 1).astype(F32)[None, :]
        mask = jnp.broadcast_to(mask, (8, 2 * face))

        def shape(*dims):
            return jax.ShapeDtypeStruct(dims, F32)

        half = shape(cols + own + 8, face)
        sl, sr, cl = pl.pallas_call(
            start_kernel,
            out_shape=(half, half, shape(cols, own)),
            in_specs=[pl.BlockSpec(memory_space=pl.ANY)] * 5,
            scratch_shapes=[
                pltpu.VMEM((rows, rows), BF16),
                pltpu.VMEM((cols, rows), F32),
                pltpu.VMEM((own, rows), F32),
                pltpu.VMEM((1, face), jnp.int32),
                pltpu.VMEM((1, own), jnp.int32),
                pltpu.SemaphoreType.DMA((5,)),
            ],
            compiler_params=pltpu.CompilerParams(vmem_limit_bytes=60 * 1024 * 1024),
        )(inverse_block, rhs, basis, nm_row, corners[None, :])
        square = jax.ShapeDtypeStruct((rows, rows), BF16)

        def exchange(sl, sr):
            return lax.ppermute(sl, along, behind), lax.ppermute(sr, along, ahead)

        def step(k, sl, sr, near, mat):
            width = own + 16 * (k - 1)
            out = cols + width + 16
            return call(
                lambda *refs: step_kernel(
                    *refs, cols=cols, width=width, scale=0.25 if k % 2 == 1 else 1.0
                ),
                (shape(out, 2 * face), shape(out + 8, face), shape(out + 8, face)),
            )(sl, sr, *near, mask, mat)

        chain = [sl, sr]
        near = exchange(sl, sr)
        schur_p = call(matrix_kernel, square)(schur_block, nm_row)
        t, sl, sr = step(1, sl, sr, near, schur_p)
        chain += [t, sl, sr]
        near = exchange(sl, sr)
        inv_p = call(matrix_kernel, square)(inverse_block, nm_row)
        t, sl, sr = step(2, sl, sr, near, inv_p)
        chain += [t, sl, sr]
        near = exchange(sl, sr)
        prev_p, mass_p, gram = call(
            lambda *refs: basis_kernel(*refs, total=total),
            (jax.ShapeDtypeStruct(earlier.shape, BF16), shape(1, rows), shape(count, count)),
        )(earlier, nm_row, weights[None, :])
        t, sl, sr = step(3, sl, sr, near, schur_p)
        chain += [t, sl, sr]
        near = exchange(sl, sr)
        size = up(4 * count + 9 * cols + 8, 8 * n_red)
        first = call(
            lambda *refs: moment_kernel(*refs, cols=cols, count=count), shape(size, LANE)
        )(chain[0], cl, gram, *chain[2:11])
        t, sl, sr = step(4, sl, sr, near, inv_p)
        chain += [t, sl, sr]
        first, sl, sr = lax.optimization_barrier((first, sl, sr))
        near = exchange(sl, sr)
        t, sl, sr = step(5, sl, sr, near, schur_p)
        chain += [t, sl, sr]
        near = exchange(sl, sr)
        t, sl, sr = step(6, sl, sr, near, inv_p)
        chain += [t, sl, sr]
        first, sl, sr = lax.optimization_barrier((first, sl, sr))
        chain[-2:] = [sl, sr]
        first = over_all(first, n_red, n_z)
        size = up(13 * cols, 8 * n_red)
        second, field, dual, scal = call(
            lambda *refs: combine_kernel(*refs, cols=cols, count=count),
            (shape(size, LANE), shape(4 * cols, rows), shape(3 * cols, face), shape(cols, LANE)),
        )(first, coarse_inverse, mass_p, prev_p, *chain)
        second = over_all(second, n_red, n_z)
        block, multi, coefficients, factor = call(
            lambda *refs: final_kernel(*refs, cols=cols, count=count),
            (shape(cols, rows), shape(cols, face), shape(cols, count), shape(cols, cols)),
        )(second, first, scal, field, dual, prev_p, nm_row)
        return block.T[None, None], multi.T[None, None], coefficients.T, factor

    split = (along, ("x", "c"))
    return jax.shard_map(
        on_device,
        mesh=fine,
        in_specs=(
            P(*split, None, None),
            P(*split, None, None),
            P(*split, None, None),
            P(*split, None),
            P(),
            P(*split, None),
            P(*split, None, None),
            P(*split, None, None),
            P(*split, None),
        ),
        out_specs=(P(*split, None, None), P(*split, None, None), P(), P()),
        check_vma=False,
    )
```

```python
import jax
import jax.numpy as jnp
import numpy as np
from jax import lax
from jax.experimental import pallas as pl
from jax.experimental.pallas import tpu as pltpu
from jax.sharding import Mesh, PartitionSpec as P

HI = lax.Precision.HIGHEST
F32 = jnp.float32
BF16 = jnp.bfloat16
RED = ("y", "x", "c")
LEVELS = 3
LANE = 128
MOVED = 64


def nn(a, b):
    return jnp.dot(a, b, precision=HI, preferred_element_type=F32)


def nt(a, b):
    return lax.dot_general(
        a, b, (((1,), (1,)), ((), ())), precision=HI, preferred_element_type=F32
    )


def lane_sum(a):
    return jnp.sum(a, axis=1, keepdims=True)


def call(kernel, outs, aliases={}):
    return pl.pallas_call(
        kernel,
        out_shape=outs,
        input_output_aliases=aliases,
        compiler_params=pltpu.CompilerParams(vmem_limit_bytes=12 * 1024 * 1024),
    )


def split_dot(t, mat):
    high = t.astype(BF16).astype(F32)
    both = jnp.concatenate([high, t - high], axis=0).astype(BF16)
    wide = jnp.dot(both, mat, preferred_element_type=F32)
    rows = t.shape[0]
    return wide[:rows] + wide[rows:]


def to_order(nm_row, face):
    nm = jnp.transpose(jnp.broadcast_to(nm_row.astype(F32), (8, face)))[:, 0:1]
    return (nm == lax.broadcasted_iota(jnp.int32, (face, face), 1).astype(F32)).astype(F32)


def from_order(nm_row, face):
    return (nm_row == lax.broadcasted_iota(jnp.int32, (face, face), 0)).astype(F32)


def start_kernel(inv_hbm, load_hbm, basis_hbm, nm_hbm, corner_hbm, sl_ref, sr_ref, cl_ref,
                 inv_ref, load_ref, basis_ref, nm_ref, corner_ref, sems):
    pairs = (
        (nm_hbm, nm_ref), (load_hbm, load_ref), (basis_hbm, basis_ref), (corner_hbm, corner_ref),
        (inv_hbm, inv_ref),
    )
    copies = [pltpu.make_async_copy(src, dst, sems.at[i]) for i, (src, dst) in enumerate(pairs)]
    for copy in copies:
        copy.start()
    for copy in copies[:-1]:
        copy.wait()
    face = nm_ref.shape[1]
    cols = load_ref.shape[0]
    corners = basis_ref.shape[0]
    rows = cols + corners
    load = load_ref[...]
    basis = basis_ref[...]
    order = to_order(nm_ref[...], face)
    cl_ref[...] = nt(load, basis)
    for ref in (sl_ref, sr_ref):
        ref[rows : rows + 8, :] = jnp.zeros((8, face), F32)
        ref[rows : rows + 1, 0:corners] = corner_ref[...].astype(F32)
    sr_ref[cols:rows, :] = basis[:, face:]
    copies[-1].wait()
    wide = split_dot(load, inv_ref[...])
    sr_ref[0:cols, :] = wide[:, face:]
    sl_ref[0:rows, :] = nn(jnp.concatenate([wide[:, :face], basis[:, :face]], axis=0), order)


def matrix_kernel(src, nm_ref, dst):
    face = nm_ref.shape[1]
    order = to_order(nm_ref[...], face).astype(BF16)
    back = from_order(nm_ref[...], face).astype(BF16)
    dst[:, face:] = src[:, face:]
    dst[:, :face] = jnp.dot(src[:, :face], order, preferred_element_type=F32).astype(BF16)
    dst[:face, :] = jnp.dot(back, dst[:face, :], preferred_element_type=F32).astype(BF16)


def basis_kernel(prev_ref, nm_ref, mass_ref, prev_out, mass_out, gram_out, *, total):
    face = nm_ref.shape[1]
    back = from_order(nm_ref[...], face).astype(BF16)
    prev_out[face:, :] = prev_ref[face:, :]
    prev_out[:face, :] = jnp.dot(back, prev_ref[:face, :], preferred_element_type=F32).astype(BF16)
    mass = mass_ref[...] / total
    mass_out[:, face:] = mass[:, face:]
    left = jnp.broadcast_to(mass[:, :face], (8, face))
    mass_out[:, :face] = nn(left, to_order(nm_ref[...], face))[0:1]
    column = jnp.transpose(jnp.broadcast_to(mass, (8, mass.shape[1])))[:, 0:1]
    wide = prev_ref[...].astype(F32)
    gram_out[...] = lax.dot_general(
        wide * column, wide, (((0,), (0,)), ((), ())), precision=HI, preferred_element_type=F32
    )


def step_kernel(sl_ref, sr_ref, nl_ref, pr_ref, mask_ref, mat_ref, t_ref, ol_ref, or_ref,
                *, cols, width, scale):
    face = sl_ref.shape[1]
    new = width + 16
    rows = cols + new
    old = cols + width
    for lanes, own, other, shift in (
        (slice(0, face), sl_ref, pr_ref, 0),
        (slice(face, 2 * face), sr_ref, nl_ref, 16),
    ):
        keep = mask_ref[0:1, lanes]
        t_ref[0:cols, lanes] = (own[0:cols, :] - other[0:cols, :]) * keep
        edge = jnp.zeros((8, face), F32)
        mine = jnp.concatenate([edge, own[cols:old, :], edge], axis=0)
        blank = jnp.zeros((16, face), F32)
        theirs = other[cols:old, :]
        theirs = jnp.concatenate([theirs, blank] if shift == 0 else [blank, theirs], axis=0)
        t_ref[cols:rows, lanes] = (mine - theirs) * keep
    v = split_dot(t_ref[...], mat_ref[...])
    if scale != 1.0:
        v = v * scale
    ids = jnp.concatenate(
        [
            pr_ref[old : old + 8, 0:8],
            sl_ref[old : old + 8, 0:width],
            nl_ref[old : old + 8, width - 8 : width],
        ],
        axis=1,
    )
    for ref, lanes in ((ol_ref, slice(0, face)), (or_ref, slice(face, 2 * face))):
        ref[0:rows, :] = v[:, lanes]
        ref[rows : rows + 8, :] = jnp.zeros((8, face), F32)
        ref[rows : rows + 8, 0:new] = ids


def one_hot(ids, count):
    dof = lax.broadcasted_iota(jnp.int32, (count, ids.shape[1]), 0).astype(F32)
    return (ids == dof).astype(F32)


def lower(half):
    row = lax.broadcasted_iota(jnp.int32, (half, half), 0)
    col = lax.broadcasted_iota(jnp.int32, (half, half), 1)
    return row, col


def packed(matrix):
    half = LANE
    row, col = lower(half)
    last = matrix[half:, half:]
    shared = jnp.where(row >= col, matrix[:half, :half], last)
    return shared, matrix[half:, :half], jnp.sum(jnp.where(row == col, last, 0.0), axis=0, keepdims=True)


def pack(ref, k, matrix, diagonals):
    half = LANE
    at = 2 * half * k
    shared, cross, diagonal = packed(matrix)
    ref[at : at + half, :] = shared
    ref[at + half : at + 2 * half, :] = cross
    ref[diagonals + k : diagonals + k + 1, :] = diagonal


def unpacked(shared, cross, diagonal):
    row, col = lower(LANE)
    flipped = jnp.transpose(shared)
    first = jnp.where(row >= col, shared, flipped)
    last = jnp.where(row < col, shared, flipped)
    last = jnp.where(row == col, diagonal, last)
    return jnp.concatenate(
        [
            jnp.concatenate([first, jnp.transpose(cross)], axis=1),
            jnp.concatenate([cross, last], axis=1),
        ],
        axis=0,
    )


def unpack(ref, k, diagonals):
    half = LANE
    at = 2 * half * k
    return unpacked(
        ref[at : at + half, :],
        ref[at + half : at + 2 * half, :],
        ref[diagonals + k : diagonals + k + 1, :],
    )


def level_moments(out, refs, k, cols, count):
    half = count // 2
    base = 8 * half - MOVED
    t_ref, l_ref, r_ref = refs
    rows, double = t_ref.shape
    face = double // 2
    width = rows - cols
    spot = one_hot(l_ref[rows : rows + 1, 0:width], count)
    tl, tr = t_ref[cols:rows, :face], t_ref[cols:rows, face:]
    inner = nt(tl, l_ref[cols:rows, :]) + nt(tr, r_ref[cols:rows, :])
    pack(out, k, nt(nn(spot, inner), spot), base + 9 * cols)
    cross = nt(l_ref[0:cols, :], tl) + nt(r_ref[0:cols, :], tr)
    put(out, base + 2 * cols * (k + 1), nt(cross, spot))
    return lane_sum(t_ref[0:cols, :face] * l_ref[0:cols, :]) + lane_sum(
        t_ref[0:cols, face:] * r_ref[0:cols, :]
    )


def put(out, at, block):
    cols, half = block.shape[0], block.shape[1] // 2
    out[at : at + cols, :] = block[:, :half]
    out[at + cols : at + 2 * cols, :] = block[:, half:]


def in_lanes(items, start=0):
    cols = items[0].shape[0]
    lane = lax.broadcasted_iota(jnp.int32, (cols, LANE), 1)
    block = jnp.zeros((cols, LANE), F32)
    for k, item in enumerate(items):
        block = jnp.where(lane == start + k, item, block)
    return block


def moment_kernel(sl0_ref, cl_ref, gram_ref, *refs, cols, count):
    out = refs[-1]
    base = 4 * count - MOVED
    at = base + 8 * cols
    out[at:, :] = jnp.zeros((out.shape[0] - at, LANE), F32)
    own = sl0_ref.shape[0] - cols - 8
    spot = one_hot(sl0_ref[cols + own : cols + own + 1, 0:own], count)
    put(out, base, nt(cl_ref[...], spot))
    sums = [level_moments(out, refs[3 * k : 3 * k + 3], k, cols, count) for k in range(2)]
    gram = gram_ref[...]
    half = count // 2
    shared, cross, diagonal = packed(gram)
    out[3 * count : 3 * count + half - MOVED, :] = shared[MOVED:, :]
    out[3 * count + half - MOVED : base, :] = cross
    out[at + cols + 3 : at + cols + 4, :] = diagonal
    out[at : at + cols, :] = in_lanes(sums)


def last_moment_kernel(given_ref, *refs, cols, count):
    out = refs[-1]
    total = level_moments(out, refs[:3], 2, cols, count)
    at = 4 * count - MOVED + 8 * cols
    out[at : at + cols, :] = given_ref[at : at + cols, :] + in_lanes([total], 2)


def coarse_kernel(sums_ref, coarse_ref, mat_ref, sl0, sr0, t1, t2, sl2, sr2, t3, sl3,
                  ol_ref, or_ref, z0_ref, w1c_ref, r1_ref, w0_ref, field_ref, scal_ref,
                  *, cols, count):
    base = 4 * count - MOVED
    face = sl0.shape[1]

    def get(at):
        return jnp.concatenate(
            [sums_ref[at : at + cols, :], sums_ref[at + cols : at + 2 * cols, :]], axis=1
        )

    m0, m1, m2 = (unpack(sums_ref, k, base + 9 * cols) for k in range(3))
    coarse = coarse_ref[...]
    c_load, w0x, w1x, w2x = (get(base + 2 * cols * k) for k in range(4))
    at = base + 8 * cols
    s0, s1, s2 = (sums_ref[at : at + cols, k : k + 1] for k in range(3))
    g0 = nn(c_load, coarse)
    m0g0, m1g0, m2g0 = nn(g0, m0), nn(g0, m1), nn(g0, m2)
    c0 = w0x + m0g0
    g1 = nn(c0, coarse)
    m0g1, m1g1 = nn(g1, m0), nn(g1, m1)
    rz0 = s0 + lane_sum(2.0 * w0x * g0 + g0 * m0g0)
    del0 = s1 + lane_sum(2.0 * w1x * g0 + g0 * m1g0 + c0 * g1)
    nu0 = s2 + lane_sum(2.0 * w2x * g0 + g0 * m2g0 + 2.0 * w1x * g1 + 2.0 * g1 * m1g0 + g1 * m0g1)
    al0 = rz0 / del0
    be1 = (rz0 - 2.0 * al0 * del0 + al0 * al0 * nu0) / rz0
    cz1 = c0 - al0 * (w1x + m1g0 + m0g1)
    gz1 = nn(cz1, coarse)
    cm = (
        (1.0 + be1) * (w1x + m1g0)
        - al0 * (m1g1 + w2x + m2g0)
        + nn(gz1, m0)
        + be1 * m0g1
    )
    gm = nn(cm, coarse)
    spot = one_hot(sl3[sl3.shape[0] - 8 : sl3.shape[0] - 7, 0:LANE], count)
    local = nn(jnp.concatenate([g0, g1, gz1, gm], axis=0), spot)

    def spread(k, ref, first, n, lanes):
        width = 8 * (2 * k + 1)
        lane = 8 * (LEVELS - k)
        wide = nn(local[first * cols : (first + n) * cols, lane : lane + width],
                  ref[cols : cols + width, lanes])
        return [wide[i * cols : (i + 1) * cols] for i in range(n)]

    every, right = slice(0, 2 * face), slice(face, 2 * face)
    p10, p11, p1z = spread(1, t1, 0, 3, every)
    (p20,) = spread(2, t2, 0, 1, every)
    (p30,) = spread(3, t3, 0, 1, every)
    z0_ref[...] = t2[0:cols, :] + p20
    w0 = t3[0:cols, :] + p30 + p11
    w0_ref[...] = w0[:, right]
    w1c_ref[...] = p1z
    r1_ref[...] = t1[0:cols, right] + p10[:, right] - al0 * w0[:, right]
    v = split_dot(w0, mat_ref[...]) * 0.25
    ol_ref[...] = v[:, :face]
    or_ref[...] = v[:, right]
    for own, u, lanes in ((sl0, sl2, slice(0, face)), (sr0, sr2, right)):
        corner = spread(0, own, 0, 4, slice(0, face))
        field_ref[0:cols, lanes] = own[0:cols, :] + corner[0]
        (u0,) = spread(2, u, 0, 1, slice(0, face))
        field_ref[cols : 2 * cols, lanes] = u[0:cols, :] + u0 + corner[1]
        field_ref[2 * cols : 3 * cols, lanes] = corner[2]
        field_ref[3 * cols : 4 * cols, lanes] = corner[3]
    scal_ref[...] = in_lanes([al0, be1, lane_sum(cm * gm)])


def joined(own_ref, other_ref, mask_ref, left):
    face = own_ref.shape[1]
    lanes = slice(0, face) if left else slice(face, 2 * face)
    return (own_ref[...] - other_ref[...]) * mask_ref[0:1, lanes]


def field_of(sl_ref, sr_ref, nl_ref, pr_ref, mask_ref):
    return jnp.concatenate(
        [joined(sl_ref, pr_ref, mask_ref, True), joined(sr_ref, nl_ref, mask_ref, False)], axis=1
    )


def dual_kernel(sl_ref, sr_ref, nl_ref, pr_ref, mask_ref, z0_ref, scal_ref, mat_ref,
                n0_ref, z1_ref, ol_ref, or_ref):
    face = sl_ref.shape[1]
    n0 = field_of(sl_ref, sr_ref, nl_ref, pr_ref, mask_ref)
    z1 = z0_ref[...] - scal_ref[:, 0:1] * n0
    n0_ref[...] = n0
    z1_ref[...] = z1[:, face:]
    u = split_dot(z1, mat_ref[...])
    ol_ref[...] = u[:, :face]
    or_ref[...] = u[:, face:]


def precondition_kernel(sl_ref, sr_ref, nl_ref, pr_ref, mask_ref, w1c_ref, mat_ref,
                        w1_ref, ol_ref, or_ref):
    face = sl_ref.shape[1]
    w1 = field_of(sl_ref, sr_ref, nl_ref, pr_ref, mask_ref) + w1c_ref[...]
    w1_ref[...] = w1[:, face:]
    v = split_dot(w1, mat_ref[...]) * 0.25
    ol_ref[...] = v[:, :face]
    or_ref[...] = v[:, face:]


def combine_kernel(sl_ref, sr_ref, nl_ref, pr_ref, mask_ref, n0_ref, mat_ref, scal_ref, z0_ref,
                   z1_ref, ul_ref, ur_ref, r1_ref, w0_ref, w1_ref, base_ref, mass_ref, prev_ref,
                   gram_ref, out_ref, field_ref, dual_ref, *, cols, count):
    half = count // 2
    face = sl_ref.shape[1]
    be1 = scal_ref[:, 1:2]
    whole = field_of(sl_ref, sr_ref, nl_ref, pr_ref, mask_ref) + be1 * n0_ref[...]
    u = split_dot(whole, mat_ref[...])
    field_ref[0 : 2 * cols, :] = base_ref[0 : 2 * cols, :]
    third, fourth = slice(2 * cols, 3 * cols), slice(3 * cols, 4 * cols)
    field_ref[third, 0:face] = base_ref[third, 0:face] + ul_ref[...]
    field_ref[third, face:] = base_ref[third, face:] + ur_ref[...]
    field_ref[fourth, :] = base_ref[fourth, :] + u
    m = whole[:, face:]
    z0, z1, w0, w1, r1 = z0_ref[:, face:], z1_ref[...], w0_ref[...], w1_ref[...], r1_ref[...]
    q1 = w1 + be1 * w0
    p1 = z1 + be1 * z0
    for i, item in enumerate((z0, z1, m)):
        dual_ref[i * cols : (i + 1) * cols, :] = item
    moments = (
        lane_sum(r1 * z1), lane_sum(r1 * m), lane_sum(q1 * z1), lane_sum(q1 * m),
        lane_sum(r1 * p1), lane_sum(p1 * q1), lane_sum(z1 * w1), lane_sum(m * w1),
        lane_sum(whole * u),
    )
    field = field_ref[...]
    scaled = field * mass_ref[...]
    tq = nn(scaled, prev_ref[...].astype(F32))
    out_ref[0 : 4 * cols, :] = tq[:, :half]
    out_ref[4 * cols : 8 * cols, :] = tq[:, half:]
    out_ref[8 * cols : 12 * cols, :] = nt(scaled, field)
    out_ref[12 * cols : 13 * cols, :] = in_lanes(moments)
    at = 13 * cols
    shared, _, _ = packed(gram_ref[...])
    out_ref[at : at + MOVED, :] = shared[:MOVED, :]
    out_ref[at + MOVED :, :] = jnp.zeros((out_ref.shape[0] - at - MOVED, LANE), F32)


def final_kernel(sums_ref, early_ref, scal_ref, field_ref, dual_ref, prev_ref, nm_ref,
                 block_ref, multi_ref, coef_ref, factor_ref, *, cols, count):
    half = count // 2
    face = dual_ref.shape[1]
    at = 12 * cols
    r1z1, r1m, q1z1, q1m, r1p1, p1q1, z1w1, mw1, mm = (
        sums_ref[at : at + cols, k : k + 1] for k in range(9)
    )
    al0, be1, extra = (scal_ref[:, k : k + 1] for k in range(3))
    mfm = mm + extra
    al1 = r1p1 / p1q1
    z2q1 = q1z1 - al1 * q1m
    be2 = -z2q1 / p1q1
    rz2 = r1z1 - al1 * (r1m + q1z1) + al1 * al1 * q1m
    z2fz2 = z1w1 - 2.0 * al1 * mw1 + al1 * al1 * mfm
    al2 = rz2 / (z2fz2 + 2.0 * be2 * z2q1 + be2 * be2 * p1q1)
    along = al1 + al2 * be2
    parts = (al0 + along * be1, along + al2, -al1 * al2)
    multi = sum(y * dual_ref[i * cols : (i + 1) * cols, :] for i, y in enumerate(parts))
    multi_ref[...] = multi
    weights = [jnp.ones((cols, 1), F32)] + [-y for y in parts]
    primal = sum(y * field_ref[i * cols : (i + 1) * cols, :] for i, y in enumerate(weights))
    g1 = sum(
        y
        * jnp.concatenate(
            [sums_ref[i * cols : (i + 1) * cols, :], sums_ref[(4 + i) * cols : (5 + i) * cols, :]],
            axis=1,
        )
        for i, y in enumerate(weights)
    )
    row = lax.broadcasted_iota(jnp.int32, (cols, cols), 0)
    col = lax.broadcasted_iota(jnp.int32, (cols, cols), 1)
    eye = (row == col).astype(F32)
    across = [jnp.sum(y * eye, axis=0, keepdims=True) for y in weights]
    gram = jnp.zeros((cols, cols), F32)
    for i in range(4):
        for j in range(4):
            tile = sums_ref[(8 + i) * cols : (9 + i) * cols, j * cols : (j + 1) * cols]
            gram = gram + weights[i] * tile * across[j]
    first = 3 * count
    base = 4 * count - MOVED
    basis = unpacked(
        jnp.concatenate(
            [sums_ref[13 * cols : 13 * cols + MOVED, :], early_ref[first : first + half - MOVED, :]],
            axis=0,
        ),
        early_ref[base - half : base, :],
        early_ref[base + 9 * cols + 3 : base + 9 * cols + 4, :],
    )
    c = 2.0 * g1 - nn(g1, basis)
    coef_ref[...] = c
    gram = gram - nt(c, g1) - nt(g1, c) + nt(nn(c, basis), c)
    gram = 0.5 * (gram + jnp.transpose(gram))
    final = primal - nt(c, prev_ref[...].astype(F32))
    work = jnp.concatenate([gram, eye], axis=1)
    index = lax.broadcasted_iota(jnp.int32, (cols, 1), 0)
    pivots = jnp.zeros((cols, 1), F32)
    for k in range(cols):
        pivot = work[k : k + 1, k : k + 1]
        pivots = jnp.where(index == k, pivot, pivots)
        times = jnp.where(index > k, work[:, k : k + 1], 0.0) / pivot
        work = work - times * work[k : k + 1, :]
    work = work / jnp.sqrt(pivots)
    factor_ref[...] = jnp.transpose(jnp.where(row <= col, work[:, :cols], 0.0))
    solved = nn(work[:, cols:], final)
    left = nn(solved[:, :face], from_order(nm_ref[...], face))
    block_ref[:, :face] = left
    block_ref[:, face:] = solved[:, face:]


def sum_kernel(parts_ref, out_ref):
    total = jnp.sum(parts_ref[...], axis=0)
    for i in range(out_ref.shape[0]):
        out_ref[i] = total


def swap(parts, axes):
    return lax.all_to_all(parts, axes, 0, 0, tiled=True)


def summed(parts, copies):
    return call(sum_kernel, jax.ShapeDtypeStruct((copies,) + parts.shape[1:], F32))(parts)


def over_all(rows, n_red, n_z):
    parts = swap(rows.reshape(n_red, rows.shape[0] // n_red, LANE), RED)
    parts = swap(summed(parts, n_z), "z")
    return swap(summed(parts, n_red), RED).reshape(rows.shape)


def up(count, unit):
    return -(-count // unit) * unit


def solution(mesh):
    n_sub, n_grp = mesh.shape["sub"], mesh.shape["grp"]
    n_y = min(4, n_sub)
    n_z = n_sub // n_y
    n_c = 2
    n_x = n_grp // n_c
    fine = Mesh(np.asarray(mesh.devices).reshape(n_y, n_z, n_x, n_c), ("y", "z", "x", "c"))
    n_red = n_y * n_x * n_c
    along = ("y", "z")
    ahead = [(i, i + 1) for i in range(n_sub - 1)]
    behind = [(i + 1, i) for i in range(n_sub - 1)]

    def on_device(schur_inverse, schur, coarse_basis, corner_index, coarse_inverse, neighbor_map,
                  load, previous, mass):
        inverse_block, schur_block, basis = schur_inverse[0, 0], schur[0, 0], coarse_basis[0, 0]
        corners, nm = corner_index[0, 0], neighbor_map[0, 0]
        rhs, earlier, weights = load[0, 0].T, previous[0, 0], mass[0, 0]
        cols, rows = rhs.shape
        face = nm.shape[0]
        count = coarse_inverse.shape[0]
        total = rows * n_sub * n_grp
        own = corners.shape[0]
        position = lax.axis_index(along)
        nm_row = nm[None, :]
        side = jnp.arange(2 * face) < face
        mask = jnp.where(side, position > 0, position < n_sub - 1).astype(F32)[None, :]
        mask = jnp.broadcast_to(mask, (8, 2 * face))

        def shape(*dims):
            return jax.ShapeDtypeStruct(dims, F32)

        half = shape(cols + own + 8, face)
        sl, sr, cl = pl.pallas_call(
            start_kernel,
            out_shape=(half, half, shape(cols, own)),
            in_specs=[pl.BlockSpec(memory_space=pl.ANY)] * 5,
            scratch_shapes=[
                pltpu.VMEM((rows, rows), BF16),
                pltpu.VMEM((cols, rows), F32),
                pltpu.VMEM((own, rows), F32),
                pltpu.VMEM((1, face), jnp.int32),
                pltpu.VMEM((1, own), jnp.int32),
                pltpu.SemaphoreType.DMA((5,)),
            ],
            compiler_params=pltpu.CompilerParams(vmem_limit_bytes=60 * 1024 * 1024),
        )(inverse_block, rhs, basis, nm_row, corners[None, :])
        square = jax.ShapeDtypeStruct((rows, rows), BF16)

        def exchange(sl, sr):
            return lax.ppermute(sl, along, behind), lax.ppermute(sr, along, ahead)

        def step(k, sl, sr, near, mat):
            width = own + 16 * (k - 1)
            out = cols + width + 16
            return call(
                lambda *refs: step_kernel(
                    *refs, cols=cols, width=width, scale=0.25 if k % 2 == 1 else 1.0
                ),
                (shape(out, 2 * face), shape(out + 8, face), shape(out + 8, face)),
            )(sl, sr, *near, mask, mat)

        chain = [sl, sr]
        near = exchange(sl, sr)
        schur_p = call(matrix_kernel, square)(schur_block, nm_row)
        t, sl, sr = step(1, sl, sr, near, schur_p)
        chain += [t, sl, sr]
        near = exchange(sl, sr)
        inv_p = call(matrix_kernel, square)(inverse_block, nm_row)
        t, sl, sr = step(2, sl, sr, near, inv_p)
        chain += [t, sl, sr]
        near = exchange(sl, sr)
        prev_p, mass_p, gram = call(
            lambda *refs: basis_kernel(*refs, total=total),
            (jax.ShapeDtypeStruct(earlier.shape, BF16), shape(1, rows), shape(count, count)),
        )(earlier, nm_row, weights[None, :])
        size = up(4 * count - MOVED + 9 * cols + 8, 8 * n_red)
        first = call(
            lambda *refs: moment_kernel(*refs, cols=cols, count=count), shape(size, LANE)
        )(chain[0], cl, gram, *chain[2:8])
        t, sl, sr = step(3, sl, sr, near, schur_p)
        chain += [t, sl, sr]
        first = call(
            lambda *refs: last_moment_kernel(*refs, cols=cols, count=count),
            shape(size, LANE),
            aliases={0: 0},
        )(first, t, sl, sr)
        first = over_all(first, n_red, n_z)

        wide, part = shape(cols, 2 * face), shape(cols, face)
        sl0, sr0, t1, _, _, t2, sl2, sr2, t3, sl3, _ = chain
        sl, sr, z0, w1c, r1, w0, base, scal = call(
            lambda *refs: coarse_kernel(*refs, cols=cols, count=count),
            (part, part, wide, wide, part, part, shape(4 * cols, rows), shape(cols, LANE)),
        )(first, coarse_inverse, schur_p, sl0, sr0, t1, t2, sl2, sr2, t3, sl3)
        near = exchange(sl, sr)
        n0, z1, ul, ur = call(dual_kernel, (wide, part, part, part))(
            sl, sr, *near, mask, z0, scal, inv_p
        )
        near = exchange(ul, ur)
        w1, sl, sr = call(precondition_kernel, (part, part, part))(
            ul, ur, *near, mask, w1c, schur_p
        )
        near = exchange(sl, sr)
        size = up(13 * cols + MOVED, 8 * n_red)
        second, field, dual = call(
            lambda *refs: combine_kernel(*refs, cols=cols, count=count),
            (shape(size, LANE), shape(4 * cols, rows), shape(3 * cols, face)),
        )(sl, sr, *near, mask, n0, inv_p, scal, z0, z1, ul, ur, r1, w0, w1, base, mass_p, prev_p, gram)
        second = over_all(second, n_red, n_z)
        block, multi, coefficients, factor = call(
            lambda *refs: final_kernel(*refs, cols=cols, count=count),
            (shape(cols, rows), shape(cols, face), shape(cols, count), shape(cols, cols)),
        )(second, first, scal, field, dual, prev_p, nm_row)
        return block.T[None, None], multi.T[None, None], coefficients.T, factor

    split = (along, ("x", "c"))
    return jax.shard_map(
        on_device,
        mesh=fine,
        in_specs=(
            P(*split, None, None),
            P(*split, None, None),
            P(*split, None, None),
            P(*split, None),
            P(),
            P(*split, None),
            P(*split, None, None),
            P(*split, None, None),
            P(*split, None),
        ),
        out_specs=(P(*split, None, None), P(*split, None, None), P(), P()),
        check_vma=False,
    )
```

```python
import jax
import jax.numpy as jnp
import numpy as np
from jax import lax
from jax.experimental import pallas as pl
from jax.experimental.pallas import tpu as pltpu
from jax.sharding import Mesh, PartitionSpec as P

HI = lax.Precision.HIGHEST
F32 = jnp.float32
BF16 = jnp.bfloat16
RED = ("y", "zl", "x", "c")
LEVELS = 3
LANE = 128


def nn(a, b):
    return jnp.dot(a, b, precision=HI, preferred_element_type=F32)


def nt(a, b):
    return lax.dot_general(
        a, b, (((1,), (1,)), ((), ())), precision=HI, preferred_element_type=F32
    )


def lane_sum(a):
    return jnp.sum(a, axis=1, keepdims=True)


def call(kernel, outs, aliases={}):
    return pl.pallas_call(
        kernel,
        out_shape=outs,
        input_output_aliases=aliases,
        compiler_params=pltpu.CompilerParams(vmem_limit_bytes=12 * 1024 * 1024),
    )


def split_dot(t, mat, parts=2):
    pieces = []
    for _ in range(parts - 1):
        pieces.append(t.astype(BF16).astype(F32))
        t = t - pieces[-1]
    wide = jnp.concatenate(pieces + [t], axis=0).astype(BF16)
    wide = jnp.dot(wide, mat, preferred_element_type=F32)
    rows = t.shape[0]
    return sum(wide[i * rows : (i + 1) * rows] for i in range(1, parts)) + wide[:rows]


def to_order(nm_row, face):
    nm = jnp.transpose(jnp.broadcast_to(nm_row.astype(F32), (8, face)))[:, 0:1]
    return (nm == lax.broadcasted_iota(jnp.int32, (face, face), 1).astype(F32)).astype(F32)


def from_order(nm_row, face):
    return (nm_row == lax.broadcasted_iota(jnp.int32, (face, face), 0)).astype(F32)


def start_kernel(inv_hbm, load_hbm, basis_hbm, nm_hbm, corner_hbm, sl_ref, sr_ref, cl_ref,
                 inv_ref, load_ref, basis_ref, nm_ref, corner_ref, sems):
    pairs = (
        (nm_hbm, nm_ref), (load_hbm, load_ref), (basis_hbm, basis_ref), (corner_hbm, corner_ref),
        (inv_hbm, inv_ref),
    )
    copies = [pltpu.make_async_copy(src, dst, sems.at[i]) for i, (src, dst) in enumerate(pairs)]
    for copy in copies:
        copy.start()
    for copy in copies[:-1]:
        copy.wait()
    face = nm_ref.shape[1]
    cols = load_ref.shape[0]
    corners = basis_ref.shape[0]
    rows = cols + corners
    load = load_ref[...]
    basis = basis_ref[...]
    order = to_order(nm_ref[...], face).astype(BF16)
    cl_ref[...] = nt(load, basis)
    for ref in (sl_ref, sr_ref):
        ref[rows : rows + 8, :] = jnp.zeros((8, face), F32)
        ref[rows : rows + 1, 0:corners] = corner_ref[...].astype(F32)
    sr_ref[cols:rows, :] = basis[:, face:]
    copies[-1].wait()
    wide = split_dot(load, inv_ref[...])
    sr_ref[0:cols, :] = wide[:, face:]
    left = [wide[:, :face], basis[:, :face], jnp.zeros((8, face), F32)]
    left = split_dot(jnp.concatenate(left, axis=0), order, 3)
    sl_ref[0:rows, :] = left[0:rows]


def matrix_kernel(src, nm_ref, dst):
    face = nm_ref.shape[1]
    order = to_order(nm_ref[...], face).astype(BF16)
    back = from_order(nm_ref[...], face).astype(BF16)
    dst[:, face:] = src[:, face:]
    dst[:, :face] = jnp.dot(src[:, :face], order, preferred_element_type=F32).astype(BF16)
    dst[:face, :] = jnp.dot(back, dst[:face, :], preferred_element_type=F32).astype(BF16)


def basis_kernel(prev_ref, nm_ref, mass_ref, prev_out, flip_out, mass_out, gram_out, *, total):
    face = nm_ref.shape[1]
    back = from_order(nm_ref[...], face).astype(BF16)
    prev_out[face:, :] = prev_ref[face:, :]
    prev_out[:face, :] = jnp.dot(back, prev_ref[:face, :], preferred_element_type=F32).astype(BF16)
    flip_out[...] = jnp.transpose(prev_out[...].astype(F32)).astype(BF16)
    mass = mass_ref[...] / total
    mass_out[:, face:] = mass[:, face:]
    left = jnp.broadcast_to(mass[:, :face], (8, face))
    mass_out[:, :face] = nn(left, to_order(nm_ref[...], face))[0:1]
    column = jnp.transpose(jnp.broadcast_to(mass, (8, mass.shape[1])))[:, 0:1]
    wide = prev_ref[...].astype(F32)
    gram_out[...] = lax.dot_general(
        wide * column, wide, (((0,), (0,)), ((), ())), precision=HI, preferred_element_type=F32
    )


def step_kernel(sl_ref, sr_ref, nl_ref, pr_ref, mask_ref, mat_ref, t_ref, ol_ref, or_ref,
                *, cols, width, scale):
    face = sl_ref.shape[1]
    new = width + 16
    rows = cols + new
    old = cols + width
    for lanes, own, other, shift in (
        (slice(0, face), sl_ref, pr_ref, 0),
        (slice(face, 2 * face), sr_ref, nl_ref, 16),
    ):
        keep = mask_ref[0:1, lanes]
        t_ref[0:cols, lanes] = (own[0:cols, :] - other[0:cols, :]) * keep
        edge = jnp.zeros((8, face), F32)
        mine = jnp.concatenate([edge, own[cols:old, :], edge], axis=0)
        blank = jnp.zeros((16, face), F32)
        theirs = other[cols:old, :]
        theirs = jnp.concatenate([theirs, blank] if shift == 0 else [blank, theirs], axis=0)
        t_ref[cols:rows, lanes] = (mine - theirs) * keep
    v = split_dot(t_ref[...], mat_ref[...])
    if scale != 1.0:
        v = v * scale
    ids = jnp.concatenate(
        [
            pr_ref[old : old + 8, 0:8],
            sl_ref[old : old + 8, 0:width],
            nl_ref[old : old + 8, width - 8 : width],
        ],
        axis=1,
    )
    for ref, lanes in ((ol_ref, slice(0, face)), (or_ref, slice(face, 2 * face))):
        ref[0:rows, :] = v[:, lanes]
        ref[rows : rows + 8, :] = jnp.zeros((8, face), F32)
        ref[rows : rows + 8, 0:new] = ids


def one_hot(ids, count):
    dof = lax.broadcasted_iota(jnp.int32, (count, ids.shape[1]), 0).astype(F32)
    return (ids == dof).astype(F32)


def lower(half):
    row = lax.broadcasted_iota(jnp.int32, (half, half), 0)
    col = lax.broadcasted_iota(jnp.int32, (half, half), 1)
    return row, col


def pack(ref, k, matrix, diagonals):
    half = LANE
    at = 2 * half * k
    row, col = lower(half)
    last = matrix[half:, half:]
    ref[at : at + half, :] = jnp.where(row >= col, matrix[:half, :half], last)
    ref[at + half : at + 2 * half, :] = matrix[half:, :half]
    ref[diagonals + k : diagonals + k + 1, :] = jnp.sum(
        jnp.where(row == col, last, 0.0), axis=0, keepdims=True
    )


def unpack(ref, k, diagonals):
    half = LANE
    at = 2 * half * k
    row, col = lower(half)
    shared = ref[at : at + half, :]
    flipped = jnp.transpose(shared)
    cross = ref[at + half : at + 2 * half, :]
    first = jnp.where(row >= col, shared, flipped)
    last = jnp.where(row < col, shared, flipped)
    last = jnp.where(row == col, ref[diagonals + k : diagonals + k + 1, :], last)
    return jnp.concatenate(
        [
            jnp.concatenate([first, jnp.transpose(cross)], axis=1),
            jnp.concatenate([cross, last], axis=1),
        ],
        axis=0,
    )


def level_moments(out, refs, k, cols, count):
    base = 4 * count
    t_ref, l_ref, r_ref = refs
    rows, double = t_ref.shape
    face = double // 2
    width = rows - cols
    spot = one_hot(l_ref[rows : rows + 1, 0:width], count)
    tl, tr = t_ref[cols:rows, :face], t_ref[cols:rows, face:]
    inner = nt(tl, l_ref[cols:rows, :]) + nt(tr, r_ref[cols:rows, :])
    pack(out, k, nt(nn(spot, inner), spot), base + 9 * cols)
    cross = nt(l_ref[0:cols, :], tl) + nt(r_ref[0:cols, :], tr)
    put(out, base + 2 * cols * (k + 1), nt(cross, spot))
    return lane_sum(t_ref[0:cols, :face] * l_ref[0:cols, :]) + lane_sum(
        t_ref[0:cols, face:] * r_ref[0:cols, :]
    )


def put(out, at, block):
    cols, half = block.shape[0], block.shape[1] // 2
    out[at : at + cols, :] = block[:, :half]
    out[at + cols : at + 2 * cols, :] = block[:, half:]


def in_lanes(items, start=0):
    cols = items[0].shape[0]
    lane = lax.broadcasted_iota(jnp.int32, (cols, LANE), 1)
    block = jnp.zeros((cols, LANE), F32)
    for k, item in enumerate(items):
        block = jnp.where(lane == start + k, item, block)
    return block


def moment_kernel(sl0_ref, cl_ref, gram_ref, *refs, cols, count):
    out = refs[-1]
    base = 4 * count
    at = base + 8 * cols
    out[at:, :] = jnp.zeros((out.shape[0] - at, LANE), F32)
    own = sl0_ref.shape[0] - cols - 8
    spot = one_hot(sl0_ref[cols + own : cols + own + 1, 0:own], count)
    put(out, base, nt(cl_ref[...], spot))
    sums = [level_moments(out, refs[3 * k : 3 * k + 3], k, cols, count) for k in range(2)]
    pack(out, 3, gram_ref[...], at + cols)
    out[at : at + cols, :] = in_lanes(sums)


def last_moment_kernel(given_ref, *refs, cols, count):
    out = refs[-1]
    total = level_moments(out, refs[:3], 2, cols, count)
    at = 4 * count + 8 * cols
    out[at : at + cols, :] = given_ref[at : at + cols, :] + in_lanes([total], 2)


def coarse_kernel(sums_ref, coarse_ref, mat_ref, sl0, sr0, t1, t2, sl2, sr2, t3, sl3,
                  ol_ref, or_ref, z0_ref, w1c_ref, r1_ref, w0_ref, field_ref, scal_ref,
                  *, cols, count):
    base = 4 * count
    face = sl0.shape[1]

    def get(at):
        return jnp.concatenate(
            [sums_ref[at : at + cols, :], sums_ref[at + cols : at + 2 * cols, :]], axis=1
        )

    m0, m1, m2 = (unpack(sums_ref, k, base + 9 * cols) for k in range(3))
    coarse = coarse_ref[...]
    c_load, w0x, w1x, w2x = (get(base + 2 * cols * k) for k in range(4))
    at = base + 8 * cols
    s0, s1, s2 = (sums_ref[at : at + cols, k : k + 1] for k in range(3))
    g0 = nn(c_load, coarse)
    m0g0, m1g0, m2g0 = nn(g0, m0), nn(g0, m1), nn(g0, m2)
    c0 = w0x + m0g0
    g1 = nn(c0, coarse)
    m0g1, m1g1 = nn(g1, m0), nn(g1, m1)
    rz0 = s0 + lane_sum(2.0 * w0x * g0 + g0 * m0g0)
    del0 = s1 + lane_sum(2.0 * w1x * g0 + g0 * m1g0 + c0 * g1)
    nu0 = s2 + lane_sum(2.0 * w2x * g0 + g0 * m2g0 + 2.0 * w1x * g1 + 2.0 * g1 * m1g0 + g1 * m0g1)
    al0 = rz0 / del0
    be1 = (rz0 - 2.0 * al0 * del0 + al0 * al0 * nu0) / rz0
    cz1 = c0 - al0 * (w1x + m1g0 + m0g1)
    gz1 = nn(cz1, coarse)
    cm = (
        (1.0 + be1) * (w1x + m1g0)
        - al0 * (m1g1 + w2x + m2g0)
        + nn(gz1, m0)
        + be1 * m0g1
    )
    gm = nn(cm, coarse)
    spot = one_hot(sl3[sl3.shape[0] - 8 : sl3.shape[0] - 7, 0:LANE], count)
    local = nn(jnp.concatenate([g0, g1, gz1, gm], axis=0), spot)

    def spread(k, ref, first, n, lanes):
        width = 8 * (2 * k + 1)
        lane = 8 * (LEVELS - k)
        wide = nn(local[first * cols : (first + n) * cols, lane : lane + width],
                  ref[cols : cols + width, lanes])
        return [wide[i * cols : (i + 1) * cols] for i in range(n)]

    every, right = slice(0, 2 * face), slice(face, 2 * face)
    p10, p11, p1z = spread(1, t1, 0, 3, every)
    (p20,) = spread(2, t2, 0, 1, every)
    (p30,) = spread(3, t3, 0, 1, every)
    z0_ref[...] = t2[0:cols, :] + p20
    w0 = t3[0:cols, :] + p30 + p11
    w0_ref[...] = w0[:, right]
    w1c_ref[...] = p1z
    r1_ref[...] = t1[0:cols, right] + p10[:, right] - al0 * w0[:, right]
    v = split_dot(w0, mat_ref[...]) * 0.25
    ol_ref[...] = v[:, :face]
    or_ref[...] = v[:, right]
    for own, u, lanes in ((sl0, sl2, slice(0, face)), (sr0, sr2, right)):
        corner = spread(0, own, 0, 4, slice(0, face))
        field_ref[0:cols, lanes] = own[0:cols, :] + corner[0]
        (u0,) = spread(2, u, 0, 1, slice(0, face))
        field_ref[cols : 2 * cols, lanes] = u[0:cols, :] + u0 + corner[1]
        field_ref[2 * cols : 3 * cols, lanes] = corner[2]
        field_ref[3 * cols : 4 * cols, lanes] = corner[3]
    scal_ref[...] = in_lanes([al0, be1, lane_sum(cm * gm)])


def joined(own_ref, other_ref, mask_ref, left):
    face = own_ref.shape[1]
    lanes = slice(0, face) if left else slice(face, 2 * face)
    return (own_ref[...] - other_ref[...]) * mask_ref[0:1, lanes]


def field_of(sl_ref, sr_ref, nl_ref, pr_ref, mask_ref):
    return jnp.concatenate(
        [joined(sl_ref, pr_ref, mask_ref, True), joined(sr_ref, nl_ref, mask_ref, False)], axis=1
    )


def dual_kernel(sl_ref, sr_ref, nl_ref, pr_ref, mask_ref, z0_ref, scal_ref, mat_ref,
                n0_ref, z1_ref, ol_ref, or_ref):
    face = sl_ref.shape[1]
    n0 = field_of(sl_ref, sr_ref, nl_ref, pr_ref, mask_ref)
    z1 = z0_ref[...] - scal_ref[:, 0:1] * n0
    n0_ref[...] = n0
    z1_ref[...] = z1[:, face:]
    u = split_dot(z1, mat_ref[...])
    ol_ref[...] = u[:, :face]
    or_ref[...] = u[:, face:]


def precondition_kernel(sl_ref, sr_ref, nl_ref, pr_ref, mask_ref, w1c_ref, mat_ref,
                        w1_ref, ol_ref, or_ref):
    face = sl_ref.shape[1]
    w1 = field_of(sl_ref, sr_ref, nl_ref, pr_ref, mask_ref) + w1c_ref[...]
    w1_ref[...] = w1[:, face:]
    v = split_dot(w1, mat_ref[...]) * 0.25
    ol_ref[...] = v[:, :face]
    or_ref[...] = v[:, face:]


def combine_kernel(sl_ref, sr_ref, nl_ref, pr_ref, mask_ref, n0_ref, mat_ref, scal_ref, z0_ref,
                   z1_ref, ul_ref, ur_ref, r1_ref, w0_ref, w1_ref, base_ref, mass_ref, prev_ref,
                   out_ref, field_ref, dual_ref, *, cols, count):
    half = count // 2
    face = sl_ref.shape[1]
    be1 = scal_ref[:, 1:2]
    whole = field_of(sl_ref, sr_ref, nl_ref, pr_ref, mask_ref) + be1 * n0_ref[...]
    u = split_dot(whole, mat_ref[...])
    field_ref[0 : 2 * cols, :] = base_ref[0 : 2 * cols, :]
    third, fourth = slice(2 * cols, 3 * cols), slice(3 * cols, 4 * cols)
    field_ref[third, 0:face] = base_ref[third, 0:face] + ul_ref[...]
    field_ref[third, face:] = base_ref[third, face:] + ur_ref[...]
    field_ref[fourth, :] = base_ref[fourth, :] + u
    m = whole[:, face:]
    z0, z1, w0, w1, r1 = z0_ref[:, face:], z1_ref[...], w0_ref[...], w1_ref[...], r1_ref[...]
    q1 = w1 + be1 * w0
    p1 = z1 + be1 * z0
    for i, item in enumerate((z0, z1, m)):
        dual_ref[i * cols : (i + 1) * cols, :] = item
    moments = (
        lane_sum(r1 * z1), lane_sum(r1 * m), lane_sum(q1 * z1), lane_sum(q1 * m),
        lane_sum(r1 * p1), lane_sum(p1 * q1), lane_sum(z1 * w1), lane_sum(m * w1),
        lane_sum(whole * u),
    )
    field = field_ref[...]
    scaled = field * mass_ref[...]
    tq = split_dot(scaled, prev_ref[...], 3)
    out_ref[0 : 4 * cols, :] = tq[:, :half]
    out_ref[4 * cols : 8 * cols, :] = tq[:, half:]
    out_ref[8 * cols : 12 * cols, :] = nt(scaled, field)
    out_ref[12 * cols : 13 * cols, :] = in_lanes(moments)
    out_ref[13 * cols :, :] = jnp.zeros((out_ref.shape[0] - 13 * cols, LANE), F32)


def final_kernel(sums_ref, early_ref, scal_ref, field_ref, dual_ref, prev_ref, nm_ref,
                 block_ref, multi_ref, coef_ref, factor_ref, *, cols, count):
    half = count // 2
    face = dual_ref.shape[1]
    at = 12 * cols
    r1z1, r1m, q1z1, q1m, r1p1, p1q1, z1w1, mw1, mm = (
        sums_ref[at : at + cols, k : k + 1] for k in range(9)
    )
    al0, be1, extra = (scal_ref[:, k : k + 1] for k in range(3))
    mfm = mm + extra
    al1 = r1p1 / p1q1
    z2q1 = q1z1 - al1 * q1m
    be2 = -z2q1 / p1q1
    rz2 = r1z1 - al1 * (r1m + q1z1) + al1 * al1 * q1m
    z2fz2 = z1w1 - 2.0 * al1 * mw1 + al1 * al1 * mfm
    al2 = rz2 / (z2fz2 + 2.0 * be2 * z2q1 + be2 * be2 * p1q1)
    along = al1 + al2 * be2
    parts = (al0 + along * be1, along + al2, -al1 * al2)
    multi = sum(y * dual_ref[i * cols : (i + 1) * cols, :] for i, y in enumerate(parts))
    multi_ref[...] = multi
    weights = [jnp.ones((cols, 1), F32)] + [-y for y in parts]
    primal = sum(y * field_ref[i * cols : (i + 1) * cols, :] for i, y in enumerate(weights))
    g1 = sum(
        y
        * jnp.concatenate(
            [sums_ref[i * cols : (i + 1) * cols, :], sums_ref[(4 + i) * cols : (5 + i) * cols, :]],
            axis=1,
        )
        for i, y in enumerate(weights)
    )
    row = lax.broadcasted_iota(jnp.int32, (cols, cols), 0)
    col = lax.broadcasted_iota(jnp.int32, (cols, cols), 1)
    eye = (row == col).astype(F32)
    stacked = jnp.concatenate(weights, axis=0)
    across = jnp.concatenate([jnp.sum(y * eye, axis=0, keepdims=True) for y in weights], axis=1)
    tiles = stacked * sums_ref[8 * cols : 12 * cols, :] * across
    tiles = sum(tiles[i * cols : (i + 1) * cols] for i in range(4))
    gram = sum(tiles[:, j * cols : (j + 1) * cols] for j in range(4))
    basis = unpack(early_ref, 3, 4 * count + 9 * cols)
    c = 2.0 * g1 - nn(g1, basis)
    coef_ref[...] = c
    gram = gram + nt(c, nn(c, basis) - 2.0 * g1)
    gram = 0.5 * (gram + jnp.transpose(gram))
    final = primal - split_dot(c, prev_ref[...], 3)
    work = jnp.concatenate([gram, eye], axis=1)
    index = lax.broadcasted_iota(jnp.int32, (cols, 1), 0)
    pivots = jnp.zeros((cols, 1), F32)
    for k in range(cols):
        pivot = work[k : k + 1, k : k + 1]
        pivots = jnp.where(index == k, pivot, pivots)
        times = jnp.where(index > k, work[:, k : k + 1], 0.0) / pivot
        work = work - times * work[k : k + 1, :]
    work = work / jnp.sqrt(pivots)
    factor_ref[...] = jnp.transpose(jnp.where(row <= col, work[:, :cols], 0.0))
    solved = nn(work[:, cols:], final)
    left = split_dot(solved[:, :face], from_order(nm_ref[...], face).astype(BF16), 3)
    block_ref[:, :face] = left
    block_ref[:, face:] = solved[:, face:]


def sum_kernel(parts_ref, out_ref):
    total = jnp.sum(parts_ref[...], axis=0)
    for i in range(out_ref.shape[0]):
        out_ref[i] = total


def swap(parts, axes):
    return lax.all_to_all(parts, axes, 0, 0, tiled=True)


def summed(parts, copies):
    return call(sum_kernel, jax.ShapeDtypeStruct((copies,) + parts.shape[1:], F32))(parts)


def over_all(rows, n_red, n_z):
    parts = swap(rows.reshape(n_red, rows.shape[0] // n_red, LANE), RED)
    parts = swap(summed(parts, n_z), "zh")
    return swap(summed(parts, n_red), RED).reshape(rows.shape)


def up(count, unit):
    return -(-count // unit) * unit


def solution(mesh):
    n_sub, n_grp = mesh.shape["sub"], mesh.shape["grp"]
    n_y = min(4, n_sub)
    n_zl, n_c = 2, 2
    n_z = n_sub // n_y // n_zl
    n_x = n_grp // n_c
    devices = np.asarray(mesh.devices).reshape(n_y, n_z, n_zl, n_x, n_c)
    fine = Mesh(devices, ("y", "zh", "zl", "x", "c"))
    n_red = n_y * n_zl * n_x * n_c
    along = ("y", "zh", "zl")
    ahead = [(i, i + 1) for i in range(n_sub - 1)]
    behind = [(i + 1, i) for i in range(n_sub - 1)]

    def on_device(schur_inverse, schur, coarse_basis, corner_index, coarse_inverse, neighbor_map,
                  load, previous, mass):
        inverse_block, schur_block, basis = schur_inverse[0, 0], schur[0, 0], coarse_basis[0, 0]
        corners, nm = corner_index[0, 0], neighbor_map[0, 0]
        rhs, earlier, weights = load[0, 0].T, previous[0, 0], mass[0, 0]
        cols, rows = rhs.shape
        face = nm.shape[0]
        count = coarse_inverse.shape[0]
        total = rows * n_sub * n_grp
        own = corners.shape[0]
        position = lax.axis_index(along)
        nm_row = nm[None, :]
        side = jnp.arange(2 * face) < face
        mask = jnp.where(side, position > 0, position < n_sub - 1).astype(F32)[None, :]
        mask = jnp.broadcast_to(mask, (8, 2 * face))

        def shape(*dims):
            return jax.ShapeDtypeStruct(dims, F32)

        half = shape(cols + own + 8, face)
        sl, sr, cl = pl.pallas_call(
            start_kernel,
            out_shape=(half, half, shape(cols, own)),
            in_specs=[pl.BlockSpec(memory_space=pl.ANY)] * 5,
            scratch_shapes=[
                pltpu.VMEM((rows, rows), BF16),
                pltpu.VMEM((cols, rows), F32),
                pltpu.VMEM((own, rows), F32),
                pltpu.VMEM((1, face), jnp.int32),
                pltpu.VMEM((1, own), jnp.int32),
                pltpu.SemaphoreType.DMA((5,)),
            ],
            compiler_params=pltpu.CompilerParams(vmem_limit_bytes=60 * 1024 * 1024),
        )(inverse_block, rhs, basis, nm_row, corners[None, :])
        square = jax.ShapeDtypeStruct((rows, rows), BF16)

        def exchange(sl, sr):
            return lax.ppermute(sl, along, behind), lax.ppermute(sr, along, ahead)

        def step(k, sl, sr, near, mat):
            width = own + 16 * (k - 1)
            out = cols + width + 16
            return call(
                lambda *refs: step_kernel(
                    *refs, cols=cols, width=width, scale=0.25 if k % 2 == 1 else 1.0
                ),
                (shape(out, 2 * face), shape(out + 8, face), shape(out + 8, face)),
            )(sl, sr, *near, mask, mat)

        chain = [sl, sr]
        near = exchange(sl, sr)
        schur_p = call(matrix_kernel, square)(schur_block, nm_row)
        t, sl, sr = step(1, sl, sr, near, schur_p)
        chain += [t, sl, sr]
        near = exchange(sl, sr)
        inv_p = call(matrix_kernel, square)(inverse_block, nm_row)
        prev_p, prev_t, mass_p, gram = call(
            lambda *refs: basis_kernel(*refs, total=total),
            (
                jax.ShapeDtypeStruct(earlier.shape, BF16),
                jax.ShapeDtypeStruct(earlier.shape[::-1], BF16),
                shape(1, rows),
                shape(count, count),
            ),
        )(earlier, nm_row, weights[None, :])
        near, gram = lax.optimization_barrier((near, gram))
        t, sl, sr = step(2, sl, sr, near, inv_p)
        chain += [t, sl, sr]
        near = exchange(sl, sr)
        size = up(4 * count + 9 * cols + 8, 8 * n_red)
        first = call(
            lambda *refs: moment_kernel(*refs, cols=cols, count=count), shape(size, LANE)
        )(chain[0], cl, gram, *chain[2:8])
        t, sl, sr = step(3, sl, sr, near, schur_p)
        chain += [t, sl, sr]
        first = call(
            lambda *refs: last_moment_kernel(*refs, cols=cols, count=count),
            shape(size, LANE),
            aliases={0: 0},
        )(first, t, sl, sr)
        first = over_all(first, n_red, n_z)

        wide, part = shape(cols, 2 * face), shape(cols, face)
        sl0, sr0, t1, _, _, t2, sl2, sr2, t3, sl3, _ = chain
        sl, sr, z0, w1c, r1, w0, base, scal = call(
            lambda *refs: coarse_kernel(*refs, cols=cols, count=count),
            (part, part, wide, wide, part, part, shape(4 * cols, rows), shape(cols, LANE)),
        )(first, coarse_inverse, schur_p, sl0, sr0, t1, t2, sl2, sr2, t3, sl3)
        near = exchange(sl, sr)
        n0, z1, ul, ur = call(dual_kernel, (wide, part, part, part))(
            sl, sr, *near, mask, z0, scal, inv_p
        )
        near = exchange(ul, ur)
        w1, sl, sr = call(precondition_kernel, (part, part, part))(
            ul, ur, *near, mask, w1c, schur_p
        )
        near = exchange(sl, sr)
        size = up(13 * cols, 8 * n_red)
        second, field, dual = call(
            lambda *refs: combine_kernel(*refs, cols=cols, count=count),
            (shape(size, LANE), shape(4 * cols, rows), shape(3 * cols, face)),
        )(sl, sr, *near, mask, n0, inv_p, scal, z0, z1, ul, ur, r1, w0, w1, base, mass_p, prev_p)
        second = over_all(second, n_red, n_z)
        block, multi, coefficients, factor = call(
            lambda *refs: final_kernel(*refs, cols=cols, count=count),
            (shape(cols, rows), shape(cols, face), shape(cols, count), shape(cols, cols)),
        )(second, first, scal, field, dual, prev_t, nm_row)
        return block.T[None, None], multi.T[None, None], coefficients.T, factor

    split = (along, ("x", "c"))
    return jax.shard_map(
        on_device,
        mesh=fine,
        in_specs=(
            P(*split, None, None),
            P(*split, None, None),
            P(*split, None, None),
            P(*split, None),
            P(),
            P(*split, None),
            P(*split, None, None),
            P(*split, None, None),
            P(*split, None),
        ),
        out_specs=(P(*split, None, None), P(*split, None, None), P(), P()),
        check_vma=False,
    )
```

```python
import jax
import jax.numpy as jnp
import numpy as np
from jax import lax
from jax.experimental import pallas as pl
from jax.experimental.pallas import tpu as pltpu
from jax.sharding import Mesh, PartitionSpec as P

HI = lax.Precision.HIGHEST
F32 = jnp.float32
BF16 = jnp.bfloat16
RED = ("y", "zl", "x", "c")
LEVELS = 3
LANE = 128


def nn(a, b):
    return jnp.dot(a, b, precision=HI, preferred_element_type=F32)


def nt(a, b):
    return lax.dot_general(
        a, b, (((1,), (1,)), ((), ())), precision=HI, preferred_element_type=F32
    )


def lane_sum(a):
    return jnp.sum(a, axis=1, keepdims=True)


def call(kernel, outs, aliases={}):
    return pl.pallas_call(
        kernel,
        out_shape=outs,
        input_output_aliases=aliases,
        compiler_params=pltpu.CompilerParams(vmem_limit_bytes=12 * 1024 * 1024),
    )


def split_dot(t, mat, parts=2):
    pieces = []
    for _ in range(parts - 1):
        pieces.append(t.astype(BF16).astype(F32))
        t = t - pieces[-1]
    wide = jnp.concatenate(pieces + [t], axis=0).astype(BF16)
    wide = jnp.dot(wide, mat, preferred_element_type=F32)
    rows = t.shape[0]
    return sum(wide[i * rows : (i + 1) * rows] for i in range(1, parts)) + wide[:rows]


def to_order(nm_row, face):
    nm = jnp.transpose(jnp.broadcast_to(nm_row.astype(F32), (8, face)))[:, 0:1]
    return (nm == lax.broadcasted_iota(jnp.int32, (face, face), 1).astype(F32)).astype(F32)


def from_order(nm_row, face):
    return (nm_row == lax.broadcasted_iota(jnp.int32, (face, face), 0)).astype(F32)


def start_kernel(inv_hbm, load_hbm, basis_hbm, nm_hbm, corner_hbm, sl_ref, sr_ref, cl_ref,
                 inv_ref, load_ref, basis_ref, nm_ref, corner_ref, sems):
    pairs = (
        (nm_hbm, nm_ref), (load_hbm, load_ref), (basis_hbm, basis_ref), (corner_hbm, corner_ref),
        (inv_hbm, inv_ref),
    )
    copies = [pltpu.make_async_copy(src, dst, sems.at[i]) for i, (src, dst) in enumerate(pairs)]
    for copy in copies:
        copy.start()
    for copy in copies[:-1]:
        copy.wait()
    face = nm_ref.shape[1]
    cols = load_ref.shape[0]
    corners = basis_ref.shape[0]
    rows = cols + corners
    load = load_ref[...]
    basis = basis_ref[...]
    order = to_order(nm_ref[...], face).astype(BF16)
    cl_ref[...] = nt(load, basis)
    for ref in (sl_ref, sr_ref):
        ref[rows : rows + 8, :] = jnp.zeros((8, face), F32)
        ref[rows : rows + 1, 0:corners] = corner_ref[...].astype(F32)
    sr_ref[cols:rows, :] = basis[:, face:]
    copies[-1].wait()
    wide = split_dot(load, inv_ref[...])
    sr_ref[0:cols, :] = wide[:, face:]
    left = [wide[:, :face], basis[:, :face], jnp.zeros((8, face), F32)]
    left = split_dot(jnp.concatenate(left, axis=0), order, 3)
    sl_ref[0:rows, :] = left[0:rows]


def matrix_kernel(src, nm_ref, dst):
    face = nm_ref.shape[1]
    order = to_order(nm_ref[...], face).astype(BF16)
    back = from_order(nm_ref[...], face).astype(BF16)
    dst[:, face:] = src[:, face:]
    dst[:, :face] = jnp.dot(src[:, :face], order, preferred_element_type=F32).astype(BF16)
    dst[:face, :] = jnp.dot(back, dst[:face, :], preferred_element_type=F32).astype(BF16)


def basis_kernel(prev_ref, nm_ref, mass_ref, prev_out, flip_out, mass_out, gram_out, *, total):
    face = nm_ref.shape[1]
    back = from_order(nm_ref[...], face).astype(BF16)
    prev_out[face:, :] = prev_ref[face:, :]
    prev_out[:face, :] = jnp.dot(back, prev_ref[:face, :], preferred_element_type=F32).astype(BF16)
    flip_out[...] = jnp.transpose(prev_out[...].astype(F32)).astype(BF16)
    mass = mass_ref[...] / total
    mass_out[:, face:] = mass[:, face:]
    left = jnp.broadcast_to(mass[:, :face], (8, face))
    mass_out[:, :face] = nn(left, to_order(nm_ref[...], face))[0:1]
    column = jnp.transpose(jnp.broadcast_to(mass, (8, mass.shape[1])))[:, 0:1]
    wide = prev_ref[...].astype(F32)
    gram_out[...] = lax.dot_general(
        wide * column, wide, (((0,), (0,)), ((), ())), precision=HI, preferred_element_type=F32
    )


def step_kernel(sl_ref, sr_ref, nl_ref, pr_ref, mask_ref, mat_ref, t_ref, ol_ref, or_ref,
                *, cols, width, scale):
    face = sl_ref.shape[1]
    new = width + 16
    rows = cols + new
    old = cols + width
    for lanes, own, other, shift in (
        (slice(0, face), sl_ref, pr_ref, 0),
        (slice(face, 2 * face), sr_ref, nl_ref, 16),
    ):
        keep = mask_ref[0:1, lanes]
        t_ref[0:cols, lanes] = (own[0:cols, :] - other[0:cols, :]) * keep
        edge = jnp.zeros((8, face), F32)
        mine = jnp.concatenate([edge, own[cols:old, :], edge], axis=0)
        blank = jnp.zeros((16, face), F32)
        theirs = other[cols:old, :]
        theirs = jnp.concatenate([theirs, blank] if shift == 0 else [blank, theirs], axis=0)
        t_ref[cols:rows, lanes] = (mine - theirs) * keep
    v = split_dot(t_ref[...], mat_ref[...])
    if scale != 1.0:
        v = v * scale
    ids = jnp.concatenate(
        [
            pr_ref[old : old + 8, 0:8],
            sl_ref[old : old + 8, 0:width],
            nl_ref[old : old + 8, width - 8 : width],
        ],
        axis=1,
    )
    for ref, lanes in ((ol_ref, slice(0, face)), (or_ref, slice(face, 2 * face))):
        ref[0:rows, :] = v[:, lanes]
        ref[rows : rows + 8, :] = jnp.zeros((8, face), F32)
        ref[rows : rows + 8, 0:new] = ids


def one_hot(ids, count):
    dof = lax.broadcasted_iota(jnp.int32, (count, ids.shape[1]), 0).astype(F32)
    return (ids == dof).astype(F32)


def lower(half):
    row = lax.broadcasted_iota(jnp.int32, (half, half), 0)
    col = lax.broadcasted_iota(jnp.int32, (half, half), 1)
    return row, col


def pack(ref, k, matrix, diagonals):
    half = LANE
    at = 2 * half * k
    row, col = lower(half)
    last = matrix[half:, half:]
    ref[at : at + half, :] = jnp.where(row >= col, matrix[:half, :half], last)
    ref[at + half : at + 2 * half, :] = matrix[half:, :half]
    ref[diagonals + k : diagonals + k + 1, :] = jnp.sum(
        jnp.where(row == col, last, 0.0), axis=0, keepdims=True
    )


def unpack(ref, k, diagonals):
    half = LANE
    at = 2 * half * k
    row, col = lower(half)
    shared = ref[at : at + half, :]
    flipped = jnp.transpose(shared)
    cross = ref[at + half : at + 2 * half, :]
    first = jnp.where(row >= col, shared, flipped)
    last = jnp.where(row < col, shared, flipped)
    last = jnp.where(row == col, ref[diagonals + k : diagonals + k + 1, :], last)
    return jnp.concatenate(
        [
            jnp.concatenate([first, jnp.transpose(cross)], axis=1),
            jnp.concatenate([cross, last], axis=1),
        ],
        axis=0,
    )


def level_moments(out, refs, k, cols, count):
    base = 4 * count
    t_ref, l_ref, r_ref = refs
    rows, double = t_ref.shape
    face = double // 2
    width = rows - cols
    spot = one_hot(l_ref[rows : rows + 1, 0:width], count)
    tl, tr = t_ref[cols:rows, :face], t_ref[cols:rows, face:]
    inner = nt(nt(l_ref[0:rows, :], tl) + nt(r_ref[0:rows, :], tr), spot)
    put(out, base + 2 * cols * (k + 1), inner[0:cols])
    pack(out, k, nn(spot, inner[cols:rows]), base + 9 * cols)
    return lane_sum(t_ref[0:cols, :face] * l_ref[0:cols, :]) + lane_sum(
        t_ref[0:cols, face:] * r_ref[0:cols, :]
    )


def put(out, at, block):
    cols, half = block.shape[0], block.shape[1] // 2
    out[at : at + cols, :] = block[:, :half]
    out[at + cols : at + 2 * cols, :] = block[:, half:]


def in_lanes(items, start=0):
    cols = items[0].shape[0]
    lane = lax.broadcasted_iota(jnp.int32, (cols, LANE), 1)
    block = jnp.zeros((cols, LANE), F32)
    for k, item in enumerate(items):
        block = jnp.where(lane == start + k, item, block)
    return block


def moment_kernel(sl0_ref, cl_ref, gram_ref, *refs, cols, count):
    out = refs[-1]
    base = 4 * count
    at = base + 8 * cols
    out[at:, :] = jnp.zeros((out.shape[0] - at, LANE), F32)
    own = sl0_ref.shape[0] - cols - 8
    spot = one_hot(sl0_ref[cols + own : cols + own + 1, 0:own], count)
    put(out, base, nt(cl_ref[...], spot))
    sums = [level_moments(out, refs[3 * k : 3 * k + 3], k, cols, count) for k in range(2)]
    pack(out, 3, gram_ref[...], at + cols)
    out[at : at + cols, :] = in_lanes(sums)


def last_moment_kernel(given_ref, *refs, cols, count):
    out = refs[-1]
    total = level_moments(out, refs[:3], 2, cols, count)
    at = 4 * count + 8 * cols
    out[at : at + cols, :] = given_ref[at : at + cols, :] + in_lanes([total], 2)


def vector(sums_ref, k, cols, count):
    at = 4 * count + 2 * cols * k
    return jnp.concatenate([sums_ref[at : at + cols, :], sums_ref[at + cols : at + 2 * cols, :]], axis=1)


def at_corners(values, ids_ref):
    rows = ids_ref.shape[0]
    spot = one_hot(ids_ref[rows - 8 : rows - 7, 0:LANE], values.shape[1])
    return nn(values, spot)


def spread(local, k, ref, lanes, cols):
    width = 8 * (2 * k + 1)
    lane = 8 * (LEVELS - k)
    wide = nn(local[:, lane : lane + width], ref[cols : cols + width, lanes])
    return [wide[i : i + cols] for i in range(0, wide.shape[0], cols)]


def coarse_kernel(sums_ref, coarse_ref, mat_ref, t1, t3, sl3, ol_ref, or_ref, w0_ref,
                  *, cols, count):
    diagonals = 4 * count + 9 * cols
    face = ol_ref.shape[1]
    every = slice(0, 2 * face)
    g0 = nn(vector(sums_ref, 0, cols, count), coarse_ref[...])
    g1 = nn(vector(sums_ref, 1, cols, count) + nn(g0, unpack(sums_ref, 0, diagonals)), coarse_ref[...])
    local = at_corners(jnp.concatenate([g0, g1], axis=0), sl3)
    (p30,) = spread(local[0:cols], 3, t3, every, cols)
    (p11,) = spread(local[cols:], 1, t1, every, cols)
    w0 = t3[0:cols, :] + p30 + p11
    w0_ref[...] = w0
    v = split_dot(w0, mat_ref[...]) * 0.25
    ol_ref[...] = v[:, :face]
    or_ref[...] = v[:, face:]


def values_kernel(sums_ref, coarse_ref, nm_ref, sl0, sr0, t1, t2, sl2, sr2, sl3, w0_ref,
                  z0_ref, w1c_ref, r1_ref, field_ref, scal_ref, gram_ref, back_ref,
                  *, cols, count):
    diagonals = 4 * count + 9 * cols
    face = sl0.shape[1]
    m0, m1, m2 = (unpack(sums_ref, k, diagonals) for k in range(3))
    coarse = coarse_ref[...]
    c_load, w0x, w1x, w2x = (vector(sums_ref, k, cols, count) for k in range(4))
    at = 4 * count + 8 * cols
    s0, s1, s2 = (sums_ref[at : at + cols, k : k + 1] for k in range(3))
    g0 = nn(c_load, coarse)
    m0g0, m1g0, m2g0 = nn(g0, m0), nn(g0, m1), nn(g0, m2)
    c0 = w0x + m0g0
    g1 = nn(c0, coarse)
    m0g1, m1g1 = nn(g1, m0), nn(g1, m1)
    rz0 = s0 + lane_sum(2.0 * w0x * g0 + g0 * m0g0)
    del0 = s1 + lane_sum(2.0 * w1x * g0 + g0 * m1g0 + c0 * g1)
    nu0 = s2 + lane_sum(2.0 * w2x * g0 + g0 * m2g0 + 2.0 * w1x * g1 + 2.0 * g1 * m1g0 + g1 * m0g1)
    al0 = rz0 / del0
    be1 = (rz0 - 2.0 * al0 * del0 + al0 * al0 * nu0) / rz0
    cz1 = c0 - al0 * (w1x + m1g0 + m0g1)
    gz1 = nn(cz1, coarse)
    cm = (
        (1.0 + be1) * (w1x + m1g0)
        - al0 * (m1g1 + w2x + m2g0)
        + nn(gz1, m0)
        + be1 * m0g1
    )
    gm = nn(cm, coarse)
    local = at_corners(jnp.concatenate([g0, g1, gz1, gm], axis=0), sl3)
    every, right, whole = slice(0, 2 * face), slice(face, 2 * face), slice(0, face)
    (p20,) = spread(local[0:cols], 2, t2, every, cols)
    (p10,) = spread(local[0:cols], 1, t1, right, cols)
    (w1c_ref[...],) = spread(local[2 * cols : 3 * cols], 1, t1, every, cols)
    z0_ref[...] = t2[0:cols, :] + p20
    r1_ref[...] = t1[0:cols, right] + p10 - al0 * w0_ref[:, right]
    for own, u, lanes in ((sl0, sl2, slice(0, face)), (sr0, sr2, right)):
        corner = spread(local, 0, own, whole, cols)
        (u0,) = spread(local[0:cols], 2, u, whole, cols)
        field_ref[0:cols, lanes] = own[0:cols, :] + corner[0]
        field_ref[cols : 2 * cols, lanes] = u[0:cols, :] + u0 + corner[1]
        field_ref[2 * cols : 3 * cols, lanes] = corner[2]
        field_ref[3 * cols : 4 * cols, lanes] = corner[3]
    scal_ref[...] = in_lanes([al0, be1, lane_sum(cm * gm)])
    gram_ref[...] = unpack(sums_ref, 3, diagonals)
    back_ref[...] = from_order(nm_ref[...], face).astype(BF16)


def joined(own_ref, other_ref, mask_ref, left):
    face = own_ref.shape[1]
    lanes = slice(0, face) if left else slice(face, 2 * face)
    return (own_ref[...] - other_ref[...]) * mask_ref[0:1, lanes]


def field_of(sl_ref, sr_ref, nl_ref, pr_ref, mask_ref):
    return jnp.concatenate(
        [joined(sl_ref, pr_ref, mask_ref, True), joined(sr_ref, nl_ref, mask_ref, False)], axis=1
    )


def dual_kernel(sl_ref, sr_ref, nl_ref, pr_ref, mask_ref, z0_ref, scal_ref, mat_ref,
                n0_ref, z1_ref, ol_ref, or_ref):
    face = sl_ref.shape[1]
    n0 = field_of(sl_ref, sr_ref, nl_ref, pr_ref, mask_ref)
    z1 = z0_ref[...] - scal_ref[:, 0:1] * n0
    n0_ref[...] = n0
    z1_ref[...] = z1[:, face:]
    u = split_dot(z1, mat_ref[...])
    ol_ref[...] = u[:, :face]
    or_ref[...] = u[:, face:]


def precondition_kernel(sl_ref, sr_ref, nl_ref, pr_ref, mask_ref, w1c_ref, mat_ref,
                        w1_ref, ol_ref, or_ref):
    face = sl_ref.shape[1]
    w1 = field_of(sl_ref, sr_ref, nl_ref, pr_ref, mask_ref) + w1c_ref[...]
    w1_ref[...] = w1[:, face:]
    v = split_dot(w1, mat_ref[...]) * 0.25
    ol_ref[...] = v[:, :face]
    or_ref[...] = v[:, face:]


def combine_kernel(sl_ref, sr_ref, nl_ref, pr_ref, mask_ref, n0_ref, mat_ref, scal_ref, z0_ref,
                   z1_ref, ul_ref, ur_ref, r1_ref, w0_ref, w1_ref, base_ref, mass_ref, prev_ref,
                   out_ref, field_ref, dual_ref, *, cols, count):
    half = count // 2
    face = sl_ref.shape[1]
    be1 = scal_ref[:, 1:2]
    whole = field_of(sl_ref, sr_ref, nl_ref, pr_ref, mask_ref) + be1 * n0_ref[...]
    u = split_dot(whole, mat_ref[...])
    field_ref[0 : 2 * cols, :] = base_ref[0 : 2 * cols, :]
    third, fourth = slice(2 * cols, 3 * cols), slice(3 * cols, 4 * cols)
    field_ref[third, 0:face] = base_ref[third, 0:face] + ul_ref[...]
    field_ref[third, face:] = base_ref[third, face:] + ur_ref[...]
    field_ref[fourth, :] = base_ref[fourth, :] + u
    m = whole[:, face:]
    z0, w0 = z0_ref[:, face:], w0_ref[:, face:]
    z1, w1, r1 = z1_ref[...], w1_ref[...], r1_ref[...]
    q1 = w1 + be1 * w0
    p1 = z1 + be1 * z0
    for i, item in enumerate((z0, z1, m)):
        dual_ref[i * cols : (i + 1) * cols, :] = item
    moments = (
        lane_sum(r1 * z1), lane_sum(r1 * m), lane_sum(q1 * z1), lane_sum(q1 * m),
        lane_sum(r1 * p1), lane_sum(p1 * q1), lane_sum(z1 * w1), lane_sum(m * w1),
        lane_sum(whole * u),
    )
    field = field_ref[...]
    scaled = field * mass_ref[...]
    tq = split_dot(scaled, prev_ref[...], 3)
    out_ref[0 : 4 * cols, :] = tq[:, :half]
    out_ref[4 * cols : 8 * cols, :] = tq[:, half:]
    out_ref[8 * cols : 12 * cols, :] = nt(scaled, field)
    out_ref[12 * cols : 13 * cols, :] = in_lanes(moments)
    out_ref[13 * cols :, :] = jnp.zeros((out_ref.shape[0] - 13 * cols, LANE), F32)


def final_kernel(sums_ref, basis_ref, scal_ref, field_ref, dual_ref, prev_ref, back_ref,
                 block_ref, multi_ref, coef_ref, factor_ref, *, cols, count):
    half = count // 2
    face = dual_ref.shape[1]
    at = 12 * cols
    r1z1, r1m, q1z1, q1m, r1p1, p1q1, z1w1, mw1, mm = (
        sums_ref[at : at + cols, k : k + 1] for k in range(9)
    )
    al0, be1, extra = (scal_ref[:, k : k + 1] for k in range(3))
    mfm = mm + extra
    al1 = r1p1 / p1q1
    z2q1 = q1z1 - al1 * q1m
    be2 = -z2q1 / p1q1
    rz2 = r1z1 - al1 * (r1m + q1z1) + al1 * al1 * q1m
    z2fz2 = z1w1 - 2.0 * al1 * mw1 + al1 * al1 * mfm
    al2 = rz2 / (z2fz2 + 2.0 * be2 * z2q1 + be2 * be2 * p1q1)
    along = al1 + al2 * be2
    parts = (al0 + along * be1, along + al2, -al1 * al2)
    multi = sum(y * dual_ref[i * cols : (i + 1) * cols, :] for i, y in enumerate(parts))
    multi_ref[...] = multi
    weights = [jnp.ones((cols, 1), F32)] + [-y for y in parts]
    primal = sum(y * field_ref[i * cols : (i + 1) * cols, :] for i, y in enumerate(weights))
    g1 = sum(
        y
        * jnp.concatenate(
            [sums_ref[i * cols : (i + 1) * cols, :], sums_ref[(4 + i) * cols : (5 + i) * cols, :]],
            axis=1,
        )
        for i, y in enumerate(weights)
    )
    row = lax.broadcasted_iota(jnp.int32, (cols, cols), 0)
    col = lax.broadcasted_iota(jnp.int32, (cols, cols), 1)
    eye = (row == col).astype(F32)
    stacked = jnp.concatenate(weights, axis=0)
    across = jnp.concatenate([jnp.sum(y * eye, axis=0, keepdims=True) for y in weights], axis=1)
    tiles = stacked * sums_ref[8 * cols : 12 * cols, :] * across
    tiles = sum(tiles[i * cols : (i + 1) * cols] for i in range(4))
    gram = sum(tiles[:, j * cols : (j + 1) * cols] for j in range(4))
    basis = basis_ref[...]
    c = 2.0 * g1 - nn(g1, basis)
    coef_ref[...] = c
    gram = gram + nt(c, nn(c, basis) - 2.0 * g1)
    gram = 0.5 * (gram + jnp.transpose(gram))
    final = primal - split_dot(c, prev_ref[...], 3)
    work = jnp.concatenate([gram, eye], axis=1)
    index = lax.broadcasted_iota(jnp.int32, (cols, 1), 0)
    pivots = jnp.zeros((cols, 1), F32)
    for k in range(0, cols, 2):
        first = work[k : k + 1, :]
        pivot = first[:, k : k + 1]
        column = work[:, k : k + 1]
        ratio = first[:, k + 1 : k + 2] / pivot
        second = work[k + 1 : k + 2, :] - ratio * first
        follow = second[:, k + 1 : k + 2]
        other = work[:, k + 1 : k + 2] - ratio * column
        pivots = jnp.where(index == k, pivot, jnp.where(index == k + 1, follow, pivots))
        work = (
            work
            - (jnp.where(index > k, column, 0.0) / pivot) * first
            - (jnp.where(index > k + 1, other, 0.0) / follow) * second
        )
    work = work / jnp.sqrt(pivots)
    factor_ref[...] = jnp.transpose(jnp.where(row <= col, work[:, :cols], 0.0))
    solved = nn(work[:, cols:], final)
    left = split_dot(solved[:, :face], back_ref[...], 3)
    block_ref[:, :face] = left
    block_ref[:, face:] = solved[:, face:]


def sum_kernel(parts_ref, out_ref):
    total = jnp.sum(parts_ref[...], axis=0)
    for i in range(out_ref.shape[0]):
        out_ref[i] = total


def swap(parts, axes):
    return lax.all_to_all(parts, axes, 0, 0, tiled=True)


def summed(parts, copies):
    return call(sum_kernel, jax.ShapeDtypeStruct((copies,) + parts.shape[1:], F32))(parts)


def over_all(rows, n_red, n_z):
    parts = swap(rows.reshape(n_red, rows.shape[0] // n_red, LANE), RED)
    parts = swap(summed(parts, n_z), "zh")
    return swap(summed(parts, n_red), RED).reshape(rows.shape)


def up(count, unit):
    return -(-count // unit) * unit


def solution(mesh):
    n_sub, n_grp = mesh.shape["sub"], mesh.shape["grp"]
    n_y = min(4, n_sub)
    n_zl, n_c = 2, 2
    n_z = n_sub // n_y // n_zl
    n_x = n_grp // n_c
    devices = np.asarray(mesh.devices).reshape(n_y, n_z, n_zl, n_x, n_c)
    fine = Mesh(devices, ("y", "zh", "zl", "x", "c"))
    n_red = n_y * n_zl * n_x * n_c
    along = ("y", "zh", "zl")
    ahead = [(i, i + 1) for i in range(n_sub - 1)]
    behind = [(i + 1, i) for i in range(n_sub - 1)]

    def on_device(schur_inverse, schur, coarse_basis, corner_index, coarse_inverse, neighbor_map,
                  load, previous, mass):
        inverse_block, schur_block, basis = schur_inverse[0, 0], schur[0, 0], coarse_basis[0, 0]
        corners, nm = corner_index[0, 0], neighbor_map[0, 0]
        rhs, earlier, weights = load[0, 0].T, previous[0, 0], mass[0, 0]
        cols, rows = rhs.shape
        face = nm.shape[0]
        count = coarse_inverse.shape[0]
        total = rows * n_sub * n_grp
        own = corners.shape[0]
        position = lax.axis_index(along)
        nm_row = nm[None, :]
        side = jnp.arange(2 * face) < face
        mask = jnp.where(side, position > 0, position < n_sub - 1).astype(F32)[None, :]
        mask = jnp.broadcast_to(mask, (8, 2 * face))

        def shape(*dims):
            return jax.ShapeDtypeStruct(dims, F32)

        half = shape(cols + own + 8, face)
        sl, sr, cl = pl.pallas_call(
            start_kernel,
            out_shape=(half, half, shape(cols, own)),
            in_specs=[pl.BlockSpec(memory_space=pl.ANY)] * 5,
            scratch_shapes=[
                pltpu.VMEM((rows, rows), BF16),
                pltpu.VMEM((cols, rows), F32),
                pltpu.VMEM((own, rows), F32),
                pltpu.VMEM((1, face), jnp.int32),
                pltpu.VMEM((1, own), jnp.int32),
                pltpu.SemaphoreType.DMA((5,)),
            ],
            compiler_params=pltpu.CompilerParams(vmem_limit_bytes=60 * 1024 * 1024),
        )(inverse_block, rhs, basis, nm_row, corners[None, :])
        square = jax.ShapeDtypeStruct((rows, rows), BF16)

        def exchange(sl, sr):
            return lax.ppermute(sl, along, behind), lax.ppermute(sr, along, ahead)

        def step(k, sl, sr, near, mat):
            width = own + 16 * (k - 1)
            out = cols + width + 16
            return call(
                lambda *refs: step_kernel(
                    *refs, cols=cols, width=width, scale=0.25 if k % 2 == 1 else 1.0
                ),
                (shape(out, 2 * face), shape(out + 8, face), shape(out + 8, face)),
            )(sl, sr, *near, mask, mat)

        chain = [sl, sr]
        near = exchange(sl, sr)
        schur_p = call(matrix_kernel, square)(schur_block, nm_row)
        t, sl, sr = step(1, sl, sr, near, schur_p)
        chain += [t, sl, sr]
        near = exchange(sl, sr)
        inv_p = call(matrix_kernel, square)(inverse_block, nm_row)
        prev_p, prev_t, mass_p, gram = call(
            lambda *refs: basis_kernel(*refs, total=total),
            (
                jax.ShapeDtypeStruct(earlier.shape, BF16),
                jax.ShapeDtypeStruct(earlier.shape[::-1], BF16),
                shape(1, rows),
                shape(count, count),
            ),
        )(earlier, nm_row, weights[None, :])
        near, gram = lax.optimization_barrier((near, gram))
        t, sl, sr = step(2, sl, sr, near, inv_p)
        chain += [t, sl, sr]
        near = exchange(sl, sr)
        size = up(4 * count + 9 * cols + 8, 8 * n_red)
        first = call(
            lambda *refs: moment_kernel(*refs, cols=cols, count=count), shape(size, LANE)
        )(chain[0], cl, gram, *chain[2:8])
        t, sl, sr = step(3, sl, sr, near, schur_p)
        chain += [t, sl, sr]
        first = call(
            lambda *refs: last_moment_kernel(*refs, cols=cols, count=count),
            shape(size, LANE),
            aliases={0: 0},
        )(first, t, sl, sr)
        first = over_all(first, n_red, n_z)

        wide, part = shape(cols, 2 * face), shape(cols, face)
        sl0, sr0, t1, _, _, t2, sl2, sr2, t3, sl3, _ = chain
        sl, sr, w0 = call(
            lambda *refs: coarse_kernel(*refs, cols=cols, count=count), (part, part, wide)
        )(first, coarse_inverse, schur_p, t1, t3, sl3)
        z0, w1c, r1, base, scal, gram, back = call(
            lambda *refs: values_kernel(*refs, cols=cols, count=count),
            (wide, wide, part, shape(4 * cols, rows), shape(cols, LANE), shape(count, count),
             jax.ShapeDtypeStruct((face, face), BF16)),
        )(first, coarse_inverse, nm_row, sl0, sr0, t1, t2, sl2, sr2, sl3, w0)
        near = exchange(sl, sr)
        n0, z1, ul, ur = call(dual_kernel, (wide, part, part, part))(
            sl, sr, *near, mask, z0, scal, inv_p
        )
        near = exchange(ul, ur)
        w1, sl, sr = call(precondition_kernel, (part, part, part))(
            ul, ur, *near, mask, w1c, schur_p
        )
        near = exchange(sl, sr)
        size = up(13 * cols, 8 * n_red)
        second, field, dual = call(
            lambda *refs: combine_kernel(*refs, cols=cols, count=count),
            (shape(size, LANE), shape(4 * cols, rows), shape(3 * cols, face)),
        )(sl, sr, *near, mask, n0, inv_p, scal, z0, z1, ul, ur, r1, w0, w1, base, mass_p, prev_p)
        second = over_all(second, n_red, n_z)
        block, multi, coefficients, factor = call(
            lambda *refs: final_kernel(*refs, cols=cols, count=count),
            (shape(cols, rows), shape(cols, face), shape(cols, count), shape(cols, cols)),
        )(second, gram, scal, field, dual, prev_t, back)
        return block.T[None, None], multi.T[None, None], coefficients.T, factor

    split = (along, ("x", "c"))
    return jax.shard_map(
        on_device,
        mesh=fine,
        in_specs=(
            P(*split, None, None),
            P(*split, None, None),
            P(*split, None, None),
            P(*split, None),
            P(),
            P(*split, None),
            P(*split, None, None),
            P(*split, None, None),
            P(*split, None),
        ),
        out_specs=(P(*split, None, None), P(*split, None, None), P(), P()),
        check_vma=False,
    )
```

```python
import jax
import jax.numpy as jnp
import numpy as np
from jax import lax
from jax.experimental import pallas as pl
from jax.experimental.pallas import tpu as pltpu
from jax.sharding import Mesh, PartitionSpec as P

HI = lax.Precision.HIGHEST
F32 = jnp.float32
BF16 = jnp.bfloat16
RED = ("y", "zl", "x", "c")
LEVELS = 3
LANE = 128


def nn(a, b):
    return jnp.dot(a, b, precision=HI, preferred_element_type=F32)


def nt(a, b):
    return lax.dot_general(
        a, b, (((1,), (1,)), ((), ())), precision=HI, preferred_element_type=F32
    )


def lane_sum(a):
    return jnp.sum(a, axis=1, keepdims=True)


def call(kernel, outs, aliases={}):
    return pl.pallas_call(
        kernel,
        out_shape=outs,
        input_output_aliases=aliases,
        compiler_params=pltpu.CompilerParams(vmem_limit_bytes=12 * 1024 * 1024),
    )


def pieces_of(t, parts, axis):
    pieces = []
    for _ in range(parts - 1):
        pieces.append(t.astype(BF16).astype(F32))
        t = t - pieces[-1]
    return jnp.concatenate(pieces + [t], axis=axis).astype(BF16)


def split_dot(t, mat, parts=2):
    wide = jnp.dot(pieces_of(t, parts, 0), mat, preferred_element_type=F32)
    rows = t.shape[0]
    return sum(wide[i * rows : (i + 1) * rows] for i in range(1, parts)) + wide[:rows]


def split_nt(t, mat):
    rows = t.shape[0]
    wide = lax.dot_general(
        pieces_of(t, 3, 0), mat, (((1,), (1,)), ((), ())), preferred_element_type=F32
    )
    return wide[2 * rows :] + wide[rows : 2 * rows] + wide[:rows]


def split_right(mat, t):
    cols = t.shape[1]
    wide = jnp.dot(mat, pieces_of(t, 3, 1), preferred_element_type=F32)
    return wide[:, 2 * cols :] + wide[:, cols : 2 * cols] + wide[:, :cols]


def to_order(nm_row, face):
    nm = jnp.transpose(jnp.broadcast_to(nm_row.astype(F32), (8, face)))[:, 0:1]
    return (nm == lax.broadcasted_iota(jnp.int32, (face, face), 1).astype(F32)).astype(F32)


def from_order(nm_row, face):
    return (nm_row == lax.broadcasted_iota(jnp.int32, (face, face), 0)).astype(F32)


def start_kernel(inv_hbm, load_hbm, basis_hbm, nm_hbm, corner_hbm, sl_ref, sr_ref, cl_ref,
                 inv_ref, load_ref, basis_ref, nm_ref, corner_ref, sems):
    pairs = (
        (nm_hbm, nm_ref), (load_hbm, load_ref), (basis_hbm, basis_ref), (corner_hbm, corner_ref),
        (inv_hbm, inv_ref),
    )
    copies = [pltpu.make_async_copy(src, dst, sems.at[i]) for i, (src, dst) in enumerate(pairs)]
    for copy in copies:
        copy.start()
    for copy in copies[:-1]:
        copy.wait()
    face = nm_ref.shape[1]
    cols = load_ref.shape[0]
    corners = basis_ref.shape[0]
    rows = cols + corners
    load = load_ref[...]
    basis = basis_ref[...]
    order = to_order(nm_ref[...], face).astype(BF16)
    cl_ref[...] = nt(load, basis)
    for ref in (sl_ref, sr_ref):
        ref[rows : rows + 8, :] = jnp.zeros((8, face), F32)
        ref[rows : rows + 1, 0:corners] = corner_ref[...].astype(F32)
    sr_ref[cols:rows, :] = basis[:, face:]
    copies[-1].wait()
    wide = split_dot(load, inv_ref[...])
    sr_ref[0:cols, :] = wide[:, face:]
    left = [wide[:, :face], basis[:, :face], jnp.zeros((8, face), F32)]
    left = split_dot(jnp.concatenate(left, axis=0), order, 3)
    sl_ref[0:rows, :] = left[0:rows]


def matrix_kernel(src, nm_ref, dst):
    face = nm_ref.shape[1]
    order = to_order(nm_ref[...], face).astype(BF16)
    back = from_order(nm_ref[...], face).astype(BF16)
    dst[:, face:] = src[:, face:]
    dst[:, :face] = jnp.dot(src[:, :face], order, preferred_element_type=F32).astype(BF16)
    dst[:face, :] = jnp.dot(back, dst[:face, :], preferred_element_type=F32).astype(BF16)


def basis_kernel(prev_ref, nm_ref, mass_ref, prev_out, flip_out, mass_out, gram_out, *, total):
    face = nm_ref.shape[1]
    back = from_order(nm_ref[...], face).astype(BF16)
    prev_out[face:, :] = prev_ref[face:, :]
    prev_out[:face, :] = jnp.dot(back, prev_ref[:face, :], preferred_element_type=F32).astype(BF16)
    flip_out[...] = jnp.transpose(prev_out[...].astype(F32)).astype(BF16)
    mass = mass_ref[...] / total
    mass_out[:, face:] = mass[:, face:]
    left = jnp.broadcast_to(mass[:, :face], (8, face))
    mass_out[:, :face] = nn(left, to_order(nm_ref[...], face))[0:1]
    column = jnp.transpose(jnp.broadcast_to(mass, (8, mass.shape[1])))[:, 0:1]
    wide = prev_ref[...].astype(F32)
    gram_out[...] = lax.dot_general(
        wide * column, wide, (((0,), (0,)), ((), ())), precision=HI, preferred_element_type=F32
    )


def step_kernel(sl_ref, sr_ref, nl_ref, pr_ref, mask_ref, mat_ref, t_ref, ol_ref, or_ref,
                *, cols, width, scale):
    face = sl_ref.shape[1]
    new = width + 16
    rows = cols + new
    old = cols + width
    for lanes, own, other, shift in (
        (slice(0, face), sl_ref, pr_ref, 0),
        (slice(face, 2 * face), sr_ref, nl_ref, 16),
    ):
        keep = mask_ref[0:1, lanes]
        t_ref[0:cols, lanes] = (own[0:cols, :] - other[0:cols, :]) * keep
        edge = jnp.zeros((8, face), F32)
        mine = jnp.concatenate([edge, own[cols:old, :], edge], axis=0)
        blank = jnp.zeros((16, face), F32)
        theirs = other[cols:old, :]
        theirs = jnp.concatenate([theirs, blank] if shift == 0 else [blank, theirs], axis=0)
        t_ref[cols:rows, lanes] = (mine - theirs) * keep
    v = split_dot(t_ref[...], mat_ref[...])
    if scale != 1.0:
        v = v * scale
    ids = jnp.concatenate(
        [
            pr_ref[old : old + 8, 0:8],
            sl_ref[old : old + 8, 0:width],
            nl_ref[old : old + 8, width - 8 : width],
        ],
        axis=1,
    )
    for ref, lanes in ((ol_ref, slice(0, face)), (or_ref, slice(face, 2 * face))):
        ref[0:rows, :] = v[:, lanes]
        ref[rows : rows + 8, :] = jnp.zeros((8, face), F32)
        ref[rows : rows + 8, 0:new] = ids


def one_hot(ids, count):
    dof = lax.broadcasted_iota(jnp.int32, (count, ids.shape[1]), 0).astype(F32)
    return (ids == dof).astype(F32).astype(BF16)


def lower(half):
    row = lax.broadcasted_iota(jnp.int32, (half, half), 0)
    col = lax.broadcasted_iota(jnp.int32, (half, half), 1)
    return row, col


def pack(ref, k, matrix, diagonals):
    half = LANE
    at = 2 * half * k
    row, col = lower(half)
    last = matrix[half:, half:]
    ref[at : at + half, :] = jnp.where(row >= col, matrix[:half, :half], last)
    ref[at + half : at + 2 * half, :] = matrix[half:, :half]
    ref[diagonals + k : diagonals + k + 1, :] = jnp.sum(
        jnp.where(row == col, last, 0.0), axis=0, keepdims=True
    )


def unpack(ref, k, diagonals):
    half = LANE
    at = 2 * half * k
    row, col = lower(half)
    shared = ref[at : at + half, :]
    flipped = jnp.transpose(shared)
    cross = ref[at + half : at + 2 * half, :]
    first = jnp.where(row >= col, shared, flipped)
    last = jnp.where(row < col, shared, flipped)
    last = jnp.where(row == col, ref[diagonals + k : diagonals + k + 1, :], last)
    return jnp.concatenate(
        [
            jnp.concatenate([first, jnp.transpose(cross)], axis=1),
            jnp.concatenate([cross, last], axis=1),
        ],
        axis=0,
    )


def level_moments(out, refs, k, cols, count):
    base = 4 * count
    t_ref, l_ref, r_ref = refs
    rows, double = t_ref.shape
    face = double // 2
    width = rows - cols
    spot = one_hot(l_ref[rows : rows + 1, 0:width], count)
    tl, tr = t_ref[cols:rows, :face], t_ref[cols:rows, face:]
    inner = split_nt(nt(l_ref[0:rows, :], tl) + nt(r_ref[0:rows, :], tr), spot)
    put(out, base + 2 * cols * (k + 1), inner[0:cols])
    pack(out, k, split_right(spot, inner[cols:rows]), base + 9 * cols)
    return lane_sum(t_ref[0:cols, :face] * l_ref[0:cols, :]) + lane_sum(
        t_ref[0:cols, face:] * r_ref[0:cols, :]
    )


def put(out, at, block):
    cols, half = block.shape[0], block.shape[1] // 2
    out[at : at + cols, :] = block[:, :half]
    out[at + cols : at + 2 * cols, :] = block[:, half:]


def in_lanes(items, start=0):
    cols = items[0].shape[0]
    lane = lax.broadcasted_iota(jnp.int32, (cols, LANE), 1)
    block = jnp.zeros((cols, LANE), F32)
    for k, item in enumerate(items):
        block = jnp.where(lane == start + k, item, block)
    return block


def moment_kernel(sl0_ref, cl_ref, gram_ref, *refs, cols, count):
    out = refs[-1]
    base = 4 * count
    at = base + 8 * cols
    out[at:, :] = jnp.zeros((out.shape[0] - at, LANE), F32)
    own = sl0_ref.shape[0] - cols - 8
    spot = one_hot(sl0_ref[cols + own : cols + own + 1, 0:own], count)
    put(out, base, split_nt(cl_ref[...], spot))
    sums = [level_moments(out, refs[3 * k : 3 * k + 3], k, cols, count) for k in range(2)]
    pack(out, 3, gram_ref[...], at + cols)
    out[at : at + cols, :] = in_lanes(sums)


def last_moment_kernel(given_ref, *refs, cols, count):
    out = refs[-1]
    total = level_moments(out, refs[:3], 2, cols, count)
    at = 4 * count + 8 * cols
    out[at : at + cols, :] = given_ref[at : at + cols, :] + in_lanes([total], 2)


def vector(sums_ref, k, cols, count):
    at = 4 * count + 2 * cols * k
    return jnp.concatenate([sums_ref[at : at + cols, :], sums_ref[at + cols : at + 2 * cols, :]], axis=1)


def at_corners(values, ids_ref):
    rows = ids_ref.shape[0]
    spot = one_hot(ids_ref[rows - 8 : rows - 7, 0:LANE], values.shape[1])
    return split_dot(values, spot, 3)


def spread(local, k, ref, lanes, cols):
    width = 8 * (2 * k + 1)
    lane = 8 * (LEVELS - k)
    wide = nn(local[:, lane : lane + width], ref[cols : cols + width, lanes])
    return [wide[i : i + cols] for i in range(0, wide.shape[0], cols)]


def coarse_kernel(sums_ref, coarse_ref, mat_ref, t1, t3, sl3, ol_ref, or_ref, w0_ref,
                  *, cols, count):
    diagonals = 4 * count + 9 * cols
    face = ol_ref.shape[1]
    every = slice(0, 2 * face)
    g0 = nn(vector(sums_ref, 0, cols, count), coarse_ref[...])
    g1 = nn(vector(sums_ref, 1, cols, count) + nn(g0, unpack(sums_ref, 0, diagonals)), coarse_ref[...])
    local = at_corners(jnp.concatenate([g0, g1], axis=0), sl3)
    (p30,) = spread(local[0:cols], 3, t3, every, cols)
    (p11,) = spread(local[cols:], 1, t1, every, cols)
    w0 = t3[0:cols, :] + p30 + p11
    w0_ref[...] = w0
    v = split_dot(w0, mat_ref[...]) * 0.25
    ol_ref[...] = v[:, :face]
    or_ref[...] = v[:, face:]


def values_kernel(sums_ref, coarse_ref, nm_ref, sl0, sr0, t1, t2, sl2, sr2, sl3, w0_ref,
                  z0_ref, w1c_ref, r1_ref, field_ref, scal_ref, gram_ref, back_ref,
                  *, cols, count):
    diagonals = 4 * count + 9 * cols
    face = sl0.shape[1]
    m0, m1, m2 = (unpack(sums_ref, k, diagonals) for k in range(3))
    coarse = coarse_ref[...]
    c_load, w0x, w1x, w2x = (vector(sums_ref, k, cols, count) for k in range(4))
    at = 4 * count + 8 * cols
    s0, s1, s2 = (sums_ref[at : at + cols, k : k + 1] for k in range(3))
    g0 = nn(c_load, coarse)
    m0g0, m1g0, m2g0 = nn(g0, m0), nn(g0, m1), nn(g0, m2)
    c0 = w0x + m0g0
    g1 = nn(c0, coarse)
    m0g1, m1g1 = nn(g1, m0), nn(g1, m1)
    rz0 = s0 + lane_sum(2.0 * w0x * g0 + g0 * m0g0)
    del0 = s1 + lane_sum(2.0 * w1x * g0 + g0 * m1g0 + c0 * g1)
    nu0 = s2 + lane_sum(2.0 * w2x * g0 + g0 * m2g0 + 2.0 * w1x * g1 + 2.0 * g1 * m1g0 + g1 * m0g1)
    al0 = rz0 / del0
    be1 = (rz0 - 2.0 * al0 * del0 + al0 * al0 * nu0) / rz0
    cz1 = c0 - al0 * (w1x + m1g0 + m0g1)
    gz1 = nn(cz1, coarse)
    cm = (
        (1.0 + be1) * (w1x + m1g0)
        - al0 * (m1g1 + w2x + m2g0)
        + nn(gz1, m0)
        + be1 * m0g1
    )
    gm = nn(cm, coarse)
    local = at_corners(jnp.concatenate([g0, g1, gz1, gm], axis=0), sl3)
    every, right, whole = slice(0, 2 * face), slice(face, 2 * face), slice(0, face)
    (p20,) = spread(local[0:cols], 2, t2, every, cols)
    (p10,) = spread(local[0:cols], 1, t1, right, cols)
    (w1c_ref[...],) = spread(local[2 * cols : 3 * cols], 1, t1, every, cols)
    z0_ref[...] = t2[0:cols, :] + p20
    r1_ref[...] = t1[0:cols, right] + p10 - al0 * w0_ref[:, right]
    for own, u, lanes in ((sl0, sl2, slice(0, face)), (sr0, sr2, right)):
        corner = spread(local, 0, own, whole, cols)
        (u0,) = spread(local[0:cols], 2, u, whole, cols)
        field_ref[0:cols, lanes] = own[0:cols, :] + corner[0]
        field_ref[cols : 2 * cols, lanes] = u[0:cols, :] + u0 + corner[1]
        field_ref[2 * cols : 3 * cols, lanes] = corner[2]
        field_ref[3 * cols : 4 * cols, lanes] = corner[3]
    scal_ref[...] = in_lanes([al0, be1, lane_sum(cm * gm)])
    gram_ref[...] = unpack(sums_ref, 3, diagonals)
    back_ref[...] = from_order(nm_ref[...], face).astype(BF16)


def joined(own_ref, other_ref, mask_ref, left):
    face = own_ref.shape[1]
    lanes = slice(0, face) if left else slice(face, 2 * face)
    return (own_ref[...] - other_ref[...]) * mask_ref[0:1, lanes]


def field_of(sl_ref, sr_ref, nl_ref, pr_ref, mask_ref):
    return jnp.concatenate(
        [joined(sl_ref, pr_ref, mask_ref, True), joined(sr_ref, nl_ref, mask_ref, False)], axis=1
    )


def dual_kernel(sl_ref, sr_ref, nl_ref, pr_ref, mask_ref, z0_ref, scal_ref, mat_ref,
                n0_ref, z1_ref, ol_ref, or_ref):
    face = sl_ref.shape[1]
    n0 = field_of(sl_ref, sr_ref, nl_ref, pr_ref, mask_ref)
    z1 = z0_ref[...] - scal_ref[:, 0:1] * n0
    n0_ref[...] = n0
    z1_ref[...] = z1[:, face:]
    u = split_dot(z1, mat_ref[...])
    ol_ref[...] = u[:, :face]
    or_ref[...] = u[:, face:]


def precondition_kernel(sl_ref, sr_ref, nl_ref, pr_ref, mask_ref, w1c_ref, mat_ref,
                        w1_ref, ol_ref, or_ref):
    face = sl_ref.shape[1]
    w1 = field_of(sl_ref, sr_ref, nl_ref, pr_ref, mask_ref) + w1c_ref[...]
    w1_ref[...] = w1[:, face:]
    v = split_dot(w1, mat_ref[...]) * 0.25
    ol_ref[...] = v[:, :face]
    or_ref[...] = v[:, face:]


def combine_kernel(sl_ref, sr_ref, nl_ref, pr_ref, mask_ref, n0_ref, mat_ref, scal_ref, z0_ref,
                   z1_ref, ul_ref, ur_ref, r1_ref, w0_ref, w1_ref, base_ref, mass_ref, prev_ref,
                   out_ref, field_ref, dual_ref, *, cols, count):
    half = count // 2
    face = sl_ref.shape[1]
    be1 = scal_ref[:, 1:2]
    whole = field_of(sl_ref, sr_ref, nl_ref, pr_ref, mask_ref) + be1 * n0_ref[...]
    u = split_dot(whole, mat_ref[...])
    field_ref[0 : 2 * cols, :] = base_ref[0 : 2 * cols, :]
    third, fourth = slice(2 * cols, 3 * cols), slice(3 * cols, 4 * cols)
    field_ref[third, 0:face] = base_ref[third, 0:face] + ul_ref[...]
    field_ref[third, face:] = base_ref[third, face:] + ur_ref[...]
    field_ref[fourth, :] = base_ref[fourth, :] + u
    m = whole[:, face:]
    z0, w0 = z0_ref[:, face:], w0_ref[:, face:]
    z1, w1, r1 = z1_ref[...], w1_ref[...], r1_ref[...]
    q1 = w1 + be1 * w0
    p1 = z1 + be1 * z0
    for i, item in enumerate((z0, z1, m)):
        dual_ref[i * cols : (i + 1) * cols, :] = item
    moments = (
        lane_sum(r1 * z1), lane_sum(r1 * m), lane_sum(q1 * z1), lane_sum(q1 * m),
        lane_sum(r1 * p1), lane_sum(p1 * q1), lane_sum(z1 * w1), lane_sum(m * w1),
        lane_sum(whole * u),
    )
    field = field_ref[...]
    scaled = field * mass_ref[...]
    tq = split_dot(scaled, prev_ref[...], 3)
    out_ref[0 : 4 * cols, :] = tq[:, :half]
    out_ref[4 * cols : 8 * cols, :] = tq[:, half:]
    out_ref[8 * cols : 12 * cols, :] = nt(scaled, field)
    out_ref[12 * cols : 13 * cols, :] = in_lanes(moments)
    out_ref[13 * cols :, :] = jnp.zeros((out_ref.shape[0] - 13 * cols, LANE), F32)


def final_kernel(sums_ref, basis_ref, scal_ref, field_ref, dual_ref, prev_ref, back_ref,
                 block_ref, multi_ref, coef_ref, factor_ref, *, cols, count):
    half = count // 2
    face = dual_ref.shape[1]
    at = 12 * cols
    r1z1, r1m, q1z1, q1m, r1p1, p1q1, z1w1, mw1, mm = (
        sums_ref[at : at + cols, k : k + 1] for k in range(9)
    )
    al0, be1, extra = (scal_ref[:, k : k + 1] for k in range(3))
    mfm = mm + extra
    al1 = r1p1 / p1q1
    z2q1 = q1z1 - al1 * q1m
    be2 = -z2q1 / p1q1
    rz2 = r1z1 - al1 * (r1m + q1z1) + al1 * al1 * q1m
    z2fz2 = z1w1 - 2.0 * al1 * mw1 + al1 * al1 * mfm
    al2 = rz2 / (z2fz2 + 2.0 * be2 * z2q1 + be2 * be2 * p1q1)
    along = al1 + al2 * be2
    parts = (al0 + along * be1, along + al2, -al1 * al2)
    multi = sum(y * dual_ref[i * cols : (i + 1) * cols, :] for i, y in enumerate(parts))
    multi_ref[...] = multi
    weights = [jnp.ones((cols, 1), F32)] + [-y for y in parts]
    primal = sum(y * field_ref[i * cols : (i + 1) * cols, :] for i, y in enumerate(weights))
    g1 = sum(
        y
        * jnp.concatenate(
            [sums_ref[i * cols : (i + 1) * cols, :], sums_ref[(4 + i) * cols : (5 + i) * cols, :]],
            axis=1,
        )
        for i, y in enumerate(weights)
    )
    row = lax.broadcasted_iota(jnp.int32, (cols, cols), 0)
    col = lax.broadcasted_iota(jnp.int32, (cols, cols), 1)
    eye = (row == col).astype(F32)
    stacked = jnp.concatenate(weights, axis=0)
    across = jnp.concatenate([jnp.sum(y * eye, axis=0, keepdims=True) for y in weights], axis=1)
    tiles = stacked * sums_ref[8 * cols : 12 * cols, :] * across
    tiles = sum(tiles[i * cols : (i + 1) * cols] for i in range(4))
    gram = sum(tiles[:, j * cols : (j + 1) * cols] for j in range(4))
    basis = basis_ref[...]
    c = 2.0 * g1 - nn(g1, basis)
    coef_ref[...] = c
    gram = gram + nt(c, nn(c, basis) - 2.0 * g1)
    gram = 0.5 * (gram + jnp.transpose(gram))
    final = primal - split_dot(c, prev_ref[...], 3)
    work = jnp.concatenate([gram, eye], axis=1)
    index = lax.broadcasted_iota(jnp.int32, (cols, 1), 0)
    pivots = jnp.zeros(work.shape, F32)
    for start in range(0, cols, 8):
        wide = [jnp.broadcast_to(work[:, start + j : start + j + 1], work.shape) for j in range(8)]
        for j in range(8):
            k = start + j
            pivot = wide[j][k : k + 1, :]
            pivots = jnp.where(index == k, pivot, pivots)
            times = jnp.where(index > k, wide[j], 0.0) * (1.0 / pivot)
            for i in range(j + 1, 8):
                wide[i] = wide[i] - times * wide[i][k : k + 1, :]
            work = work - times * work[k : k + 1, :]
    work = work / jnp.sqrt(pivots)
    factor_ref[...] = jnp.transpose(jnp.where(row <= col, work[:, :cols], 0.0))
    solved = nn(work[:, cols:], final)
    left = split_dot(solved[:, :face], back_ref[...], 3)
    block_ref[:, :face] = left
    block_ref[:, face:] = solved[:, face:]


def sum_kernel(parts_ref, out_ref):
    total = jnp.sum(parts_ref[...], axis=0)
    for i in range(out_ref.shape[0]):
        out_ref[i] = total


def swap(parts, axes):
    return lax.all_to_all(parts, axes, 0, 0, tiled=True)


def summed(parts, copies):
    return call(sum_kernel, jax.ShapeDtypeStruct((copies,) + parts.shape[1:], F32))(parts)


def over_all(rows, n_red, n_z):
    parts = swap(rows.reshape(n_red, rows.shape[0] // n_red, LANE), RED)
    parts = swap(summed(parts, n_z), "zh")
    return swap(summed(parts, n_red), RED).reshape(rows.shape)


def up(count, unit):
    return -(-count // unit) * unit


def solution(mesh):
    n_sub, n_grp = mesh.shape["sub"], mesh.shape["grp"]
    n_y = min(4, n_sub)
    n_zl, n_c = 2, 2
    n_z = n_sub // n_y // n_zl
    n_x = n_grp // n_c
    devices = np.asarray(mesh.devices).reshape(n_y, n_z, n_zl, n_x, n_c)
    fine = Mesh(devices, ("y", "zh", "zl", "x", "c"))
    n_red = n_y * n_zl * n_x * n_c
    along = ("y", "zh", "zl")
    ahead = [(i, i + 1) for i in range(n_sub - 1)]
    behind = [(i + 1, i) for i in range(n_sub - 1)]

    def on_device(schur_inverse, schur, coarse_basis, corner_index, coarse_inverse, neighbor_map,
                  load, previous, mass):
        inverse_block, schur_block, basis = schur_inverse[0, 0], schur[0, 0], coarse_basis[0, 0]
        corners, nm = corner_index[0, 0], neighbor_map[0, 0]
        rhs, earlier, weights = load[0, 0].T, previous[0, 0], mass[0, 0]
        cols, rows = rhs.shape
        face = nm.shape[0]
        count = coarse_inverse.shape[0]
        total = rows * n_sub * n_grp
        own = corners.shape[0]
        position = lax.axis_index(along)
        nm_row = nm[None, :]
        side = jnp.arange(2 * face) < face
        mask = jnp.where(side, position > 0, position < n_sub - 1).astype(F32)[None, :]
        mask = jnp.broadcast_to(mask, (8, 2 * face))

        def shape(*dims):
            return jax.ShapeDtypeStruct(dims, F32)

        half = shape(cols + own + 8, face)
        sl, sr, cl = pl.pallas_call(
            start_kernel,
            out_shape=(half, half, shape(cols, own)),
            in_specs=[pl.BlockSpec(memory_space=pl.ANY)] * 5,
            scratch_shapes=[
                pltpu.VMEM((rows, rows), BF16),
                pltpu.VMEM((cols, rows), F32),
                pltpu.VMEM((own, rows), F32),
                pltpu.VMEM((1, face), jnp.int32),
                pltpu.VMEM((1, own), jnp.int32),
                pltpu.SemaphoreType.DMA((5,)),
            ],
            compiler_params=pltpu.CompilerParams(vmem_limit_bytes=60 * 1024 * 1024),
        )(inverse_block, rhs, basis, nm_row, corners[None, :])
        square = jax.ShapeDtypeStruct((rows, rows), BF16)

        def exchange(sl, sr):
            return lax.ppermute(sl, along, behind), lax.ppermute(sr, along, ahead)

        def step(k, sl, sr, near, mat):
            width = own + 16 * (k - 1)
            out = cols + width + 16
            return call(
                lambda *refs: step_kernel(
                    *refs, cols=cols, width=width, scale=0.25 if k % 2 == 1 else 1.0
                ),
                (shape(out, 2 * face), shape(out + 8, face), shape(out + 8, face)),
            )(sl, sr, *near, mask, mat)

        chain = [sl, sr]
        near = exchange(sl, sr)
        schur_p = call(matrix_kernel, square)(schur_block, nm_row)
        t, sl, sr = step(1, sl, sr, near, schur_p)
        chain += [t, sl, sr]
        near = exchange(sl, sr)
        inv_p = call(matrix_kernel, square)(inverse_block, nm_row)
        prev_p, prev_t, mass_p, gram = call(
            lambda *refs: basis_kernel(*refs, total=total),
            (
                jax.ShapeDtypeStruct(earlier.shape, BF16),
                jax.ShapeDtypeStruct(earlier.shape[::-1], BF16),
                shape(1, rows),
                shape(count, count),
            ),
        )(earlier, nm_row, weights[None, :])
        near, gram = lax.optimization_barrier((near, gram))
        t, sl, sr = step(2, sl, sr, near, inv_p)
        chain += [t, sl, sr]
        near = exchange(sl, sr)
        size = up(4 * count + 9 * cols + 8, 8 * n_red)
        first = call(
            lambda *refs: moment_kernel(*refs, cols=cols, count=count), shape(size, LANE)
        )(chain[0], cl, gram, *chain[2:8])
        t, sl, sr = step(3, sl, sr, near, schur_p)
        chain += [t, sl, sr]
        first = call(
            lambda *refs: last_moment_kernel(*refs, cols=cols, count=count),
            shape(size, LANE),
            aliases={0: 0},
        )(first, t, sl, sr)
        first = over_all(first, n_red, n_z)

        wide, part = shape(cols, 2 * face), shape(cols, face)
        sl0, sr0, t1, _, _, t2, sl2, sr2, t3, sl3, _ = chain
        sl, sr, w0 = call(
            lambda *refs: coarse_kernel(*refs, cols=cols, count=count), (part, part, wide)
        )(first, coarse_inverse, schur_p, t1, t3, sl3)
        z0, w1c, r1, base, scal, gram, back = call(
            lambda *refs: values_kernel(*refs, cols=cols, count=count),
            (wide, wide, part, shape(4 * cols, rows), shape(cols, LANE), shape(count, count),
             jax.ShapeDtypeStruct((face, face), BF16)),
        )(first, coarse_inverse, nm_row, sl0, sr0, t1, t2, sl2, sr2, sl3, w0)
        near = exchange(sl, sr)
        n0, z1, ul, ur = call(dual_kernel, (wide, part, part, part))(
            sl, sr, *near, mask, z0, scal, inv_p
        )
        near = exchange(ul, ur)
        w1, sl, sr = call(precondition_kernel, (part, part, part))(
            ul, ur, *near, mask, w1c, schur_p
        )
        near = exchange(sl, sr)
        size = up(13 * cols, 8 * n_red)
        second, field, dual = call(
            lambda *refs: combine_kernel(*refs, cols=cols, count=count),
            (shape(size, LANE), shape(4 * cols, rows), shape(3 * cols, face)),
        )(sl, sr, *near, mask, n0, inv_p, scal, z0, z1, ul, ur, r1, w0, w1, base, mass_p, prev_p)
        second = over_all(second, n_red, n_z)
        block, multi, coefficients, factor = call(
            lambda *refs: final_kernel(*refs, cols=cols, count=count),
            (shape(cols, rows), shape(cols, face), shape(cols, count), shape(cols, cols)),
        )(second, gram, scal, field, dual, prev_t, back)
        return block.T[None, None], multi.T[None, None], coefficients.T, factor

    split = (along, ("x", "c"))
    return jax.shard_map(
        on_device,
        mesh=fine,
        in_specs=(
            P(*split, None, None),
            P(*split, None, None),
            P(*split, None, None),
            P(*split, None),
            P(),
            P(*split, None),
            P(*split, None, None),
            P(*split, None, None),
            P(*split, None),
        ),
        out_specs=(P(*split, None, None), P(*split, None, None), P(), P()),
        check_vma=False,
    )
```

```python
import jax
import jax.numpy as jnp
import numpy as np
from jax import lax
from jax.experimental import pallas as pl
from jax.experimental.pallas import tpu as pltpu
from jax.sharding import Mesh, PartitionSpec as P

HI = lax.Precision.HIGHEST
F32 = jnp.float32
BF16 = jnp.bfloat16
RED = ("y", "zl", "x", "c")
LEVELS = 3
LANE = 128


def nn(a, b):
    return jnp.dot(a, b, precision=HI, preferred_element_type=F32)


def nt(a, b):
    return lax.dot_general(
        a, b, (((1,), (1,)), ((), ())), precision=HI, preferred_element_type=F32
    )


def lane_sum(a):
    return jnp.sum(a, axis=1, keepdims=True)


def call(kernel, outs):
    return pl.pallas_call(
        kernel,
        out_shape=outs,
        compiler_params=pltpu.CompilerParams(vmem_limit_bytes=12 * 1024 * 1024),
    )


def pieces_of(t, parts, axis):
    pieces = []
    for _ in range(parts - 1):
        pieces.append(t.astype(BF16).astype(F32))
        t = t - pieces[-1]
    return jnp.concatenate(pieces + [t], axis=axis).astype(BF16)


def split_dot(t, mat, parts=2):
    wide = jnp.dot(pieces_of(t, parts, 0), mat, preferred_element_type=F32)
    rows = t.shape[0]
    return sum(wide[i * rows : (i + 1) * rows] for i in range(1, parts)) + wide[:rows]


def split_nt(t, mat):
    rows = t.shape[0]
    wide = lax.dot_general(
        pieces_of(t, 3, 0), mat, (((1,), (1,)), ((), ())), preferred_element_type=F32
    )
    return wide[2 * rows :] + wide[rows : 2 * rows] + wide[:rows]


def split_right(mat, t):
    cols = t.shape[1]
    wide = jnp.dot(mat, pieces_of(t, 3, 1), preferred_element_type=F32)
    return wide[:, 2 * cols :] + wide[:, cols : 2 * cols] + wide[:, :cols]


def to_order(nm_row, face):
    nm = jnp.transpose(jnp.broadcast_to(nm_row.astype(F32), (8, face)))[:, 0:1]
    return (nm == lax.broadcasted_iota(jnp.int32, (face, face), 1).astype(F32)).astype(F32)


def from_order(nm_row, face):
    return (nm_row == lax.broadcasted_iota(jnp.int32, (face, face), 0)).astype(F32)


def start_kernel(inv_hbm, load_hbm, basis_hbm, nm_hbm, corner_hbm, sl_ref, sr_ref, cl_ref,
                 inv_ref, load_ref, basis_ref, nm_ref, corner_ref, sems):
    pairs = (
        (nm_hbm, nm_ref), (load_hbm, load_ref), (basis_hbm, basis_ref), (corner_hbm, corner_ref),
        (inv_hbm, inv_ref),
    )
    copies = [pltpu.make_async_copy(src, dst, sems.at[i]) for i, (src, dst) in enumerate(pairs)]
    for copy in copies:
        copy.start()
    for copy in copies[:-1]:
        copy.wait()
    face = nm_ref.shape[1]
    cols = load_ref.shape[0]
    corners = basis_ref.shape[0]
    rows = cols + corners
    load = load_ref[...]
    basis = basis_ref[...]
    order = to_order(nm_ref[...], face).astype(BF16)
    cl_ref[...] = nt(load, basis)
    for ref in (sl_ref, sr_ref):
        ref[rows : rows + 8, :] = jnp.zeros((8, face), F32)
        ref[rows : rows + 1, 0:corners] = corner_ref[...].astype(F32)
    sr_ref[cols:rows, :] = basis[:, face:]
    copies[-1].wait()
    wide = split_dot(load, inv_ref[...])
    sr_ref[0:cols, :] = wide[:, face:]
    left = [wide[:, :face], basis[:, :face], jnp.zeros((8, face), F32)]
    left = split_dot(jnp.concatenate(left, axis=0), order, 3)
    sl_ref[0:rows, :] = left[0:rows]


def matrix_kernel(src, nm_ref, dst):
    face = nm_ref.shape[1]
    order = to_order(nm_ref[...], face).astype(BF16)
    back = from_order(nm_ref[...], face).astype(BF16)
    dst[:, face:] = src[:, face:]
    dst[:, :face] = jnp.dot(src[:, :face], order, preferred_element_type=F32).astype(BF16)
    dst[:face, :] = jnp.dot(back, dst[:face, :], preferred_element_type=F32).astype(BF16)


def basis_kernel(prev_ref, nm_ref, mass_ref, prev_out, flip_out, mass_out, gram_out, *, total):
    face = nm_ref.shape[1]
    back = from_order(nm_ref[...], face).astype(BF16)
    prev_out[face:, :] = prev_ref[face:, :]
    prev_out[:face, :] = jnp.dot(back, prev_ref[:face, :], preferred_element_type=F32).astype(BF16)
    flip_out[...] = jnp.transpose(prev_out[...].astype(F32)).astype(BF16)
    mass = mass_ref[...] / total
    mass_out[:, face:] = mass[:, face:]
    left = jnp.broadcast_to(mass[:, :face], (8, face))
    mass_out[:, :face] = nn(left, to_order(nm_ref[...], face))[0:1]
    column = jnp.transpose(jnp.broadcast_to(mass, (8, mass.shape[1])))[:, 0:1]
    wide = prev_ref[...].astype(F32)
    gram_out[...] = lax.dot_general(
        wide * column, wide, (((0,), (0,)), ((), ())), precision=HI, preferred_element_type=F32
    )


def step_kernel(sl_ref, sr_ref, nl_ref, pr_ref, mask_ref, mat_ref, t_ref, ol_ref, or_ref,
                *, cols, width, scale):
    face = sl_ref.shape[1]
    new = width + 16
    rows = cols + new
    old = cols + width
    for lanes, own, other, shift in (
        (slice(0, face), sl_ref, pr_ref, 0),
        (slice(face, 2 * face), sr_ref, nl_ref, 16),
    ):
        keep = mask_ref[0:1, lanes]
        t_ref[0:cols, lanes] = (own[0:cols, :] - other[0:cols, :]) * keep
        edge = jnp.zeros((8, face), F32)
        mine = jnp.concatenate([edge, own[cols:old, :], edge], axis=0)
        blank = jnp.zeros((16, face), F32)
        theirs = other[cols:old, :]
        theirs = jnp.concatenate([theirs, blank] if shift == 0 else [blank, theirs], axis=0)
        t_ref[cols:rows, lanes] = (mine - theirs) * keep
    v = split_dot(t_ref[...], mat_ref[...])
    if scale != 1.0:
        v = v * scale
    ids = jnp.concatenate(
        [
            pr_ref[old : old + 8, 0:8],
            sl_ref[old : old + 8, 0:width],
            nl_ref[old : old + 8, width - 8 : width],
        ],
        axis=1,
    )
    for ref, lanes in ((ol_ref, slice(0, face)), (or_ref, slice(face, 2 * face))):
        ref[0:rows, :] = v[:, lanes]
        ref[rows : rows + 8, :] = jnp.zeros((8, face), F32)
        ref[rows : rows + 8, 0:new] = ids


def one_hot(ids, count):
    dof = lax.broadcasted_iota(jnp.int32, (count, ids.shape[1]), 0).astype(F32)
    return (ids == dof).astype(F32).astype(BF16)


def lower(half):
    row = lax.broadcasted_iota(jnp.int32, (half, half), 0)
    col = lax.broadcasted_iota(jnp.int32, (half, half), 1)
    return row, col


def pack(ref, k, matrix, diagonals):
    half = LANE
    at = 2 * half * k
    row, col = lower(half)
    last = matrix[half:, half:]
    ref[at : at + half, :] = jnp.where(row >= col, matrix[:half, :half], last)
    ref[at + half : at + 2 * half, :] = matrix[half:, :half]
    ref[diagonals + k : diagonals + k + 1, :] = jnp.sum(
        jnp.where(row == col, last, 0.0), axis=0, keepdims=True
    )


def unpack(ref, k, diagonals):
    half = LANE
    at = 2 * half * k
    row, col = lower(half)
    shared = ref[at : at + half, :]
    flipped = jnp.transpose(shared)
    cross = ref[at + half : at + 2 * half, :]
    first = jnp.where(row >= col, shared, flipped)
    last = jnp.where(row < col, shared, flipped)
    last = jnp.where(row == col, ref[diagonals + k : diagonals + k + 1, :], last)
    return jnp.concatenate(
        [
            jnp.concatenate([first, jnp.transpose(cross)], axis=1),
            jnp.concatenate([cross, last], axis=1),
        ],
        axis=0,
    )


def level_moments(out, refs, k, cols, count):
    base = 4 * count
    t_ref, l_ref, r_ref = refs
    rows, double = t_ref.shape
    face = double // 2
    width = rows - cols
    spot = one_hot(l_ref[rows : rows + 1, 0:width], count)
    tl, tr = t_ref[cols:rows, :face], t_ref[cols:rows, face:]
    inner = split_nt(nt(l_ref[0:rows, :], tl) + nt(r_ref[0:rows, :], tr), spot)
    put(out, base + 2 * cols * (k + 1), inner[0:cols])
    pack(out, k, split_right(spot, inner[cols:rows]), base + 9 * cols)
    return lane_sum(t_ref[0:cols, :face] * l_ref[0:cols, :]) + lane_sum(
        t_ref[0:cols, face:] * r_ref[0:cols, :]
    )


def put(out, at, block):
    cols, half = block.shape[0], block.shape[1] // 2
    out[at : at + cols, :] = block[:, :half]
    out[at + cols : at + 2 * cols, :] = block[:, half:]


def in_lanes(items, start=0):
    cols = items[0].shape[0]
    lane = lax.broadcasted_iota(jnp.int32, (cols, LANE), 1)
    block = jnp.zeros((cols, LANE), F32)
    for k, item in enumerate(items):
        block = jnp.where(lane == start + k, item, block)
    return block


def moment_kernel(sl0_ref, cl_ref, gram_ref, *refs, cols, count):
    out = refs[-1]
    base = 4 * count
    at = base + 8 * cols
    out[at:, :] = jnp.zeros((out.shape[0] - at, LANE), F32)
    own = sl0_ref.shape[0] - cols - 8
    spot = one_hot(sl0_ref[cols + own : cols + own + 1, 0:own], count)
    put(out, base, split_nt(cl_ref[...], spot))
    sums = [level_moments(out, refs[3 * k : 3 * k + 3], k, cols, count) for k in range(2)]
    pack(out, 3, gram_ref[...], at + cols)
    out[at : at + cols, :] = in_lanes(sums)


def last_moment_kernel(given_ref, *refs, cols, count):
    out = refs[-1]
    out[...] = given_ref[...]
    total = level_moments(out, refs[:3], 2, cols, count)
    at = 4 * count + 8 * cols
    out[at : at + cols, :] = given_ref[at : at + cols, :] + in_lanes([total], 2)


def vector(sums_ref, k, cols, count):
    at = 4 * count + 2 * cols * k
    return jnp.concatenate([sums_ref[at : at + cols, :], sums_ref[at + cols : at + 2 * cols, :]], axis=1)


def at_corners(values, ids_ref):
    rows = ids_ref.shape[0]
    spot = one_hot(ids_ref[rows - 8 : rows - 7, 0:LANE], values.shape[1])
    return split_dot(values, spot, 3)


def spread(local, k, ref, lanes, cols):
    width = 8 * (2 * k + 1)
    lane = 8 * (LEVELS - k)
    wide = nn(local[:, lane : lane + width], ref[cols : cols + width, lanes])
    return [wide[i : i + cols] for i in range(0, wide.shape[0], cols)]


def coarse_kernel(sums_ref, coarse_ref, mat_ref, t1, t3, sl3, ol_ref, or_ref, w0_ref,
                  *, cols, count):
    diagonals = 4 * count + 9 * cols
    face = ol_ref.shape[1]
    every = slice(0, 2 * face)
    g0 = nn(vector(sums_ref, 0, cols, count), coarse_ref[...])
    g1 = nn(vector(sums_ref, 1, cols, count) + nn(g0, unpack(sums_ref, 0, diagonals)), coarse_ref[...])
    local = at_corners(jnp.concatenate([g0, g1], axis=0), sl3)
    (p30,) = spread(local[0:cols], 3, t3, every, cols)
    (p11,) = spread(local[cols:], 1, t1, every, cols)
    w0 = t3[0:cols, :] + p30 + p11
    w0_ref[...] = w0
    v = split_dot(w0, mat_ref[...]) * 0.25
    ol_ref[...] = v[:, :face]
    or_ref[...] = v[:, face:]


def values_kernel(sums_ref, coarse_ref, nm_ref, sl0, sr0, t1, t2, sl2, sr2, sl3, w0_ref,
                  z0_ref, w1c_ref, r1_ref, field_ref, scal_ref, gram_ref, back_ref,
                  *, cols, count):
    diagonals = 4 * count + 9 * cols
    face = sl0.shape[1]
    m0, m1, m2 = (unpack(sums_ref, k, diagonals) for k in range(3))
    coarse = coarse_ref[...]
    c_load, w0x, w1x, w2x = (vector(sums_ref, k, cols, count) for k in range(4))
    at = 4 * count + 8 * cols
    s0, s1, s2 = (sums_ref[at : at + cols, k : k + 1] for k in range(3))
    g0 = nn(c_load, coarse)
    m0g0, m1g0, m2g0 = nn(g0, m0), nn(g0, m1), nn(g0, m2)
    c0 = w0x + m0g0
    g1 = nn(c0, coarse)
    m0g1, m1g1 = nn(g1, m0), nn(g1, m1)
    rz0 = s0 + lane_sum(2.0 * w0x * g0 + g0 * m0g0)
    del0 = s1 + lane_sum(2.0 * w1x * g0 + g0 * m1g0 + c0 * g1)
    nu0 = s2 + lane_sum(2.0 * w2x * g0 + g0 * m2g0 + 2.0 * w1x * g1 + 2.0 * g1 * m1g0 + g1 * m0g1)
    al0 = rz0 / del0
    be1 = (rz0 - 2.0 * al0 * del0 + al0 * al0 * nu0) / rz0
    cz1 = c0 - al0 * (w1x + m1g0 + m0g1)
    gz1 = nn(cz1, coarse)
    cm = (
        (1.0 + be1) * (w1x + m1g0)
        - al0 * (m1g1 + w2x + m2g0)
        + nn(gz1, m0)
        + be1 * m0g1
    )
    gm = nn(cm, coarse)
    local = at_corners(jnp.concatenate([g0, g1, gz1, gm], axis=0), sl3)
    every, right, whole = slice(0, 2 * face), slice(face, 2 * face), slice(0, face)
    (p20,) = spread(local[0:cols], 2, t2, every, cols)
    (p10,) = spread(local[0:cols], 1, t1, right, cols)
    (w1c_ref[...],) = spread(local[2 * cols : 3 * cols], 1, t1, every, cols)
    z0_ref[...] = t2[0:cols, :] + p20
    r1_ref[...] = t1[0:cols, right] + p10 - al0 * w0_ref[:, right]
    for own, u, lanes in ((sl0, sl2, slice(0, face)), (sr0, sr2, right)):
        corner = spread(local, 0, own, whole, cols)
        (u0,) = spread(local[0:cols], 2, u, whole, cols)
        field_ref[0:cols, lanes] = own[0:cols, :] + corner[0]
        field_ref[cols : 2 * cols, lanes] = u[0:cols, :] + u0 + corner[1]
        field_ref[2 * cols : 3 * cols, lanes] = corner[2]
        field_ref[3 * cols : 4 * cols, lanes] = corner[3]
    scal_ref[...] = in_lanes([al0, be1, lane_sum(cm * gm)])
    gram_ref[...] = unpack(sums_ref, 3, diagonals)
    back_ref[...] = from_order(nm_ref[...], face).astype(BF16)


def joined(own_ref, other_ref, mask_ref, left):
    face = own_ref.shape[1]
    lanes = slice(0, face) if left else slice(face, 2 * face)
    return (own_ref[...] - other_ref[...]) * mask_ref[0:1, lanes]


def field_of(sl_ref, sr_ref, nl_ref, pr_ref, mask_ref):
    return jnp.concatenate(
        [joined(sl_ref, pr_ref, mask_ref, True), joined(sr_ref, nl_ref, mask_ref, False)], axis=1
    )


def dual_kernel(sl_ref, sr_ref, nl_ref, pr_ref, mask_ref, z0_ref, scal_ref, mat_ref,
                n0_ref, z1_ref, ol_ref, or_ref):
    face = sl_ref.shape[1]
    n0 = field_of(sl_ref, sr_ref, nl_ref, pr_ref, mask_ref)
    z1 = z0_ref[...] - scal_ref[:, 0:1] * n0
    n0_ref[...] = n0
    z1_ref[...] = z1[:, face:]
    u = split_dot(z1, mat_ref[...])
    ol_ref[...] = u[:, :face]
    or_ref[...] = u[:, face:]


def precondition_kernel(sl_ref, sr_ref, nl_ref, pr_ref, mask_ref, w1c_ref, mat_ref,
                        w1_ref, ol_ref, or_ref):
    face = sl_ref.shape[1]
    w1 = field_of(sl_ref, sr_ref, nl_ref, pr_ref, mask_ref) + w1c_ref[...]
    w1_ref[...] = w1[:, face:]
    v = split_dot(w1, mat_ref[...]) * 0.25
    ol_ref[...] = v[:, :face]
    or_ref[...] = v[:, face:]


def early_kernel(scal_ref, z0_ref, z1_ref, ul_ref, ur_ref, r1_ref, w0_ref, w1_ref, base_ref,
                 mass_ref, prev_ref, out_ref, field_ref, *, cols, count):
    half = count // 2
    face = ul_ref.shape[1]
    third = slice(2 * cols, 3 * cols)
    field_ref[0 : 2 * cols, :] = base_ref[0 : 2 * cols, :]
    field_ref[third, 0:face] = base_ref[third, 0:face] + ul_ref[...]
    field_ref[third, face:] = base_ref[third, face:] + ur_ref[...]
    field_ref[3 * cols :, :] = base_ref[3 * cols :, :]
    be1 = scal_ref[:, 1:2]
    z0, w0 = z0_ref[:, face:], w0_ref[:, face:]
    z1, w1, r1 = z1_ref[...], w1_ref[...], r1_ref[...]
    q1 = w1 + be1 * w0
    out_ref[...] = jnp.zeros(out_ref.shape, F32)
    out_ref[12 * cols : 13 * cols, :] = in_lanes([
        lane_sum(r1 * z1), lane_sum(q1 * z1), lane_sum(r1 * (z1 + be1 * z0)),
        lane_sum((z1 + be1 * z0) * q1), lane_sum(z1 * w1),
    ])
    known = field_ref[0 : 3 * cols, :]
    scaled = known * mass_ref[...]
    tq = split_dot(scaled, prev_ref[...], 3)
    out_ref[0 : 3 * cols, :] = tq[:, :half]
    out_ref[4 * cols : 7 * cols, :] = tq[:, half:]
    out_ref[8 * cols : 11 * cols, 0 : 3 * cols] = nt(scaled, known)


def combine_kernel(given_ref, known_ref, sl_ref, sr_ref, nl_ref, pr_ref, mask_ref, n0_ref, mat_ref,
                   scal_ref, r1_ref, w0_ref, w1_ref, mass_ref, prev_ref,
                   out_ref, field_ref, m_ref, *, cols, count):
    half = count // 2
    face = sl_ref.shape[1]
    be1 = scal_ref[:, 1:2]
    out_ref[...] = given_ref[...]
    field_ref[0 : 3 * cols, :] = known_ref[0 : 3 * cols, :]
    whole = field_of(sl_ref, sr_ref, nl_ref, pr_ref, mask_ref) + be1 * n0_ref[...]
    u = split_dot(whole, mat_ref[...])
    last = known_ref[3 * cols :, :] + u
    field_ref[3 * cols :, :] = last
    m = whole[:, face:]
    m_ref[...] = m
    w0, w1 = w0_ref[:, face:], w1_ref[...]
    scaled = last * mass_ref[...]
    tq = split_dot(scaled, prev_ref[...], 3)
    out_ref[3 * cols : 4 * cols, :] = tq[:, :half]
    out_ref[7 * cols : 8 * cols, :] = tq[:, half:]
    out_ref[11 * cols : 12 * cols, :] = nt(scaled, field_ref[...])
    at = 12 * cols
    out_ref[at : at + cols, :] = given_ref[at : at + cols, :] + in_lanes([
        lane_sum(r1_ref[...] * m), lane_sum((w1 + be1 * w0) * m), lane_sum(m * w1),
        lane_sum(whole * u),
    ], 5)


def final_kernel(sums_ref, basis_ref, scal_ref, field_ref, z0_ref, z1_ref, m_ref, prev_ref, back_ref,
                 block_ref, multi_ref, coef_ref, factor_ref, *, cols, count):
    half = count // 2
    face = m_ref.shape[1]
    at = 12 * cols
    r1z1, q1z1, r1p1, p1q1, z1w1, r1m, q1m, mw1, mm = (
        sums_ref[at : at + cols, k : k + 1] for k in range(9)
    )
    al0, be1, extra = (scal_ref[:, k : k + 1] for k in range(3))
    mfm = mm + extra
    al1 = r1p1 / p1q1
    z2q1 = q1z1 - al1 * q1m
    be2 = -z2q1 / p1q1
    rz2 = r1z1 - al1 * (r1m + q1z1) + al1 * al1 * q1m
    z2fz2 = z1w1 - 2.0 * al1 * mw1 + al1 * al1 * mfm
    al2 = rz2 / (z2fz2 + 2.0 * be2 * z2q1 + be2 * be2 * p1q1)
    along = al1 + al2 * be2
    parts = (al0 + along * be1, along + al2, -al1 * al2)
    duals = (z0_ref[:, face:], z1_ref[...], m_ref[...])
    multi_ref[...] = sum(y * dual for y, dual in zip(parts, duals))
    weights = [jnp.ones((cols, 1), F32)] + [-y for y in parts]
    primal = sum(y * field_ref[i * cols : (i + 1) * cols, :] for i, y in enumerate(weights))
    g1 = sum(
        y
        * jnp.concatenate(
            [sums_ref[i * cols : (i + 1) * cols, :], sums_ref[(4 + i) * cols : (5 + i) * cols, :]],
            axis=1,
        )
        for i, y in enumerate(weights)
    )
    row = lax.broadcasted_iota(jnp.int32, (cols, cols), 0)
    col = lax.broadcasted_iota(jnp.int32, (cols, cols), 1)
    eye = (row == col).astype(F32)
    stacked = jnp.concatenate(weights, axis=0)
    across = jnp.concatenate([jnp.sum(y * eye, axis=0, keepdims=True) for y in weights], axis=1)
    tiles = stacked * sums_ref[8 * cols : 12 * cols, :] * across
    cross = tiles[3 * cols :]
    cross = sum(cross[:, j * cols : (j + 1) * cols] for j in range(3))
    tiles = sum(tiles[i * cols : (i + 1) * cols] for i in range(4))
    gram = sum(tiles[:, j * cols : (j + 1) * cols] for j in range(4))
    gram = gram + jnp.transpose(cross)
    basis = basis_ref[...]
    c = 2.0 * g1 - nn(g1, basis)
    coef_ref[...] = c
    gram = gram + nt(c, nn(c, basis) - 2.0 * g1)
    gram = 0.5 * (gram + jnp.transpose(gram))
    final = primal - split_dot(c, prev_ref[...], 3)
    work = jnp.concatenate([gram, eye], axis=1)
    index = lax.broadcasted_iota(jnp.int32, (cols, 1), 0)
    pivots = jnp.zeros(work.shape, F32)
    for start in range(0, cols, 8):
        wide = [jnp.broadcast_to(work[:, start + j : start + j + 1], work.shape) for j in range(8)]
        for j in range(8):
            k = start + j
            pivot = wide[j][k : k + 1, :]
            pivots = jnp.where(index == k, pivot, pivots)
            times = jnp.where(index > k, wide[j], 0.0) * (1.0 / pivot)
            for i in range(j + 1, 8):
                wide[i] = wide[i] - times * wide[i][k : k + 1, :]
            work = work - times * work[k : k + 1, :]
    work = work / jnp.sqrt(pivots)
    factor_ref[...] = jnp.transpose(jnp.where(row <= col, work[:, :cols], 0.0))
    solved = nn(work[:, cols:], final)
    left = split_dot(solved[:, :face], back_ref[...], 3)
    block_ref[:, :face] = left
    block_ref[:, face:] = solved[:, face:]


def sum_kernel(parts_ref, out_ref):
    total = jnp.sum(parts_ref[...], axis=0)
    for i in range(out_ref.shape[0]):
        out_ref[i] = total


def swap(parts, axes):
    return lax.all_to_all(parts, axes, 0, 0, tiled=True)


def summed(parts, copies):
    return call(sum_kernel, jax.ShapeDtypeStruct((copies,) + parts.shape[1:], F32))(parts)


def over_all(rows, n_red, n_z):
    parts = swap(rows.reshape(n_red, rows.shape[0] // n_red, LANE), RED)
    parts = swap(summed(parts, n_z), "zh")
    return swap(summed(parts, n_red), RED).reshape(rows.shape)


def up(count, unit):
    return -(-count // unit) * unit


def solution(mesh):
    n_sub, n_grp = mesh.shape["sub"], mesh.shape["grp"]
    n_y = min(4, n_sub)
    n_zl, n_c = 2, 2
    n_z = n_sub // n_y // n_zl
    n_x = n_grp // n_c
    devices = np.asarray(mesh.devices).reshape(n_y, n_z, n_zl, n_x, n_c)
    fine = Mesh(devices, ("y", "zh", "zl", "x", "c"))
    n_red = n_y * n_zl * n_x * n_c
    along = ("y", "zh", "zl")
    ahead = [(i, i + 1) for i in range(n_sub - 1)]
    behind = [(i + 1, i) for i in range(n_sub - 1)]

    def on_device(schur_inverse, schur, coarse_basis, corner_index, coarse_inverse, neighbor_map,
                  load, previous, mass):
        inverse_block, schur_block, basis = schur_inverse[0, 0], schur[0, 0], coarse_basis[0, 0]
        corners, nm = corner_index[0, 0], neighbor_map[0, 0]
        rhs, earlier, weights = load[0, 0].T, previous[0, 0], mass[0, 0]
        cols, rows = rhs.shape
        face = nm.shape[0]
        count = coarse_inverse.shape[0]
        total = rows * n_sub * n_grp
        own = corners.shape[0]
        position = lax.axis_index(along)
        nm_row = nm[None, :]
        side = jnp.arange(2 * face) < face
        mask = jnp.where(side, position > 0, position < n_sub - 1).astype(F32)[None, :]
        mask = jnp.broadcast_to(mask, (8, 2 * face))

        def shape(*dims):
            return jax.ShapeDtypeStruct(dims, F32)

        half = shape(cols + own + 8, face)
        sl, sr, cl = pl.pallas_call(
            start_kernel,
            out_shape=(half, half, shape(cols, own)),
            in_specs=[pl.BlockSpec(memory_space=pl.ANY)] * 5,
            scratch_shapes=[
                pltpu.VMEM((rows, rows), BF16),
                pltpu.VMEM((cols, rows), F32),
                pltpu.VMEM((own, rows), F32),
                pltpu.VMEM((1, face), jnp.int32),
                pltpu.VMEM((1, own), jnp.int32),
                pltpu.SemaphoreType.DMA((5,)),
            ],
            compiler_params=pltpu.CompilerParams(vmem_limit_bytes=60 * 1024 * 1024),
        )(inverse_block, rhs, basis, nm_row, corners[None, :])
        square = jax.ShapeDtypeStruct((rows, rows), BF16)

        def exchange(sl, sr):
            return lax.ppermute(sl, along, behind), lax.ppermute(sr, along, ahead)

        def step(k, sl, sr, near, mat):
            width = own + 16 * (k - 1)
            out = cols + width + 16
            return call(
                lambda *refs: step_kernel(
                    *refs, cols=cols, width=width, scale=0.25 if k % 2 == 1 else 1.0
                ),
                (shape(out, 2 * face), shape(out + 8, face), shape(out + 8, face)),
            )(sl, sr, *near, mask, mat)

        chain = [sl, sr]
        near = exchange(sl, sr)
        schur_p = call(matrix_kernel, square)(schur_block, nm_row)
        t, sl, sr = step(1, sl, sr, near, schur_p)
        chain += [t, sl, sr]
        near = exchange(sl, sr)
        inv_p = call(matrix_kernel, square)(inverse_block, nm_row)
        prev_p, prev_t, mass_p, gram = call(
            lambda *refs: basis_kernel(*refs, total=total),
            (
                jax.ShapeDtypeStruct(earlier.shape, BF16),
                jax.ShapeDtypeStruct(earlier.shape[::-1], BF16),
                shape(1, rows),
                shape(count, count),
            ),
        )(earlier, nm_row, weights[None, :])
        near, gram = lax.optimization_barrier((near, gram))
        t, sl, sr = step(2, sl, sr, near, inv_p)
        chain += [t, sl, sr]
        near = exchange(sl, sr)
        size = up(4 * count + 9 * cols + 8, 8 * n_red)
        first = call(
            lambda *refs: moment_kernel(*refs, cols=cols, count=count), shape(size, LANE)
        )(chain[0], cl, gram, *chain[2:8])
        t, sl, sr = step(3, sl, sr, near, schur_p)
        chain += [t, sl, sr]
        first = call(
            lambda *refs: last_moment_kernel(*refs, cols=cols, count=count),
            shape(size, LANE),
        )(first, t, sl, sr)
        first = over_all(first, n_red, n_z)

        wide, part = shape(cols, 2 * face), shape(cols, face)
        sl0, sr0, t1, _, _, t2, sl2, sr2, t3, sl3, _ = chain
        sl, sr, w0 = call(
            lambda *refs: coarse_kernel(*refs, cols=cols, count=count), (part, part, wide)
        )(first, coarse_inverse, schur_p, t1, t3, sl3)
        z0, w1c, r1, base, scal, gram, back = call(
            lambda *refs: values_kernel(*refs, cols=cols, count=count),
            (wide, wide, part, shape(4 * cols, rows), shape(cols, LANE), shape(count, count),
             jax.ShapeDtypeStruct((face, face), BF16)),
        )(first, coarse_inverse, nm_row, sl0, sr0, t1, t2, sl2, sr2, sl3, w0)
        near = exchange(sl, sr)
        n0, z1, ul, ur = call(dual_kernel, (wide, part, part, part))(
            sl, sr, *near, mask, z0, scal, inv_p
        )
        near = exchange(ul, ur)
        w1, sl, sr = call(precondition_kernel, (part, part, part))(
            ul, ur, *near, mask, w1c, schur_p
        )
        near = exchange(sl, sr)
        size = up(13 * cols, 8 * n_red)
        second, field = call(
            lambda *refs: early_kernel(*refs, cols=cols, count=count),
            (shape(size, LANE), shape(4 * cols, rows)),
        )(scal, z0, z1, ul, ur, r1, w0, w1, base, mass_p, prev_p)
        second, field, m = call(
            lambda *refs: combine_kernel(*refs, cols=cols, count=count),
            (shape(size, LANE), shape(4 * cols, rows), part),
        )(second, field, sl, sr, *near, mask, n0, inv_p, scal, r1, w0, w1, mass_p, prev_p)
        second = over_all(second, n_red, n_z)
        block, multi, coefficients, factor = call(
            lambda *refs: final_kernel(*refs, cols=cols, count=count),
            (shape(cols, rows), shape(cols, face), shape(cols, count), shape(cols, cols)),
        )(second, gram, scal, field, z0, z1, m, prev_t, back)
        return block.T[None, None], multi.T[None, None], coefficients.T, factor

    split = (along, ("x", "c"))
    return jax.shard_map(
        on_device,
        mesh=fine,
        in_specs=(
            P(*split, None, None),
            P(*split, None, None),
            P(*split, None, None),
            P(*split, None),
            P(),
            P(*split, None),
            P(*split, None, None),
            P(*split, None, None),
            P(*split, None),
        ),
        out_specs=(P(*split, None, None), P(*split, None, None), P(), P()),
        check_vma=False,
    )
```

```python
import jax
import jax.numpy as jnp
import numpy as np
from jax import lax
from jax.experimental import pallas as pl
from jax.experimental.pallas import tpu as pltpu
from jax.sharding import Mesh, PartitionSpec as P

HI = lax.Precision.HIGHEST
F32 = jnp.float32
BF16 = jnp.bfloat16
RED = ("y", "zl", "x", "c")
LEVELS = 3
LANE = 128


def nn(a, b):
    return jnp.dot(a, b, precision=HI, preferred_element_type=F32)


def nt(a, b):
    return lax.dot_general(
        a, b, (((1,), (1,)), ((), ())), precision=HI, preferred_element_type=F32
    )


def lane_sum(a):
    return jnp.sum(a, axis=1, keepdims=True)


def call(kernel, outs):
    return pl.pallas_call(
        kernel,
        out_shape=outs,
        compiler_params=pltpu.CompilerParams(vmem_limit_bytes=12 * 1024 * 1024),
    )


def pieces_of(t, parts, axis):
    pieces = []
    for _ in range(parts - 1):
        pieces.append(t.astype(BF16).astype(F32))
        t = t - pieces[-1]
    return jnp.concatenate(pieces + [t], axis=axis).astype(BF16)


def split_dot(t, mat, parts=2):
    wide = jnp.dot(pieces_of(t, parts, 0), mat, preferred_element_type=F32)
    rows = t.shape[0]
    return sum(wide[i * rows : (i + 1) * rows] for i in range(1, parts)) + wide[:rows]


def split_nt(t, mat):
    rows = t.shape[0]
    wide = lax.dot_general(
        pieces_of(t, 3, 0), mat, (((1,), (1,)), ((), ())), preferred_element_type=F32
    )
    return wide[2 * rows :] + wide[rows : 2 * rows] + wide[:rows]


def split_right(mat, t):
    cols = t.shape[1]
    wide = jnp.dot(mat, pieces_of(t, 3, 1), preferred_element_type=F32)
    return wide[:, 2 * cols :] + wide[:, cols : 2 * cols] + wide[:, :cols]


def to_order(nm_row, face):
    nm = jnp.transpose(jnp.broadcast_to(nm_row.astype(F32), (8, face)))[:, 0:1]
    return (nm == lax.broadcasted_iota(jnp.int32, (face, face), 1).astype(F32)).astype(F32)


def from_order(nm_row, face):
    return (nm_row == lax.broadcasted_iota(jnp.int32, (face, face), 0)).astype(F32)


def start_kernel(inv_hbm, load_hbm, basis_hbm, nm_hbm, corner_hbm, sl_ref, sr_ref, cl_ref,
                 inv_ref, load_ref, basis_ref, nm_ref, corner_ref, sems):
    pairs = (
        (nm_hbm, nm_ref), (load_hbm, load_ref), (basis_hbm, basis_ref), (corner_hbm, corner_ref),
        (inv_hbm, inv_ref),
    )
    copies = [pltpu.make_async_copy(src, dst, sems.at[i]) for i, (src, dst) in enumerate(pairs)]
    for copy in copies:
        copy.start()
    for copy in copies[:-1]:
        copy.wait()
    face = nm_ref.shape[1]
    cols = load_ref.shape[0]
    corners = basis_ref.shape[0]
    rows = cols + corners
    load = load_ref[...]
    basis = basis_ref[...]
    order = to_order(nm_ref[...], face).astype(BF16)
    cl_ref[...] = nt(load, basis)
    for ref in (sl_ref, sr_ref):
        ref[rows : rows + 8, :] = jnp.zeros((8, face), F32)
        ref[rows : rows + 1, 0:corners] = corner_ref[...].astype(F32)
    sr_ref[cols:rows, :] = basis[:, face:]
    copies[-1].wait()
    wide = split_dot(load, inv_ref[...])
    sr_ref[0:cols, :] = wide[:, face:]
    left = [wide[:, :face], basis[:, :face], jnp.zeros((8, face), F32)]
    left = split_dot(jnp.concatenate(left, axis=0), order, 3)
    sl_ref[0:rows, :] = left[0:rows]


def matrix_kernel(src, nm_ref, dst):
    face = nm_ref.shape[1]
    order = to_order(nm_ref[...], face).astype(BF16)
    back = from_order(nm_ref[...], face).astype(BF16)
    dst[:, face:] = src[:, face:]
    dst[:, :face] = jnp.dot(src[:, :face], order, preferred_element_type=F32).astype(BF16)
    dst[:face, :] = jnp.dot(back, dst[:face, :], preferred_element_type=F32).astype(BF16)


def basis_kernel(prev_ref, nm_ref, mass_ref, prev_out, flip_out, mass_out, gram_out, *, total):
    face = nm_ref.shape[1]
    back = from_order(nm_ref[...], face).astype(BF16)
    prev_out[face:, :] = prev_ref[face:, :]
    prev_out[:face, :] = jnp.dot(back, prev_ref[:face, :], preferred_element_type=F32).astype(BF16)
    flip_out[...] = jnp.transpose(prev_out[...].astype(F32)).astype(BF16)
    mass = mass_ref[...] / total
    mass_out[:, face:] = mass[:, face:]
    left = jnp.broadcast_to(mass[:, :face], (8, face))
    mass_out[:, :face] = nn(left, to_order(nm_ref[...], face))[0:1]
    column = jnp.transpose(jnp.broadcast_to(mass, (8, mass.shape[1])))[:, 0:1]
    wide = prev_ref[...].astype(F32)
    gram_out[...] = lax.dot_general(
        wide * column, wide, (((0,), (0,)), ((), ())), precision=HI, preferred_element_type=F32
    )


def step_kernel(sl_ref, sr_ref, nl_ref, pr_ref, mask_ref, mat_ref, t_ref, ol_ref, or_ref,
                *, cols, width, scale):
    face = sl_ref.shape[1]
    new = width + 16
    rows = cols + new
    old = cols + width
    for lanes, own, other, shift in (
        (slice(0, face), sl_ref, pr_ref, 0),
        (slice(face, 2 * face), sr_ref, nl_ref, 16),
    ):
        keep = mask_ref[0:1, lanes]
        t_ref[0:cols, lanes] = (own[0:cols, :] - other[0:cols, :]) * keep
        edge = jnp.zeros((8, face), F32)
        mine = jnp.concatenate([edge, own[cols:old, :], edge], axis=0)
        blank = jnp.zeros((16, face), F32)
        theirs = other[cols:old, :]
        theirs = jnp.concatenate([theirs, blank] if shift == 0 else [blank, theirs], axis=0)
        t_ref[cols:rows, lanes] = (mine - theirs) * keep
    v = split_dot(t_ref[...], mat_ref[...])
    if scale != 1.0:
        v = v * scale
    ids = jnp.concatenate(
        [
            pr_ref[old : old + 8, 0:8],
            sl_ref[old : old + 8, 0:width],
            nl_ref[old : old + 8, width - 8 : width],
        ],
        axis=1,
    )
    for ref, lanes in ((ol_ref, slice(0, face)), (or_ref, slice(face, 2 * face))):
        ref[0:rows, :] = v[:, lanes]
        ref[rows : rows + 8, :] = jnp.zeros((8, face), F32)
        ref[rows : rows + 8, 0:new] = ids


def one_hot(ids, count):
    dof = lax.broadcasted_iota(jnp.int32, (count, ids.shape[1]), 0).astype(F32)
    return (ids == dof).astype(F32).astype(BF16)


def lower(half):
    row = lax.broadcasted_iota(jnp.int32, (half, half), 0)
    col = lax.broadcasted_iota(jnp.int32, (half, half), 1)
    return row, col


def pack(ref, k, matrix, diagonals):
    half = LANE
    at = 2 * half * k
    row, col = lower(half)
    last = matrix[half:, half:]
    ref[at : at + half, :] = jnp.where(row >= col, matrix[:half, :half], last)
    ref[at + half : at + 2 * half, :] = matrix[half:, :half]
    ref[diagonals + k : diagonals + k + 1, :] = jnp.sum(
        jnp.where(row == col, last, 0.0), axis=0, keepdims=True
    )


def unpack(ref, k, diagonals):
    half = LANE
    at = 2 * half * k
    row, col = lower(half)
    shared = ref[at : at + half, :]
    flipped = jnp.transpose(shared)
    cross = ref[at + half : at + 2 * half, :]
    first = jnp.where(row >= col, shared, flipped)
    last = jnp.where(row < col, shared, flipped)
    last = jnp.where(row == col, ref[diagonals + k : diagonals + k + 1, :], last)
    return jnp.concatenate(
        [
            jnp.concatenate([first, jnp.transpose(cross)], axis=1),
            jnp.concatenate([cross, last], axis=1),
        ],
        axis=0,
    )


def level_moments(out, refs, k, cols, count):
    base = 4 * count
    t_ref, l_ref, r_ref = refs
    rows, double = t_ref.shape
    face = double // 2
    width = rows - cols
    spot = one_hot(l_ref[rows : rows + 1, 0:width], count)
    tl, tr = t_ref[cols:rows, :face], t_ref[cols:rows, face:]
    inner = split_nt(nt(l_ref[0:rows, :], tl) + nt(r_ref[0:rows, :], tr), spot)
    put(out, base + 2 * cols * (k + 1), inner[0:cols])
    pack(out, k, split_right(spot, inner[cols:rows]), base + 9 * cols)
    return lane_sum(t_ref[0:cols, :face] * l_ref[0:cols, :]) + lane_sum(
        t_ref[0:cols, face:] * r_ref[0:cols, :]
    )


def put(out, at, block):
    cols, half = block.shape[0], block.shape[1] // 2
    out[at : at + cols, :] = block[:, :half]
    out[at + cols : at + 2 * cols, :] = block[:, half:]


def in_lanes(items, start=0):
    cols = items[0].shape[0]
    lane = lax.broadcasted_iota(jnp.int32, (cols, LANE), 1)
    block = jnp.zeros((cols, LANE), F32)
    for k, item in enumerate(items):
        block = jnp.where(lane == start + k, item, block)
    return block


def moment_kernel(sl0_ref, cl_ref, gram_ref, *refs, cols, count):
    out = refs[-1]
    base = 4 * count
    at = base + 8 * cols
    out[at:, :] = jnp.zeros((out.shape[0] - at, LANE), F32)
    own = sl0_ref.shape[0] - cols - 8
    spot = one_hot(sl0_ref[cols + own : cols + own + 1, 0:own], count)
    put(out, base, split_nt(cl_ref[...], spot))
    sums = [level_moments(out, refs[3 * k : 3 * k + 3], k, cols, count) for k in range(2)]
    pack(out, 3, gram_ref[...], at + cols)
    out[at : at + cols, :] = in_lanes(sums)


def last_moment_kernel(given_ref, *refs, cols, count):
    out = refs[-1]
    out[...] = given_ref[...]
    total = level_moments(out, refs[:3], 2, cols, count)
    at = 4 * count + 8 * cols
    out[at : at + cols, :] = given_ref[at : at + cols, :] + in_lanes([total], 2)


def vector(sums_ref, k, cols, count):
    at = 4 * count + 2 * cols * k
    return jnp.concatenate([sums_ref[at : at + cols, :], sums_ref[at + cols : at + 2 * cols, :]], axis=1)


def at_corners(values, ids_ref):
    rows = ids_ref.shape[0]
    spot = one_hot(ids_ref[rows - 8 : rows - 7, 0:LANE], values.shape[1])
    return split_dot(values, spot, 3)


def spread(local, k, ref, lanes, cols):
    width = 8 * (2 * k + 1)
    lane = 8 * (LEVELS - k)
    wide = nn(local[:, lane : lane + width], ref[cols : cols + width, lanes])
    return [wide[i : i + cols] for i in range(0, wide.shape[0], cols)]


def coarse_kernel(sums_ref, coarse_ref, mat_ref, t1, t3, sl3, ol_ref, or_ref, w0_ref,
                  *, cols, count):
    diagonals = 4 * count + 9 * cols
    face = ol_ref.shape[1]
    every = slice(0, 2 * face)
    g0 = nn(vector(sums_ref, 0, cols, count), coarse_ref[...])
    g1 = nn(vector(sums_ref, 1, cols, count) + nn(g0, unpack(sums_ref, 0, diagonals)), coarse_ref[...])
    local = at_corners(jnp.concatenate([g0, g1], axis=0), sl3)
    (p30,) = spread(local[0:cols], 3, t3, every, cols)
    (p11,) = spread(local[cols:], 1, t1, every, cols)
    w0 = t3[0:cols, :] + p30 + p11
    w0_ref[...] = w0
    v = split_dot(w0, mat_ref[...]) * 0.25
    ol_ref[...] = v[:, :face]
    or_ref[...] = v[:, face:]


def values_kernel(sums_ref, coarse_ref, t2, sl3, z0_ref, local_ref, scal_ref, *, cols, count):
    diagonals = 4 * count + 9 * cols
    m0, m1, m2 = (unpack(sums_ref, k, diagonals) for k in range(3))
    coarse = coarse_ref[...]
    c_load, w0x, w1x, w2x = (vector(sums_ref, k, cols, count) for k in range(4))
    at = 4 * count + 8 * cols
    s0, s1, s2 = (sums_ref[at : at + cols, k : k + 1] for k in range(3))
    g0 = nn(c_load, coarse)
    m0g0, m1g0, m2g0 = nn(g0, m0), nn(g0, m1), nn(g0, m2)
    c0 = w0x + m0g0
    g1 = nn(c0, coarse)
    m0g1, m1g1 = nn(g1, m0), nn(g1, m1)
    rz0 = s0 + lane_sum(2.0 * w0x * g0 + g0 * m0g0)
    del0 = s1 + lane_sum(2.0 * w1x * g0 + g0 * m1g0 + c0 * g1)
    nu0 = s2 + lane_sum(2.0 * w2x * g0 + g0 * m2g0 + 2.0 * w1x * g1 + 2.0 * g1 * m1g0 + g1 * m0g1)
    al0 = rz0 / del0
    be1 = (rz0 - 2.0 * al0 * del0 + al0 * al0 * nu0) / rz0
    cz1 = c0 - al0 * (w1x + m1g0 + m0g1)
    gz1 = nn(cz1, coarse)
    cm = (
        (1.0 + be1) * (w1x + m1g0)
        - al0 * (m1g1 + w2x + m2g0)
        + nn(gz1, m0)
        + be1 * m0g1
    )
    gm = nn(cm, coarse)
    local = at_corners(jnp.concatenate([g0, g1, gz1, gm], axis=0), sl3)
    local_ref[...] = local
    (p20,) = spread(local[0:cols], 2, t2, slice(0, t2.shape[1]), cols)
    z0_ref[...] = t2[0:cols, :] + p20
    scal_ref[...] = in_lanes([al0, be1, lane_sum(cm * gm)])


def base_kernel(sums_ref, local_ref, scal_ref, nm_ref, sl0, sr0, t1, sl2, sr2, w0_ref,
                w1c_ref, r1_ref, field_ref, gram_ref, back_ref, *, cols, count):
    diagonals = 4 * count + 9 * cols
    face = sl0.shape[1]
    local = local_ref[...]
    al0 = scal_ref[:, 0:1]
    every, right, whole = slice(0, 2 * face), slice(face, 2 * face), slice(0, face)
    (p10,) = spread(local[0:cols], 1, t1, right, cols)
    (w1c_ref[...],) = spread(local[2 * cols : 3 * cols], 1, t1, every, cols)
    r1_ref[...] = t1[0:cols, right] + p10 - al0 * w0_ref[:, right]
    for own, u, lanes in ((sl0, sl2, slice(0, face)), (sr0, sr2, right)):
        corner = spread(local, 0, own, whole, cols)
        (u0,) = spread(local[0:cols], 2, u, whole, cols)
        field_ref[0:cols, lanes] = own[0:cols, :] + corner[0]
        field_ref[cols : 2 * cols, lanes] = u[0:cols, :] + u0 + corner[1]
        field_ref[2 * cols : 3 * cols, lanes] = corner[2]
        field_ref[3 * cols : 4 * cols, lanes] = corner[3]
    gram_ref[...] = unpack(sums_ref, 3, diagonals)
    back_ref[...] = from_order(nm_ref[...], face).astype(BF16)


def joined(own_ref, other_ref, mask_ref, left):
    face = own_ref.shape[1]
    lanes = slice(0, face) if left else slice(face, 2 * face)
    return (own_ref[...] - other_ref[...]) * mask_ref[0:1, lanes]


def field_of(sl_ref, sr_ref, nl_ref, pr_ref, mask_ref):
    return jnp.concatenate(
        [joined(sl_ref, pr_ref, mask_ref, True), joined(sr_ref, nl_ref, mask_ref, False)], axis=1
    )


def dual_kernel(sl_ref, sr_ref, nl_ref, pr_ref, mask_ref, z0_ref, scal_ref, mat_ref,
                n0_ref, z1_ref, ol_ref, or_ref):
    face = sl_ref.shape[1]
    n0 = field_of(sl_ref, sr_ref, nl_ref, pr_ref, mask_ref)
    z1 = z0_ref[...] - scal_ref[:, 0:1] * n0
    n0_ref[...] = n0
    z1_ref[...] = z1[:, face:]
    u = split_dot(z1, mat_ref[...])
    ol_ref[...] = u[:, :face]
    or_ref[...] = u[:, face:]


def precondition_kernel(sl_ref, sr_ref, nl_ref, pr_ref, mask_ref, w1c_ref, mat_ref,
                        w1_ref, ol_ref, or_ref):
    face = sl_ref.shape[1]
    w1 = field_of(sl_ref, sr_ref, nl_ref, pr_ref, mask_ref) + w1c_ref[...]
    w1_ref[...] = w1[:, face:]
    v = split_dot(w1, mat_ref[...]) * 0.25
    ol_ref[...] = v[:, :face]
    or_ref[...] = v[:, face:]


def early_kernel(scal_ref, z0_ref, z1_ref, ul_ref, ur_ref, r1_ref, w0_ref, w1_ref, base_ref,
                 mass_ref, prev_ref, out_ref, field_ref, *, cols, count):
    half = count // 2
    face = ul_ref.shape[1]
    third = slice(2 * cols, 3 * cols)
    field_ref[0 : 2 * cols, :] = base_ref[0 : 2 * cols, :]
    field_ref[third, 0:face] = base_ref[third, 0:face] + ul_ref[...]
    field_ref[third, face:] = base_ref[third, face:] + ur_ref[...]
    field_ref[3 * cols :, :] = base_ref[3 * cols :, :]
    be1 = scal_ref[:, 1:2]
    z0, w0 = z0_ref[:, face:], w0_ref[:, face:]
    z1, w1, r1 = z1_ref[...], w1_ref[...], r1_ref[...]
    q1 = w1 + be1 * w0
    out_ref[...] = jnp.zeros(out_ref.shape, F32)
    out_ref[12 * cols : 13 * cols, :] = in_lanes([
        lane_sum(r1 * z1), lane_sum(q1 * z1), lane_sum(r1 * (z1 + be1 * z0)),
        lane_sum((z1 + be1 * z0) * q1), lane_sum(z1 * w1),
    ])
    known = field_ref[0 : 3 * cols, :]
    scaled = known * mass_ref[...]
    tq = split_dot(scaled, prev_ref[...], 3)
    out_ref[0 : 3 * cols, :] = tq[:, :half]
    out_ref[4 * cols : 7 * cols, :] = tq[:, half:]
    out_ref[8 * cols : 11 * cols, 0 : 3 * cols] = nt(scaled, known)


def combine_kernel(given_ref, known_ref, sl_ref, sr_ref, nl_ref, pr_ref, mask_ref, n0_ref, mat_ref,
                   scal_ref, r1_ref, w0_ref, w1_ref, mass_ref, prev_ref,
                   out_ref, field_ref, m_ref, *, cols, count):
    half = count // 2
    face = sl_ref.shape[1]
    be1 = scal_ref[:, 1:2]
    out_ref[...] = given_ref[...]
    field_ref[0 : 3 * cols, :] = known_ref[0 : 3 * cols, :]
    whole = field_of(sl_ref, sr_ref, nl_ref, pr_ref, mask_ref) + be1 * n0_ref[...]
    u = split_dot(whole, mat_ref[...])
    last = known_ref[3 * cols :, :] + u
    field_ref[3 * cols :, :] = last
    m = whole[:, face:]
    m_ref[...] = m
    w0, w1 = w0_ref[:, face:], w1_ref[...]
    scaled = last * mass_ref[...]
    tq = split_dot(scaled, prev_ref[...], 3)
    out_ref[3 * cols : 4 * cols, :] = tq[:, :half]
    out_ref[7 * cols : 8 * cols, :] = tq[:, half:]
    out_ref[11 * cols : 12 * cols, :] = nt(scaled, field_ref[...])
    at = 12 * cols
    out_ref[at : at + cols, :] = given_ref[at : at + cols, :] + in_lanes([
        lane_sum(r1_ref[...] * m), lane_sum((w1 + be1 * w0) * m), lane_sum(m * w1),
        lane_sum(whole * u),
    ], 5)


def final_kernel(sums_ref, basis_ref, scal_ref, field_ref, z0_ref, z1_ref, m_ref, prev_ref, back_ref,
                 block_ref, multi_ref, coef_ref, factor_ref, *, cols, count):
    half = count // 2
    face = m_ref.shape[1]
    at = 12 * cols
    r1z1, q1z1, r1p1, p1q1, z1w1, r1m, q1m, mw1, mm = (
        sums_ref[at : at + cols, k : k + 1] for k in range(9)
    )
    al0, be1, extra = (scal_ref[:, k : k + 1] for k in range(3))
    mfm = mm + extra
    al1 = r1p1 / p1q1
    z2q1 = q1z1 - al1 * q1m
    be2 = -z2q1 / p1q1
    rz2 = r1z1 - al1 * (r1m + q1z1) + al1 * al1 * q1m
    z2fz2 = z1w1 - 2.0 * al1 * mw1 + al1 * al1 * mfm
    al2 = rz2 / (z2fz2 + 2.0 * be2 * z2q1 + be2 * be2 * p1q1)
    along = al1 + al2 * be2
    parts = (al0 + along * be1, along + al2, -al1 * al2)
    duals = (z0_ref[:, face:], z1_ref[...], m_ref[...])
    multi_ref[...] = sum(y * dual for y, dual in zip(parts, duals))
    weights = [jnp.ones((cols, 1), F32)] + [-y for y in parts]
    primal = sum(y * field_ref[i * cols : (i + 1) * cols, :] for i, y in enumerate(weights))
    g1 = sum(
        y
        * jnp.concatenate(
            [sums_ref[i * cols : (i + 1) * cols, :], sums_ref[(4 + i) * cols : (5 + i) * cols, :]],
            axis=1,
        )
        for i, y in enumerate(weights)
    )
    row = lax.broadcasted_iota(jnp.int32, (cols, cols), 0)
    col = lax.broadcasted_iota(jnp.int32, (cols, cols), 1)
    eye = (row == col).astype(F32)
    stacked = jnp.concatenate(weights, axis=0)
    across = jnp.concatenate([jnp.sum(y * eye, axis=0, keepdims=True) for y in weights], axis=1)
    tiles = stacked * sums_ref[8 * cols : 12 * cols, :] * across
    cross = tiles[3 * cols :]
    cross = sum(cross[:, j * cols : (j + 1) * cols] for j in range(3))
    tiles = sum(tiles[i * cols : (i + 1) * cols] for i in range(4))
    gram = sum(tiles[:, j * cols : (j + 1) * cols] for j in range(4))
    gram = gram + jnp.transpose(cross)
    basis = basis_ref[...]
    c = 2.0 * g1 - nn(g1, basis)
    coef_ref[...] = c
    gram = gram + nt(c, nn(c, basis) - 2.0 * g1)
    gram = 0.5 * (gram + jnp.transpose(gram))
    final = primal - split_dot(c, prev_ref[...], 3)
    work = jnp.concatenate([gram, eye], axis=1)
    index = lax.broadcasted_iota(jnp.int32, (cols, 1), 0)
    pivots = jnp.zeros(work.shape, F32)
    for start in range(0, cols, 8):
        wide = [jnp.broadcast_to(work[:, start + j : start + j + 1], work.shape) for j in range(8)]
        for j in range(8):
            k = start + j
            pivot = wide[j][k : k + 1, :]
            pivots = jnp.where(index == k, pivot, pivots)
            times = jnp.where(index > k, wide[j], 0.0) * (1.0 / pivot)
            for i in range(j + 1, 8):
                wide[i] = wide[i] - times * wide[i][k : k + 1, :]
            work = work - times * work[k : k + 1, :]
    work = work / jnp.sqrt(pivots)
    factor_ref[...] = jnp.transpose(jnp.where(row <= col, work[:, :cols], 0.0))
    solved = nn(work[:, cols:], final)
    left = split_dot(solved[:, :face], back_ref[...], 3)
    block_ref[:, :face] = left
    block_ref[:, face:] = solved[:, face:]


def sum_kernel(parts_ref, out_ref):
    total = jnp.sum(parts_ref[...], axis=0)
    for i in range(out_ref.shape[0]):
        out_ref[i] = total


def swap(parts, axes):
    return lax.all_to_all(parts, axes, 0, 0, tiled=True)


def summed(parts, copies):
    return call(sum_kernel, jax.ShapeDtypeStruct((copies,) + parts.shape[1:], F32))(parts)


def over_all(rows, n_red, n_z):
    parts = swap(rows.reshape(n_red, rows.shape[0] // n_red, LANE), RED)
    parts = swap(summed(parts, n_z), "zh")
    return swap(summed(parts, n_red), RED).reshape(rows.shape)


def up(count, unit):
    return -(-count // unit) * unit


def solution(mesh):
    n_sub, n_grp = mesh.shape["sub"], mesh.shape["grp"]
    n_y = min(4, n_sub)
    n_zl, n_c = 2, 2
    n_z = n_sub // n_y // n_zl
    n_x = n_grp // n_c
    devices = np.asarray(mesh.devices).reshape(n_y, n_z, n_zl, n_x, n_c)
    fine = Mesh(devices, ("y", "zh", "zl", "x", "c"))
    n_red = n_y * n_zl * n_x * n_c
    along = ("y", "zh", "zl")
    ahead = [(i, i + 1) for i in range(n_sub - 1)]
    behind = [(i + 1, i) for i in range(n_sub - 1)]

    def on_device(schur_inverse, schur, coarse_basis, corner_index, coarse_inverse, neighbor_map,
                  load, previous, mass):
        inverse_block, schur_block, basis = schur_inverse[0, 0], schur[0, 0], coarse_basis[0, 0]
        corners, nm = corner_index[0, 0], neighbor_map[0, 0]
        rhs, earlier, weights = load[0, 0].T, previous[0, 0], mass[0, 0]
        cols, rows = rhs.shape
        face = nm.shape[0]
        count = coarse_inverse.shape[0]
        total = rows * n_sub * n_grp
        own = corners.shape[0]
        position = lax.axis_index(along)
        nm_row = nm[None, :]
        side = jnp.arange(2 * face) < face
        mask = jnp.where(side, position > 0, position < n_sub - 1).astype(F32)[None, :]
        mask = jnp.broadcast_to(mask, (8, 2 * face))

        def shape(*dims):
            return jax.ShapeDtypeStruct(dims, F32)

        half = shape(cols + own + 8, face)
        sl, sr, cl = pl.pallas_call(
            start_kernel,
            out_shape=(half, half, shape(cols, own)),
            in_specs=[pl.BlockSpec(memory_space=pl.ANY)] * 5,
            scratch_shapes=[
                pltpu.VMEM((rows, rows), BF16),
                pltpu.VMEM((cols, rows), F32),
                pltpu.VMEM((own, rows), F32),
                pltpu.VMEM((1, face), jnp.int32),
                pltpu.VMEM((1, own), jnp.int32),
                pltpu.SemaphoreType.DMA((5,)),
            ],
            compiler_params=pltpu.CompilerParams(vmem_limit_bytes=60 * 1024 * 1024),
        )(inverse_block, rhs, basis, nm_row, corners[None, :])
        square = jax.ShapeDtypeStruct((rows, rows), BF16)

        def exchange(sl, sr):
            return lax.ppermute(sl, along, behind), lax.ppermute(sr, along, ahead)

        def step(k, sl, sr, near, mat):
            width = own + 16 * (k - 1)
            out = cols + width + 16
            return call(
                lambda *refs: step_kernel(
                    *refs, cols=cols, width=width, scale=0.25 if k % 2 == 1 else 1.0
                ),
                (shape(out, 2 * face), shape(out + 8, face), shape(out + 8, face)),
            )(sl, sr, *near, mask, mat)

        chain = [sl, sr]
        near = exchange(sl, sr)
        schur_p = call(matrix_kernel, square)(schur_block, nm_row)
        t, sl, sr = step(1, sl, sr, near, schur_p)
        chain += [t, sl, sr]
        near = exchange(sl, sr)
        inv_p = call(matrix_kernel, square)(inverse_block, nm_row)
        prev_p, prev_t, mass_p, gram = call(
            lambda *refs: basis_kernel(*refs, total=total),
            (
                jax.ShapeDtypeStruct(earlier.shape, BF16),
                jax.ShapeDtypeStruct(earlier.shape[::-1], BF16),
                shape(1, rows),
                shape(count, count),
            ),
        )(earlier, nm_row, weights[None, :])
        near, gram = lax.optimization_barrier((near, gram))
        t, sl, sr = step(2, sl, sr, near, inv_p)
        chain += [t, sl, sr]
        near = exchange(sl, sr)
        size = up(4 * count + 9 * cols + 8, 8 * n_red)
        first = call(
            lambda *refs: moment_kernel(*refs, cols=cols, count=count), shape(size, LANE)
        )(chain[0], cl, gram, *chain[2:8])
        t, sl, sr = step(3, sl, sr, near, schur_p)
        chain += [t, sl, sr]
        first = call(
            lambda *refs: last_moment_kernel(*refs, cols=cols, count=count),
            shape(size, LANE),
        )(first, t, sl, sr)
        first = over_all(first, n_red, n_z)

        wide, part = shape(cols, 2 * face), shape(cols, face)
        sl0, sr0, t1, _, _, t2, sl2, sr2, t3, sl3, _ = chain
        sl, sr, w0 = call(
            lambda *refs: coarse_kernel(*refs, cols=cols, count=count), (part, part, wide)
        )(first, coarse_inverse, schur_p, t1, t3, sl3)
        z0, local, scal = call(
            lambda *refs: values_kernel(*refs, cols=cols, count=count),
            (wide, shape(4 * cols, LANE), shape(cols, LANE)),
        )(first, coarse_inverse, t2, sl3)
        near = exchange(sl, sr)
        n0, z1, ul, ur = call(dual_kernel, (wide, part, part, part))(
            sl, sr, *near, mask, z0, scal, inv_p
        )
        near = exchange(ul, ur)
        w1c, r1, base, gram, back = call(
            lambda *refs: base_kernel(*refs, cols=cols, count=count),
            (wide, part, shape(4 * cols, rows), shape(count, count),
             jax.ShapeDtypeStruct((face, face), BF16)),
        )(first, local, scal, nm_row, sl0, sr0, t1, sl2, sr2, w0)
        w1, sl, sr = call(precondition_kernel, (part, part, part))(
            ul, ur, *near, mask, w1c, schur_p
        )
        near = exchange(sl, sr)
        size = up(13 * cols, 8 * n_red)
        second, field = call(
            lambda *refs: early_kernel(*refs, cols=cols, count=count),
            (shape(size, LANE), shape(4 * cols, rows)),
        )(scal, z0, z1, ul, ur, r1, w0, w1, base, mass_p, prev_p)
        second, field, m = call(
            lambda *refs: combine_kernel(*refs, cols=cols, count=count),
            (shape(size, LANE), shape(4 * cols, rows), part),
        )(second, field, sl, sr, *near, mask, n0, inv_p, scal, r1, w0, w1, mass_p, prev_p)
        second = over_all(second, n_red, n_z)
        block, multi, coefficients, factor = call(
            lambda *refs: final_kernel(*refs, cols=cols, count=count),
            (shape(cols, rows), shape(cols, face), shape(cols, count), shape(cols, cols)),
        )(second, gram, scal, field, z0, z1, m, prev_t, back)
        return block.T[None, None], multi.T[None, None], coefficients.T, factor

    split = (along, ("x", "c"))
    return jax.shard_map(
        on_device,
        mesh=fine,
        in_specs=(
            P(*split, None, None),
            P(*split, None, None),
            P(*split, None, None),
            P(*split, None),
            P(),
            P(*split, None),
            P(*split, None, None),
            P(*split, None, None),
            P(*split, None),
        ),
        out_specs=(P(*split, None, None), P(*split, None, None), P(), P()),
        check_vma=False,
    )
```

```python
import jax
import jax.numpy as jnp
import numpy as np
from jax import lax
from jax.experimental import pallas as pl
from jax.experimental.pallas import tpu as pltpu
from jax.sharding import Mesh, PartitionSpec as P

HI = lax.Precision.HIGHEST
F32 = jnp.float32
BF16 = jnp.bfloat16
RED = ("y", "zl", "x", "c")
LEVELS = 3
LANE = 128


def nn(a, b):
    return jnp.dot(a, b, precision=HI, preferred_element_type=F32)


def nt(a, b):
    return lax.dot_general(
        a, b, (((1,), (1,)), ((), ())), precision=HI, preferred_element_type=F32
    )


def lane_sum(a):
    return jnp.sum(a, axis=1, keepdims=True)


def call(kernel, outs):
    return pl.pallas_call(
        kernel,
        out_shape=outs,
        compiler_params=pltpu.CompilerParams(vmem_limit_bytes=12 * 1024 * 1024),
    )


def pieces_of(t, parts, axis):
    pieces = []
    for _ in range(parts - 1):
        pieces.append(t.astype(BF16).astype(F32))
        t = t - pieces[-1]
    return jnp.concatenate(pieces + [t], axis=axis).astype(BF16)


def split_dot(t, mat, parts=2):
    wide = jnp.dot(pieces_of(t, parts, 0), mat, preferred_element_type=F32)
    rows = t.shape[0]
    return sum(wide[i * rows : (i + 1) * rows] for i in range(1, parts)) + wide[:rows]


def split_nt(t, mat):
    rows = t.shape[0]
    wide = lax.dot_general(
        pieces_of(t, 3, 0), mat, (((1,), (1,)), ((), ())), preferred_element_type=F32
    )
    return wide[2 * rows :] + wide[rows : 2 * rows] + wide[:rows]


def split_right(mat, t):
    cols = t.shape[1]
    wide = jnp.dot(mat, pieces_of(t, 3, 1), preferred_element_type=F32)
    return wide[:, 2 * cols :] + wide[:, cols : 2 * cols] + wide[:, :cols]


def to_order(nm_row, face):
    nm = jnp.transpose(jnp.broadcast_to(nm_row.astype(F32), (8, face)))[:, 0:1]
    return (nm == lax.broadcasted_iota(jnp.int32, (face, face), 1).astype(F32)).astype(F32)


def from_order(nm_row, face):
    return (nm_row == lax.broadcasted_iota(jnp.int32, (face, face), 0)).astype(F32)


def start_kernel(inv_hbm, load_hbm, basis_hbm, nm_hbm, corner_hbm, sl_ref, sr_ref, cl_ref,
                 inv_ref, load_ref, basis_ref, nm_ref, corner_ref, sems):
    pairs = (
        (nm_hbm, nm_ref), (load_hbm, load_ref), (basis_hbm, basis_ref), (corner_hbm, corner_ref),
        (inv_hbm, inv_ref),
    )
    copies = [pltpu.make_async_copy(src, dst, sems.at[i]) for i, (src, dst) in enumerate(pairs)]
    for copy in copies:
        copy.start()
    for copy in copies[:-1]:
        copy.wait()
    face = nm_ref.shape[1]
    cols = load_ref.shape[0]
    corners = basis_ref.shape[0]
    rows = cols + corners
    load = load_ref[...]
    basis = basis_ref[...]
    order = to_order(nm_ref[...], face).astype(BF16)
    cl_ref[...] = nt(load, basis)
    for ref in (sl_ref, sr_ref):
        ref[rows : rows + 8, :] = jnp.zeros((8, face), F32)
        ref[rows : rows + 1, 0:corners] = corner_ref[...].astype(F32)
    sr_ref[cols:rows, :] = basis[:, face:]
    copies[-1].wait()
    wide = split_dot(load, inv_ref[...])
    sr_ref[0:cols, :] = wide[:, face:]
    left = [wide[:, :face], basis[:, :face], jnp.zeros((8, face), F32)]
    left = split_dot(jnp.concatenate(left, axis=0), order, 3)
    sl_ref[0:rows, :] = left[0:rows]


def matrix_kernel(src, nm_ref, dst):
    face = nm_ref.shape[1]
    order = to_order(nm_ref[...], face).astype(BF16)
    back = from_order(nm_ref[...], face).astype(BF16)
    dst[:, face:] = src[:, face:]
    dst[:, :face] = jnp.dot(src[:, :face], order, preferred_element_type=F32).astype(BF16)
    dst[:face, :] = jnp.dot(back, dst[:face, :], preferred_element_type=F32).astype(BF16)


def basis_kernel(prev_ref, nm_ref, mass_ref, prev_out, flip_out, mass_out, *, total):
    face = nm_ref.shape[1]
    back = from_order(nm_ref[...], face).astype(BF16)
    prev_out[face:, :] = prev_ref[face:, :]
    prev_out[:face, :] = jnp.dot(back, prev_ref[:face, :], preferred_element_type=F32).astype(BF16)
    flip_out[...] = jnp.transpose(prev_out[...].astype(F32)).astype(BF16)
    mass = mass_ref[...] / total
    mass_out[:, face:] = mass[:, face:]
    left = jnp.broadcast_to(mass[:, :face], (8, face))
    mass_out[:, :face] = nn(left, to_order(nm_ref[...], face))[0:1]


def gram_kernel(prev_ref, mass_ref, gram_out, *, total):
    mass = mass_ref[...] / total
    column = jnp.transpose(jnp.broadcast_to(mass, (8, mass.shape[1])))[:, 0:1]
    wide = prev_ref[...].astype(F32)
    gram_out[...] = lax.dot_general(
        wide * column, wide, (((0,), (0,)), ((), ())), precision=HI, preferred_element_type=F32
    )


def step_kernel(sl_ref, sr_ref, nl_ref, pr_ref, mask_ref, mat_ref, t_ref, ol_ref, or_ref,
                *, cols, width, scale):
    face = sl_ref.shape[1]
    new = width + 16
    rows = cols + new
    old = cols + width
    for lanes, own, other, shift in (
        (slice(0, face), sl_ref, pr_ref, 0),
        (slice(face, 2 * face), sr_ref, nl_ref, 16),
    ):
        keep = mask_ref[0:1, lanes]
        t_ref[0:cols, lanes] = (own[0:cols, :] - other[0:cols, :]) * keep
        edge = jnp.zeros((8, face), F32)
        mine = jnp.concatenate([edge, own[cols:old, :], edge], axis=0)
        blank = jnp.zeros((16, face), F32)
        theirs = other[cols:old, :]
        theirs = jnp.concatenate([theirs, blank] if shift == 0 else [blank, theirs], axis=0)
        t_ref[cols:rows, lanes] = (mine - theirs) * keep
    v = split_dot(t_ref[...], mat_ref[...])
    if scale != 1.0:
        v = v * scale
    ids = jnp.concatenate(
        [
            pr_ref[old : old + 8, 0:8],
            sl_ref[old : old + 8, 0:width],
            nl_ref[old : old + 8, width - 8 : width],
        ],
        axis=1,
    )
    for ref, lanes in ((ol_ref, slice(0, face)), (or_ref, slice(face, 2 * face))):
        ref[0:rows, :] = v[:, lanes]
        ref[rows : rows + 8, :] = jnp.zeros((8, face), F32)
        ref[rows : rows + 8, 0:new] = ids


def one_hot(ids, count):
    dof = lax.broadcasted_iota(jnp.int32, (count, ids.shape[1]), 0).astype(F32)
    return (ids == dof).astype(F32).astype(BF16)


def lower(half):
    row = lax.broadcasted_iota(jnp.int32, (half, half), 0)
    col = lax.broadcasted_iota(jnp.int32, (half, half), 1)
    return row, col


def pack(ref, k, matrix, diagonals):
    half = LANE
    at = 2 * half * k
    row, col = lower(half)
    last = matrix[half:, half:]
    ref[at : at + half, :] = jnp.where(row >= col, matrix[:half, :half], last)
    ref[at + half : at + 2 * half, :] = matrix[half:, :half]
    ref[diagonals + k : diagonals + k + 1, :] = jnp.sum(
        jnp.where(row == col, last, 0.0), axis=0, keepdims=True
    )


def unpack(ref, k, diagonals):
    half = LANE
    at = 2 * half * k
    row, col = lower(half)
    shared = ref[at : at + half, :]
    flipped = jnp.transpose(shared)
    cross = ref[at + half : at + 2 * half, :]
    first = jnp.where(row >= col, shared, flipped)
    last = jnp.where(row < col, shared, flipped)
    last = jnp.where(row == col, ref[diagonals + k : diagonals + k + 1, :], last)
    return jnp.concatenate(
        [
            jnp.concatenate([first, jnp.transpose(cross)], axis=1),
            jnp.concatenate([cross, last], axis=1),
        ],
        axis=0,
    )


def level_moments(out, refs, k, cols, count):
    base = 4 * count
    t_ref, l_ref, r_ref = refs
    rows, double = t_ref.shape
    face = double // 2
    width = rows - cols
    spot = one_hot(l_ref[rows : rows + 1, 0:width], count)
    tl, tr = t_ref[cols:rows, :face], t_ref[cols:rows, face:]
    inner = split_nt(nt(l_ref[0:rows, :], tl) + nt(r_ref[0:rows, :], tr), spot)
    put(out, base + 2 * cols * (k + 1), inner[0:cols])
    pack(out, k, split_right(spot, inner[cols:rows]), base + 9 * cols)
    return lane_sum(t_ref[0:cols, :face] * l_ref[0:cols, :]) + lane_sum(
        t_ref[0:cols, face:] * r_ref[0:cols, :]
    )


def put(out, at, block):
    cols, half = block.shape[0], block.shape[1] // 2
    out[at : at + cols, :] = block[:, :half]
    out[at + cols : at + 2 * cols, :] = block[:, half:]


def in_lanes(items, start=0):
    cols = items[0].shape[0]
    lane = lax.broadcasted_iota(jnp.int32, (cols, LANE), 1)
    block = jnp.zeros((cols, LANE), F32)
    for k, item in enumerate(items):
        block = jnp.where(lane == start + k, item, block)
    return block


def moment_kernel(sl0_ref, cl_ref, gram_ref, *refs, cols, count):
    out = refs[-1]
    base = 4 * count
    at = base + 8 * cols
    out[at:, :] = jnp.zeros((out.shape[0] - at, LANE), F32)
    own = sl0_ref.shape[0] - cols - 8
    spot = one_hot(sl0_ref[cols + own : cols + own + 1, 0:own], count)
    put(out, base, split_nt(cl_ref[...], spot))
    sums = [level_moments(out, refs[3 * k : 3 * k + 3], k, cols, count) for k in range(2)]
    pack(out, 3, gram_ref[...], at + cols)
    out[at : at + cols, :] = in_lanes(sums)


def last_moment_kernel(given_ref, *refs, cols, count):
    out = refs[-1]
    out[...] = given_ref[...]
    total = level_moments(out, refs[:3], 2, cols, count)
    at = 4 * count + 8 * cols
    out[at : at + cols, :] = given_ref[at : at + cols, :] + in_lanes([total], 2)


def vector(sums_ref, k, cols, count):
    at = 4 * count + 2 * cols * k
    return jnp.concatenate([sums_ref[at : at + cols, :], sums_ref[at + cols : at + 2 * cols, :]], axis=1)


def at_corners(values, ids_ref):
    rows = ids_ref.shape[0]
    spot = one_hot(ids_ref[rows - 8 : rows - 7, 0:LANE], values.shape[1])
    return split_dot(values, spot, 3)


def spread(local, k, ref, lanes, cols):
    width = 8 * (2 * k + 1)
    lane = 8 * (LEVELS - k)
    wide = nn(local[:, lane : lane + width], ref[cols : cols + width, lanes])
    return [wide[i : i + cols] for i in range(0, wide.shape[0], cols)]


def coarse_kernel(sums_ref, coarse_ref, mat_ref, t1, t3, sl3, ol_ref, or_ref, w0_ref,
                  *, cols, count):
    diagonals = 4 * count + 9 * cols
    face = ol_ref.shape[1]
    every = slice(0, 2 * face)
    g0 = nn(vector(sums_ref, 0, cols, count), coarse_ref[...])
    g1 = nn(vector(sums_ref, 1, cols, count) + nn(g0, unpack(sums_ref, 0, diagonals)), coarse_ref[...])
    local = at_corners(jnp.concatenate([g0, g1], axis=0), sl3)
    (p30,) = spread(local[0:cols], 3, t3, every, cols)
    (p11,) = spread(local[cols:], 1, t1, every, cols)
    w0 = t3[0:cols, :] + p30 + p11
    w0_ref[...] = w0
    v = split_dot(w0, mat_ref[...]) * 0.25
    ol_ref[...] = v[:, :face]
    or_ref[...] = v[:, face:]


def values_kernel(sums_ref, coarse_ref, t2, sl3, z0_ref, local_ref, scal_ref, *, cols, count):
    diagonals = 4 * count + 9 * cols
    m0, m1, m2 = (unpack(sums_ref, k, diagonals) for k in range(3))
    coarse = coarse_ref[...]
    c_load, w0x, w1x, w2x = (vector(sums_ref, k, cols, count) for k in range(4))
    at = 4 * count + 8 * cols
    s0, s1, s2 = (sums_ref[at : at + cols, k : k + 1] for k in range(3))
    g0 = nn(c_load, coarse)
    m0g0, m1g0, m2g0 = nn(g0, m0), nn(g0, m1), nn(g0, m2)
    c0 = w0x + m0g0
    g1 = nn(c0, coarse)
    m0g1, m1g1 = nn(g1, m0), nn(g1, m1)
    rz0 = s0 + lane_sum(2.0 * w0x * g0 + g0 * m0g0)
    del0 = s1 + lane_sum(2.0 * w1x * g0 + g0 * m1g0 + c0 * g1)
    nu0 = s2 + lane_sum(2.0 * w2x * g0 + g0 * m2g0 + 2.0 * w1x * g1 + 2.0 * g1 * m1g0 + g1 * m0g1)
    al0 = rz0 / del0
    be1 = (rz0 - 2.0 * al0 * del0 + al0 * al0 * nu0) / rz0
    cz1 = c0 - al0 * (w1x + m1g0 + m0g1)
    gz1 = nn(cz1, coarse)
    cm = (
        (1.0 + be1) * (w1x + m1g0)
        - al0 * (m1g1 + w2x + m2g0)
        + nn(gz1, m0)
        + be1 * m0g1
    )
    gm = nn(cm, coarse)
    local = at_corners(jnp.concatenate([g0, g1, gz1, gm], axis=0), sl3)
    local_ref[...] = local
    (p20,) = spread(local[0:cols], 2, t2, slice(0, t2.shape[1]), cols)
    z0_ref[...] = t2[0:cols, :] + p20
    scal_ref[...] = in_lanes([al0, be1, lane_sum(cm * gm)])


def base_kernel(sums_ref, local_ref, scal_ref, nm_ref, sl0, sr0, t1, sl2, sr2, w0_ref,
                w1c_ref, r1_ref, field_ref, gram_ref, back_ref, *, cols, count):
    diagonals = 4 * count + 9 * cols
    face = sl0.shape[1]
    local = local_ref[...]
    al0 = scal_ref[:, 0:1]
    every, right, whole = slice(0, 2 * face), slice(face, 2 * face), slice(0, face)
    (p10,) = spread(local[0:cols], 1, t1, right, cols)
    (w1c_ref[...],) = spread(local[2 * cols : 3 * cols], 1, t1, every, cols)
    r1_ref[...] = t1[0:cols, right] + p10 - al0 * w0_ref[:, right]
    for own, u, lanes in ((sl0, sl2, slice(0, face)), (sr0, sr2, right)):
        corner = spread(local, 0, own, whole, cols)
        (u0,) = spread(local[0:cols], 2, u, whole, cols)
        field_ref[0:cols, lanes] = own[0:cols, :] + corner[0]
        field_ref[cols : 2 * cols, lanes] = u[0:cols, :] + u0 + corner[1]
        field_ref[2 * cols : 3 * cols, lanes] = corner[2]
        field_ref[3 * cols : 4 * cols, lanes] = corner[3]
    gram_ref[...] = unpack(sums_ref, 3, diagonals)
    back_ref[...] = from_order(nm_ref[...], face).astype(BF16)


def joined(own_ref, other_ref, mask_ref, left):
    face = own_ref.shape[1]
    lanes = slice(0, face) if left else slice(face, 2 * face)
    return (own_ref[...] - other_ref[...]) * mask_ref[0:1, lanes]


def field_of(sl_ref, sr_ref, nl_ref, pr_ref, mask_ref):
    return jnp.concatenate(
        [joined(sl_ref, pr_ref, mask_ref, True), joined(sr_ref, nl_ref, mask_ref, False)], axis=1
    )


def dual_kernel(sl_ref, sr_ref, nl_ref, pr_ref, mask_ref, z0_ref, scal_ref, mat_ref,
                n0_ref, z1_ref, ol_ref, or_ref):
    face = sl_ref.shape[1]
    n0 = field_of(sl_ref, sr_ref, nl_ref, pr_ref, mask_ref)
    z1 = z0_ref[...] - scal_ref[:, 0:1] * n0
    n0_ref[...] = n0
    z1_ref[...] = z1[:, face:]
    u = split_dot(z1, mat_ref[...])
    ol_ref[...] = u[:, :face]
    or_ref[...] = u[:, face:]


def precondition_kernel(sl_ref, sr_ref, nl_ref, pr_ref, mask_ref, w1c_ref, mat_ref,
                        w1_ref, ol_ref, or_ref):
    face = sl_ref.shape[1]
    w1 = field_of(sl_ref, sr_ref, nl_ref, pr_ref, mask_ref) + w1c_ref[...]
    w1_ref[...] = w1[:, face:]
    v = split_dot(w1, mat_ref[...]) * 0.25
    ol_ref[...] = v[:, :face]
    or_ref[...] = v[:, face:]


def early_kernel(scal_ref, z0_ref, z1_ref, ul_ref, ur_ref, r1_ref, w0_ref, w1_ref, base_ref,
                 mass_ref, prev_ref, out_ref, field_ref, *, cols, count):
    half = count // 2
    face = ul_ref.shape[1]
    third = slice(2 * cols, 3 * cols)
    field_ref[0 : 2 * cols, :] = base_ref[0 : 2 * cols, :]
    field_ref[third, 0:face] = base_ref[third, 0:face] + ul_ref[...]
    field_ref[third, face:] = base_ref[third, face:] + ur_ref[...]
    field_ref[3 * cols :, :] = base_ref[3 * cols :, :]
    be1 = scal_ref[:, 1:2]
    z0, w0 = z0_ref[:, face:], w0_ref[:, face:]
    z1, w1, r1 = z1_ref[...], w1_ref[...], r1_ref[...]
    q1 = w1 + be1 * w0
    out_ref[...] = jnp.zeros(out_ref.shape, F32)
    out_ref[12 * cols : 13 * cols, :] = in_lanes([
        lane_sum(r1 * z1), lane_sum(q1 * z1), lane_sum(r1 * (z1 + be1 * z0)),
        lane_sum((z1 + be1 * z0) * q1), lane_sum(z1 * w1),
    ])
    known = field_ref[0 : 3 * cols, :]
    scaled = known * mass_ref[...]
    tq = split_dot(scaled, prev_ref[...], 3)
    out_ref[0 : 3 * cols, :] = tq[:, :half]
    out_ref[4 * cols : 7 * cols, :] = tq[:, half:]
    out_ref[8 * cols : 11 * cols, 0 : 3 * cols] = nt(scaled, known)


def combine_kernel(given_ref, known_ref, sl_ref, sr_ref, nl_ref, pr_ref, mask_ref, n0_ref, mat_ref,
                   scal_ref, r1_ref, w0_ref, w1_ref, mass_ref, prev_ref,
                   out_ref, field_ref, m_ref, *, cols, count):
    half = count // 2
    face = sl_ref.shape[1]
    be1 = scal_ref[:, 1:2]
    out_ref[...] = given_ref[...]
    field_ref[0 : 3 * cols, :] = known_ref[0 : 3 * cols, :]
    whole = field_of(sl_ref, sr_ref, nl_ref, pr_ref, mask_ref) + be1 * n0_ref[...]
    u = split_dot(whole, mat_ref[...])
    last = known_ref[3 * cols :, :] + u
    field_ref[3 * cols :, :] = last
    m = whole[:, face:]
    m_ref[...] = m
    w0, w1 = w0_ref[:, face:], w1_ref[...]
    scaled = last * mass_ref[...]
    tq = split_dot(scaled, prev_ref[...], 3)
    out_ref[3 * cols : 4 * cols, :] = tq[:, :half]
    out_ref[7 * cols : 8 * cols, :] = tq[:, half:]
    out_ref[11 * cols : 12 * cols, :] = nt(scaled, field_ref[...])
    at = 12 * cols
    out_ref[at : at + cols, :] = given_ref[at : at + cols, :] + in_lanes([
        lane_sum(r1_ref[...] * m), lane_sum((w1 + be1 * w0) * m), lane_sum(m * w1),
        lane_sum(whole * u),
    ], 5)


def final_kernel(sums_ref, basis_ref, scal_ref, field_ref, z0_ref, z1_ref, m_ref, prev_ref, back_ref,
                 block_ref, multi_ref, coef_ref, factor_ref, *, cols, count):
    half = count // 2
    face = m_ref.shape[1]
    at = 12 * cols
    r1z1, q1z1, r1p1, p1q1, z1w1, r1m, q1m, mw1, mm = (
        sums_ref[at : at + cols, k : k + 1] for k in range(9)
    )
    al0, be1, extra = (scal_ref[:, k : k + 1] for k in range(3))
    mfm = mm + extra
    al1 = r1p1 / p1q1
    z2q1 = q1z1 - al1 * q1m
    be2 = -z2q1 / p1q1
    rz2 = r1z1 - al1 * (r1m + q1z1) + al1 * al1 * q1m
    z2fz2 = z1w1 - 2.0 * al1 * mw1 + al1 * al1 * mfm
    al2 = rz2 / (z2fz2 + 2.0 * be2 * z2q1 + be2 * be2 * p1q1)
    along = al1 + al2 * be2
    parts = (al0 + along * be1, along + al2, -al1 * al2)
    duals = (z0_ref[:, face:], z1_ref[...], m_ref[...])
    multi_ref[...] = sum(y * dual for y, dual in zip(parts, duals))
    weights = [jnp.ones((cols, 1), F32)] + [-y for y in parts]
    primal = sum(y * field_ref[i * cols : (i + 1) * cols, :] for i, y in enumerate(weights))
    g1 = sum(
        y
        * jnp.concatenate(
            [sums_ref[i * cols : (i + 1) * cols, :], sums_ref[(4 + i) * cols : (5 + i) * cols, :]],
            axis=1,
        )
        for i, y in enumerate(weights)
    )
    row = lax.broadcasted_iota(jnp.int32, (cols, cols), 0)
    col = lax.broadcasted_iota(jnp.int32, (cols, cols), 1)
    eye = (row == col).astype(F32)
    stacked = jnp.concatenate(weights, axis=0)
    across = jnp.concatenate([jnp.sum(y * eye, axis=0, keepdims=True) for y in weights], axis=1)
    tiles = stacked * sums_ref[8 * cols : 12 * cols, :] * across
    cross = tiles[3 * cols :]
    cross = sum(cross[:, j * cols : (j + 1) * cols] for j in range(3))
    tiles = sum(tiles[i * cols : (i + 1) * cols] for i in range(4))
    gram = sum(tiles[:, j * cols : (j + 1) * cols] for j in range(4))
    gram = gram + jnp.transpose(cross)
    basis = basis_ref[...]
    c = 2.0 * g1 - nn(g1, basis)
    coef_ref[...] = c
    gram = gram + nt(c, nn(c, basis) - 2.0 * g1)
    gram = 0.5 * (gram + jnp.transpose(gram))
    final = primal - split_dot(c, prev_ref[...], 3)
    work = jnp.concatenate([gram, eye], axis=1)
    index = lax.broadcasted_iota(jnp.int32, (cols, 1), 0)
    pivots = jnp.zeros(work.shape, F32)
    for start in range(0, cols, 8):
        wide = [jnp.broadcast_to(work[:, start + j : start + j + 1], work.shape) for j in range(8)]
        for j in range(8):
            k = start + j
            pivot = wide[j][k : k + 1, :]
            pivots = jnp.where(index == k, pivot, pivots)
            times = jnp.where(index > k, wide[j], 0.0) * (1.0 / pivot)
            for i in range(j + 1, 8):
                wide[i] = wide[i] - times * wide[i][k : k + 1, :]
            work = work - times * work[k : k + 1, :]
    work = work / jnp.sqrt(pivots)
    factor_ref[...] = jnp.transpose(jnp.where(row <= col, work[:, :cols], 0.0))
    solved = nn(work[:, cols:], final)
    left = split_dot(solved[:, :face], back_ref[...], 3)
    block_ref[:, :face] = left
    block_ref[:, face:] = solved[:, face:]


def sum_kernel(parts_ref, out_ref):
    total = jnp.sum(parts_ref[...], axis=0)
    for i in range(out_ref.shape[0]):
        out_ref[i] = total


def swap(parts, axes):
    return lax.all_to_all(parts, axes, 0, 0, tiled=True)


def summed(parts, copies):
    return call(sum_kernel, jax.ShapeDtypeStruct((copies,) + parts.shape[1:], F32))(parts)


def over_all(rows, n_red, n_z):
    parts = swap(rows.reshape(n_red, rows.shape[0] // n_red, LANE), RED)
    parts = swap(summed(parts, n_z), "zh")
    return swap(summed(parts, n_red), RED).reshape(rows.shape)


def up(count, unit):
    return -(-count // unit) * unit


def solution(mesh):
    n_sub, n_grp = mesh.shape["sub"], mesh.shape["grp"]
    n_y = min(4, n_sub)
    n_zl, n_c = 2, 2
    n_z = n_sub // n_y // n_zl
    n_x = n_grp // n_c
    devices = np.asarray(mesh.devices).reshape(n_y, n_z, n_zl, n_x, n_c)
    fine = Mesh(devices, ("y", "zh", "zl", "x", "c"))
    n_red = n_y * n_zl * n_x * n_c
    along = ("y", "zh", "zl")
    ahead = [(i, i + 1) for i in range(n_sub - 1)]
    behind = [(i + 1, i) for i in range(n_sub - 1)]

    def on_device(schur_inverse, schur, coarse_basis, corner_index, coarse_inverse, neighbor_map,
                  load, previous, mass):
        inverse_block, schur_block, basis = schur_inverse[0, 0], schur[0, 0], coarse_basis[0, 0]
        corners, nm = corner_index[0, 0], neighbor_map[0, 0]
        rhs, earlier, weights = load[0, 0].T, previous[0, 0], mass[0, 0]
        cols, rows = rhs.shape
        face = nm.shape[0]
        count = coarse_inverse.shape[0]
        total = rows * n_sub * n_grp
        own = corners.shape[0]
        position = lax.axis_index(along)
        nm_row = nm[None, :]
        side = jnp.arange(2 * face) < face
        mask = jnp.where(side, position > 0, position < n_sub - 1).astype(F32)[None, :]
        mask = jnp.broadcast_to(mask, (8, 2 * face))

        def shape(*dims):
            return jax.ShapeDtypeStruct(dims, F32)

        half = shape(cols + own + 8, face)
        sl, sr, cl = pl.pallas_call(
            start_kernel,
            out_shape=(half, half, shape(cols, own)),
            in_specs=[pl.BlockSpec(memory_space=pl.ANY)] * 5,
            scratch_shapes=[
                pltpu.VMEM((rows, rows), BF16),
                pltpu.VMEM((cols, rows), F32),
                pltpu.VMEM((own, rows), F32),
                pltpu.VMEM((1, face), jnp.int32),
                pltpu.VMEM((1, own), jnp.int32),
                pltpu.SemaphoreType.DMA((5,)),
            ],
            compiler_params=pltpu.CompilerParams(vmem_limit_bytes=60 * 1024 * 1024),
        )(inverse_block, rhs, basis, nm_row, corners[None, :])
        square = jax.ShapeDtypeStruct((rows, rows), BF16)

        def exchange(sl, sr):
            return lax.ppermute(sl, along, behind), lax.ppermute(sr, along, ahead)

        def step(k, sl, sr, near, mat):
            width = own + 16 * (k - 1)
            out = cols + width + 16
            return call(
                lambda *refs: step_kernel(
                    *refs, cols=cols, width=width, scale=0.25 if k % 2 == 1 else 1.0
                ),
                (shape(out, 2 * face), shape(out + 8, face), shape(out + 8, face)),
            )(sl, sr, *near, mask, mat)

        chain = [sl, sr]
        near = exchange(sl, sr)
        schur_p = call(matrix_kernel, square)(schur_block, nm_row)
        t, sl, sr = step(1, sl, sr, near, schur_p)
        chain += [t, sl, sr]
        near = exchange(sl, sr)
        inv_p = call(matrix_kernel, square)(inverse_block, nm_row)
        gram = call(lambda *refs: gram_kernel(*refs, total=total), shape(count, count))(
            earlier, weights[None, :]
        )
        near, gram = lax.optimization_barrier((near, gram))
        t, sl, sr = step(2, sl, sr, near, inv_p)
        chain += [t, sl, sr]
        near = exchange(sl, sr)
        size = up(4 * count + 9 * cols + 8, 8 * n_red)
        first = call(
            lambda *refs: moment_kernel(*refs, cols=cols, count=count), shape(size, LANE)
        )(chain[0], cl, gram, *chain[2:8])
        t, sl, sr = step(3, sl, sr, near, schur_p)
        chain += [t, sl, sr]
        first = call(
            lambda *refs: last_moment_kernel(*refs, cols=cols, count=count),
            shape(size, LANE),
        )(first, t, sl, sr)
        first = over_all(first, n_red, n_z)

        wide, part = shape(cols, 2 * face), shape(cols, face)
        sl0, sr0, t1, _, _, t2, sl2, sr2, t3, sl3, _ = chain
        sl, sr, w0 = call(
            lambda *refs: coarse_kernel(*refs, cols=cols, count=count), (part, part, wide)
        )(first, coarse_inverse, schur_p, t1, t3, sl3)
        z0, local, scal = call(
            lambda *refs: values_kernel(*refs, cols=cols, count=count),
            (wide, shape(4 * cols, LANE), shape(cols, LANE)),
        )(first, coarse_inverse, t2, sl3)
        near = exchange(sl, sr)
        n0, z1, ul, ur = call(dual_kernel, (wide, part, part, part))(
            sl, sr, *near, mask, z0, scal, inv_p
        )
        near = exchange(ul, ur)
        late, ul = lax.optimization_barrier((earlier, ul))
        prev_p, prev_t, mass_p = call(
            lambda *refs: basis_kernel(*refs, total=total),
            (
                jax.ShapeDtypeStruct(earlier.shape, BF16),
                jax.ShapeDtypeStruct(earlier.shape[::-1], BF16),
                shape(1, rows),
            ),
        )(late, nm_row, weights[None, :])
        near, prev_p = lax.optimization_barrier((near, prev_p))
        w1c, r1, base, gram, back = call(
            lambda *refs: base_kernel(*refs, cols=cols, count=count),
            (wide, part, shape(4 * cols, rows), shape(count, count),
             jax.ShapeDtypeStruct((face, face), BF16)),
        )(first, local, scal, nm_row, sl0, sr0, t1, sl2, sr2, w0)
        w1, sl, sr = call(precondition_kernel, (part, part, part))(
            ul, ur, *near, mask, w1c, schur_p
        )
        near = exchange(sl, sr)
        size = up(13 * cols, 8 * n_red)
        second, field = call(
            lambda *refs: early_kernel(*refs, cols=cols, count=count),
            (shape(size, LANE), shape(4 * cols, rows)),
        )(scal, z0, z1, ul, ur, r1, w0, w1, base, mass_p, prev_p)
        second, field, m = call(
            lambda *refs: combine_kernel(*refs, cols=cols, count=count),
            (shape(size, LANE), shape(4 * cols, rows), part),
        )(second, field, sl, sr, *near, mask, n0, inv_p, scal, r1, w0, w1, mass_p, prev_p)
        second = over_all(second, n_red, n_z)
        block, multi, coefficients, factor = call(
            lambda *refs: final_kernel(*refs, cols=cols, count=count),
            (shape(cols, rows), shape(cols, face), shape(cols, count), shape(cols, cols)),
        )(second, gram, scal, field, z0, z1, m, prev_t, back)
        return block.T[None, None], multi.T[None, None], coefficients.T, factor

    split = (along, ("x", "c"))
    return jax.shard_map(
        on_device,
        mesh=fine,
        in_specs=(
            P(*split, None, None),
            P(*split, None, None),
            P(*split, None, None),
            P(*split, None),
            P(),
            P(*split, None),
            P(*split, None, None),
            P(*split, None, None),
            P(*split, None),
        ),
        out_specs=(P(*split, None, None), P(*split, None, None), P(), P()),
        check_vma=False,
    )
```

```python
import jax
import jax.numpy as jnp
import numpy as np
from jax import lax
from jax.experimental import pallas as pl
from jax.experimental.pallas import tpu as pltpu
from jax.sharding import Mesh, PartitionSpec as P

HI = lax.Precision.HIGHEST
F32 = jnp.float32
BF16 = jnp.bfloat16
RED = ("y", "zl", "x", "c")
LEVELS = 3
LANE = 128


def nn(a, b):
    return jnp.dot(a, b, precision=HI, preferred_element_type=F32)


def nt(a, b):
    return lax.dot_general(
        a, b, (((1,), (1,)), ((), ())), precision=HI, preferred_element_type=F32
    )


def lane_sum(a):
    return jnp.sum(a, axis=1, keepdims=True)


def call(kernel, outs):
    return pl.pallas_call(
        kernel,
        out_shape=outs,
        compiler_params=pltpu.CompilerParams(vmem_limit_bytes=12 * 1024 * 1024),
    )


def pieces_of(t, parts, axis):
    pieces = []
    for _ in range(parts - 1):
        pieces.append(t.astype(BF16).astype(F32))
        t = t - pieces[-1]
    return jnp.concatenate(pieces + [t], axis=axis).astype(BF16)


def split_dot(t, mat, parts=2):
    wide = jnp.dot(pieces_of(t, parts, 0), mat, preferred_element_type=F32)
    rows = t.shape[0]
    return sum(wide[i * rows : (i + 1) * rows] for i in range(1, parts)) + wide[:rows]


def split_nt(t, mat):
    rows = t.shape[0]
    wide = lax.dot_general(
        pieces_of(t, 3, 0), mat, (((1,), (1,)), ((), ())), preferred_element_type=F32
    )
    return wide[2 * rows :] + wide[rows : 2 * rows] + wide[:rows]


def split_right(mat, t):
    cols = t.shape[1]
    wide = jnp.dot(mat, pieces_of(t, 3, 1), preferred_element_type=F32)
    return wide[:, 2 * cols :] + wide[:, cols : 2 * cols] + wide[:, :cols]


def to_order(nm_row, face):
    nm = jnp.transpose(jnp.broadcast_to(nm_row.astype(F32), (8, face)))[:, 0:1]
    return (nm == lax.broadcasted_iota(jnp.int32, (face, face), 1).astype(F32)).astype(F32)


def from_order(nm_row, face):
    return (nm_row == lax.broadcasted_iota(jnp.int32, (face, face), 0)).astype(F32)


def start_kernel(inv_hbm, load_hbm, basis_hbm, nm_hbm, corner_hbm, sl_ref, sr_ref, cl_ref,
                 inv_ref, load_ref, basis_ref, nm_ref, corner_ref, sems):
    pairs = (
        (nm_hbm, nm_ref), (load_hbm, load_ref), (basis_hbm, basis_ref), (corner_hbm, corner_ref),
        (inv_hbm, inv_ref),
    )
    copies = [pltpu.make_async_copy(src, dst, sems.at[i]) for i, (src, dst) in enumerate(pairs)]
    for copy in copies:
        copy.start()
    for copy in copies[:-1]:
        copy.wait()
    face = nm_ref.shape[1]
    cols = load_ref.shape[0]
    corners = basis_ref.shape[0]
    rows = cols + corners
    load = load_ref[...]
    basis = basis_ref[...]
    order = to_order(nm_ref[...], face).astype(BF16)
    cl_ref[...] = nt(load, basis)
    for ref in (sl_ref, sr_ref):
        ref[rows : rows + 8, :] = jnp.zeros((8, face), F32)
        ref[rows : rows + 1, 0:corners] = corner_ref[...].astype(F32)
    sr_ref[cols:rows, :] = basis[:, face:]
    copies[-1].wait()
    wide = split_dot(load, inv_ref[...])
    sr_ref[0:cols, :] = wide[:, face:]
    left = [wide[:, :face], basis[:, :face], jnp.zeros((8, face), F32)]
    left = split_dot(jnp.concatenate(left, axis=0), order, 3)
    sl_ref[0:rows, :] = left[0:rows]


def matrix_kernel(src, nm_ref, dst):
    face = nm_ref.shape[1]
    order = to_order(nm_ref[...], face).astype(BF16)
    back = from_order(nm_ref[...], face).astype(BF16)
    dst[:, face:] = src[:, face:]
    dst[:, :face] = jnp.dot(src[:, :face], order, preferred_element_type=F32).astype(BF16)
    dst[:face, :] = jnp.dot(back, dst[:face, :], preferred_element_type=F32).astype(BF16)


def basis_kernel(prev_ref, nm_ref, mass_ref, prev_out, flip_out, mass_out, *, total):
    face = nm_ref.shape[1]
    back = from_order(nm_ref[...], face).astype(BF16)
    prev_out[face:, :] = prev_ref[face:, :]
    prev_out[:face, :] = jnp.dot(back, prev_ref[:face, :], preferred_element_type=F32).astype(BF16)
    flip_out[...] = jnp.transpose(prev_out[...].astype(F32)).astype(BF16)
    mass = mass_ref[...] / total
    mass_out[:, face:] = mass[:, face:]
    left = jnp.broadcast_to(mass[:, :face], (8, face))
    mass_out[:, :face] = nn(left, to_order(nm_ref[...], face))[0:1]


def gram_kernel(prev_ref, mass_ref, gram_out, *, total):
    mass = mass_ref[...] / total
    column = jnp.transpose(jnp.broadcast_to(mass, (8, mass.shape[1])))[:, 0:1]
    wide = prev_ref[...].astype(F32)
    gram_out[...] = lax.dot_general(
        wide * column, wide, (((0,), (0,)), ((), ())), precision=HI, preferred_element_type=F32
    )


def step_kernel(sl_ref, sr_ref, nl_ref, pr_ref, mask_ref, mat_ref, t_ref, ol_ref, or_ref,
                *, cols, width, scale):
    face = sl_ref.shape[1]
    new = width + 16
    rows = cols + new
    old = cols + width
    for lanes, own, other, shift in (
        (slice(0, face), sl_ref, pr_ref, 0),
        (slice(face, 2 * face), sr_ref, nl_ref, 16),
    ):
        keep = mask_ref[0:1, lanes]
        t_ref[0:cols, lanes] = (own[0:cols, :] - other[0:cols, :]) * keep
        edge = jnp.zeros((8, face), F32)
        mine = jnp.concatenate([edge, own[cols:old, :], edge], axis=0)
        blank = jnp.zeros((16, face), F32)
        theirs = other[cols:old, :]
        theirs = jnp.concatenate([theirs, blank] if shift == 0 else [blank, theirs], axis=0)
        t_ref[cols:rows, lanes] = (mine - theirs) * keep
    v = split_dot(t_ref[...], mat_ref[...])
    if scale != 1.0:
        v = v * scale
    ids = jnp.concatenate(
        [
            pr_ref[old : old + 8, 0:8],
            sl_ref[old : old + 8, 0:width],
            nl_ref[old : old + 8, width - 8 : width],
        ],
        axis=1,
    )
    for ref, lanes in ((ol_ref, slice(0, face)), (or_ref, slice(face, 2 * face))):
        ref[0:rows, :] = v[:, lanes]
        ref[rows : rows + 8, :] = jnp.zeros((8, face), F32)
        ref[rows : rows + 8, 0:new] = ids


def one_hot(ids, count):
    dof = lax.broadcasted_iota(jnp.int32, (count, ids.shape[1]), 0).astype(F32)
    return (ids == dof).astype(F32).astype(BF16)


def lower(half):
    row = lax.broadcasted_iota(jnp.int32, (half, half), 0)
    col = lax.broadcasted_iota(jnp.int32, (half, half), 1)
    return row, col


def pack(ref, k, matrix, diagonals):
    half = LANE
    at = 2 * half * k
    row, col = lower(half)
    last = matrix[half:, half:]
    ref[at : at + half, :] = jnp.where(row >= col, matrix[:half, :half], last)
    ref[at + half : at + 2 * half, :] = matrix[half:, :half]
    ref[diagonals + k : diagonals + k + 1, :] = jnp.sum(
        jnp.where(row == col, last, 0.0), axis=0, keepdims=True
    )


def unpack(ref, k, diagonals):
    half = LANE
    at = 2 * half * k
    row, col = lower(half)
    shared = ref[at : at + half, :]
    flipped = jnp.transpose(shared)
    cross = ref[at + half : at + 2 * half, :]
    first = jnp.where(row >= col, shared, flipped)
    last = jnp.where(row < col, shared, flipped)
    last = jnp.where(row == col, ref[diagonals + k : diagonals + k + 1, :], last)
    return jnp.concatenate(
        [
            jnp.concatenate([first, jnp.transpose(cross)], axis=1),
            jnp.concatenate([cross, last], axis=1),
        ],
        axis=0,
    )


def level_moments(out, refs, k, cols, count):
    base = 4 * count
    t_ref, l_ref, r_ref = refs
    rows, double = t_ref.shape
    face = double // 2
    width = rows - cols
    spot = one_hot(l_ref[rows : rows + 1, 0:width], count)
    tl, tr = t_ref[cols:rows, :face], t_ref[cols:rows, face:]
    inner = split_nt(nt(l_ref[0:rows, :], tl) + nt(r_ref[0:rows, :], tr), spot)
    put(out, base + 2 * cols * (k + 1), inner[0:cols])
    pack(out, k, split_right(spot, inner[cols:rows]), base + 9 * cols)
    return lane_sum(t_ref[0:cols, :face] * l_ref[0:cols, :]) + lane_sum(
        t_ref[0:cols, face:] * r_ref[0:cols, :]
    )


def put(out, at, block):
    cols, half = block.shape[0], block.shape[1] // 2
    out[at : at + cols, :] = block[:, :half]
    out[at + cols : at + 2 * cols, :] = block[:, half:]


def in_lanes(items, start=0):
    cols = items[0].shape[0]
    lane = lax.broadcasted_iota(jnp.int32, (cols, LANE), 1)
    block = jnp.zeros((cols, LANE), F32)
    for k, item in enumerate(items):
        block = jnp.where(lane == start + k, item, block)
    return block


def moment_kernel(sl0_ref, cl_ref, gram_ref, *refs, cols, count):
    out = refs[-1]
    base = 4 * count
    at = base + 8 * cols
    out[at:, :] = jnp.zeros((out.shape[0] - at, LANE), F32)
    own = sl0_ref.shape[0] - cols - 8
    spot = one_hot(sl0_ref[cols + own : cols + own + 1, 0:own], count)
    put(out, base, split_nt(cl_ref[...], spot))
    sums = [level_moments(out, refs[3 * k : 3 * k + 3], k, cols, count) for k in range(2)]
    pack(out, 3, gram_ref[...], at + cols)
    out[at : at + cols, :] = in_lanes(sums)


def last_moment_kernel(given_ref, *refs, cols, count):
    out = refs[-1]
    out[...] = given_ref[...]
    total = level_moments(out, refs[:3], 2, cols, count)
    at = 4 * count + 8 * cols
    out[at : at + cols, :] = given_ref[at : at + cols, :] + in_lanes([total], 2)


def vector(sums_ref, k, cols, count):
    at = 4 * count + 2 * cols * k
    return jnp.concatenate([sums_ref[at : at + cols, :], sums_ref[at + cols : at + 2 * cols, :]], axis=1)


def at_corners(values, ids_ref):
    rows = ids_ref.shape[0]
    spot = one_hot(ids_ref[rows - 8 : rows - 7, 0:LANE], values.shape[1])
    return split_dot(values, spot, 3)


def spread(local, k, ref, lanes, cols):
    width = 8 * (2 * k + 1)
    lane = 8 * (LEVELS - k)
    wide = nn(local[:, lane : lane + width], ref[cols : cols + width, lanes])
    return [wide[i : i + cols] for i in range(0, wide.shape[0], cols)]


def coarse_kernel(sums_ref, coarse_ref, mat_ref, t1, t3, sl3, ol_ref, or_ref, w0_ref,
                  *, cols, count):
    diagonals = 4 * count + 9 * cols
    face = ol_ref.shape[1]
    every = slice(0, 2 * face)
    g0 = nn(vector(sums_ref, 0, cols, count), coarse_ref[...])
    g1 = nn(vector(sums_ref, 1, cols, count) + nn(g0, unpack(sums_ref, 0, diagonals)), coarse_ref[...])
    local = at_corners(jnp.concatenate([g0, g1], axis=0), sl3)
    (p30,) = spread(local[0:cols], 3, t3, every, cols)
    (p11,) = spread(local[cols:], 1, t1, every, cols)
    w0 = t3[0:cols, :] + p30 + p11
    w0_ref[...] = w0
    v = split_dot(w0, mat_ref[...]) * 0.25
    ol_ref[...] = v[:, :face]
    or_ref[...] = v[:, face:]


def values_kernel(sums_ref, coarse_ref, t2, sl3, z0_ref, local_ref, scal_ref, *, cols, count):
    diagonals = 4 * count + 9 * cols
    m0, m1, m2 = (unpack(sums_ref, k, diagonals) for k in range(3))
    coarse = coarse_ref[...]
    c_load, w0x, w1x, w2x = (vector(sums_ref, k, cols, count) for k in range(4))
    at = 4 * count + 8 * cols
    s0, s1, s2 = (sums_ref[at : at + cols, k : k + 1] for k in range(3))
    g0 = nn(c_load, coarse)
    m0g0, m1g0, m2g0 = nn(g0, m0), nn(g0, m1), nn(g0, m2)
    c0 = w0x + m0g0
    g1 = nn(c0, coarse)
    m0g1, m1g1 = nn(g1, m0), nn(g1, m1)
    rz0 = s0 + lane_sum(2.0 * w0x * g0 + g0 * m0g0)
    del0 = s1 + lane_sum(2.0 * w1x * g0 + g0 * m1g0 + c0 * g1)
    nu0 = s2 + lane_sum(2.0 * w2x * g0 + g0 * m2g0 + 2.0 * w1x * g1 + 2.0 * g1 * m1g0 + g1 * m0g1)
    al0 = rz0 / del0
    be1 = (rz0 - 2.0 * al0 * del0 + al0 * al0 * nu0) / rz0
    cz1 = c0 - al0 * (w1x + m1g0 + m0g1)
    gz1 = nn(cz1, coarse)
    cm = (
        (1.0 + be1) * (w1x + m1g0)
        - al0 * (m1g1 + w2x + m2g0)
        + nn(gz1, m0)
        + be1 * m0g1
    )
    gm = nn(cm, coarse)
    local = at_corners(jnp.concatenate([g0, g1, gz1, gm], axis=0), sl3)
    local_ref[...] = local
    (p20,) = spread(local[0:cols], 2, t2, slice(0, t2.shape[1]), cols)
    z0_ref[...] = t2[0:cols, :] + p20
    scal_ref[...] = in_lanes([al0, be1, lane_sum(cm * gm)])


def base_kernel(sums_ref, local_ref, scal_ref, nm_ref, sl0, sr0, t1, sl2, sr2, w0_ref,
                w1c_ref, r1_ref, field_ref, gram_ref, back_ref, *, cols, count):
    diagonals = 4 * count + 9 * cols
    face = sl0.shape[1]
    local = local_ref[...]
    al0 = scal_ref[:, 0:1]
    every, right, whole = slice(0, 2 * face), slice(face, 2 * face), slice(0, face)
    (p10,) = spread(local[0:cols], 1, t1, right, cols)
    (w1c_ref[...],) = spread(local[2 * cols : 3 * cols], 1, t1, every, cols)
    r1_ref[...] = t1[0:cols, right] + p10 - al0 * w0_ref[:, right]
    for own, u, lanes in ((sl0, sl2, slice(0, face)), (sr0, sr2, right)):
        corner = spread(local, 0, own, whole, cols)
        (u0,) = spread(local[0:cols], 2, u, whole, cols)
        field_ref[0:cols, lanes] = own[0:cols, :] + corner[0]
        field_ref[cols : 2 * cols, lanes] = u[0:cols, :] + u0 + corner[1]
        field_ref[2 * cols : 3 * cols, lanes] = corner[2]
        field_ref[3 * cols : 4 * cols, lanes] = corner[3]
    gram_ref[...] = unpack(sums_ref, 3, diagonals)
    back_ref[...] = from_order(nm_ref[...], face).astype(BF16)


def joined(own_ref, other_ref, mask_ref, left):
    face = own_ref.shape[1]
    lanes = slice(0, face) if left else slice(face, 2 * face)
    return (own_ref[...] - other_ref[...]) * mask_ref[0:1, lanes]


def field_of(sl_ref, sr_ref, nl_ref, pr_ref, mask_ref):
    return jnp.concatenate(
        [joined(sl_ref, pr_ref, mask_ref, True), joined(sr_ref, nl_ref, mask_ref, False)], axis=1
    )


def dual_kernel(sl_ref, sr_ref, nl_ref, pr_ref, mask_ref, z0_ref, scal_ref, mat_ref,
                n0_ref, z1_ref, ol_ref, or_ref):
    face = sl_ref.shape[1]
    n0 = field_of(sl_ref, sr_ref, nl_ref, pr_ref, mask_ref)
    z1 = z0_ref[...] - scal_ref[:, 0:1] * n0
    n0_ref[...] = n0
    z1_ref[...] = z1[:, face:]
    u = split_dot(z1, mat_ref[...])
    ol_ref[...] = u[:, :face]
    or_ref[...] = u[:, face:]


def precondition_kernel(sl_ref, sr_ref, nl_ref, pr_ref, mask_ref, w1c_ref, mat_ref,
                        w1_ref, ol_ref, or_ref):
    face = sl_ref.shape[1]
    w1 = field_of(sl_ref, sr_ref, nl_ref, pr_ref, mask_ref) + w1c_ref[...]
    w1_ref[...] = w1[:, face:]
    v = split_dot(w1, mat_ref[...]) * 0.25
    ol_ref[...] = v[:, :face]
    or_ref[...] = v[:, face:]


def early_kernel(scal_ref, z0_ref, z1_ref, ul_ref, ur_ref, r1_ref, w0_ref, w1_ref, base_ref,
                 mass_ref, prev_ref, out_ref, field_ref, *, cols, count):
    half = count // 2
    face = ul_ref.shape[1]
    third = slice(2 * cols, 3 * cols)
    field_ref[0 : 2 * cols, :] = base_ref[0 : 2 * cols, :]
    field_ref[third, 0:face] = base_ref[third, 0:face] + ul_ref[...]
    field_ref[third, face:] = base_ref[third, face:] + ur_ref[...]
    field_ref[3 * cols :, :] = base_ref[3 * cols :, :]
    be1 = scal_ref[:, 1:2]
    z0, w0 = z0_ref[:, face:], w0_ref[:, face:]
    z1, w1, r1 = z1_ref[...], w1_ref[...], r1_ref[...]
    q1 = w1 + be1 * w0
    out_ref[...] = jnp.zeros(out_ref.shape, F32)
    out_ref[12 * cols : 13 * cols, :] = in_lanes([
        lane_sum(r1 * z1), lane_sum(q1 * z1), lane_sum(r1 * (z1 + be1 * z0)),
        lane_sum((z1 + be1 * z0) * q1), lane_sum(z1 * w1),
    ])
    known = field_ref[0 : 3 * cols, :]
    scaled = known * mass_ref[...]
    tq = split_dot(scaled, prev_ref[...], 3)
    out_ref[0 : 3 * cols, :] = tq[:, :half]
    out_ref[4 * cols : 7 * cols, :] = tq[:, half:]
    out_ref[8 * cols : 11 * cols, 0 : 3 * cols] = nt(scaled, known)


def combine_kernel(given_ref, known_ref, sl_ref, sr_ref, nl_ref, pr_ref, mask_ref, n0_ref, mat_ref,
                   scal_ref, r1_ref, w0_ref, w1_ref, mass_ref, prev_ref,
                   out_ref, field_ref, m_ref, *, cols, count):
    half = count // 2
    face = sl_ref.shape[1]
    be1 = scal_ref[:, 1:2]
    out_ref[...] = given_ref[...]
    field_ref[0 : 3 * cols, :] = known_ref[0 : 3 * cols, :]
    whole = field_of(sl_ref, sr_ref, nl_ref, pr_ref, mask_ref) + be1 * n0_ref[...]
    u = split_dot(whole, mat_ref[...])
    last = known_ref[3 * cols :, :] + u
    field_ref[3 * cols :, :] = last
    m = whole[:, face:]
    m_ref[...] = m
    w0, w1 = w0_ref[:, face:], w1_ref[...]
    scaled = last * mass_ref[...]
    tq = split_dot(scaled, prev_ref[...], 3)
    out_ref[3 * cols : 4 * cols, :] = tq[:, :half]
    out_ref[7 * cols : 8 * cols, :] = tq[:, half:]
    out_ref[11 * cols : 12 * cols, :] = nt(scaled, field_ref[...])
    at = 12 * cols
    out_ref[at : at + cols, :] = given_ref[at : at + cols, :] + in_lanes([
        lane_sum(r1_ref[...] * m), lane_sum((w1 + be1 * w0) * m), lane_sum(m * w1),
        lane_sum(whole * u),
    ], 5)


def final_kernel(sums_ref, basis_ref, scal_ref, field_ref, z0_ref, z1_ref, m_ref, prev_ref, back_ref,
                 block_ref, multi_ref, coef_ref, factor_ref, *, cols, count):
    half = count // 2
    face = m_ref.shape[1]
    at = 12 * cols
    r1z1, q1z1, r1p1, p1q1, z1w1, r1m, q1m, mw1, mm = (
        sums_ref[at : at + cols, k : k + 1] for k in range(9)
    )
    al0, be1, extra = (scal_ref[:, k : k + 1] for k in range(3))
    mfm = mm + extra
    al1 = r1p1 / p1q1
    z2q1 = q1z1 - al1 * q1m
    be2 = -z2q1 / p1q1
    rz2 = r1z1 - al1 * (r1m + q1z1) + al1 * al1 * q1m
    z2fz2 = z1w1 - 2.0 * al1 * mw1 + al1 * al1 * mfm
    al2 = rz2 / (z2fz2 + 2.0 * be2 * z2q1 + be2 * be2 * p1q1)
    along = al1 + al2 * be2
    parts = (al0 + along * be1, along + al2, -al1 * al2)
    duals = (z0_ref[:, face:], z1_ref[...], m_ref[...])
    multi_ref[...] = sum(y * dual for y, dual in zip(parts, duals))
    weights = [jnp.ones((cols, 1), F32)] + [-y for y in parts]
    primal = sum(y * field_ref[i * cols : (i + 1) * cols, :] for i, y in enumerate(weights))
    g1 = sum(
        y
        * jnp.concatenate(
            [sums_ref[i * cols : (i + 1) * cols, :], sums_ref[(4 + i) * cols : (5 + i) * cols, :]],
            axis=1,
        )
        for i, y in enumerate(weights)
    )
    row = lax.broadcasted_iota(jnp.int32, (cols, cols), 0)
    col = lax.broadcasted_iota(jnp.int32, (cols, cols), 1)
    eye = (row == col).astype(F32)
    stacked = jnp.concatenate(weights, axis=0)
    across = jnp.concatenate([jnp.sum(y * eye, axis=0, keepdims=True) for y in weights], axis=1)
    tiles = stacked * sums_ref[8 * cols : 12 * cols, :] * across
    cross = tiles[3 * cols :]
    cross = sum(cross[:, j * cols : (j + 1) * cols] for j in range(3))
    tiles = sum(tiles[i * cols : (i + 1) * cols] for i in range(4))
    gram = sum(tiles[:, j * cols : (j + 1) * cols] for j in range(4))
    gram = gram + jnp.transpose(cross)
    basis = basis_ref[...]
    c = 2.0 * g1 - nn(g1, basis)
    coef_ref[...] = c
    gram = gram + nt(c, nn(c, basis) - 2.0 * g1)
    gram = 0.5 * (gram + jnp.transpose(gram))
    final = primal - split_dot(c, prev_ref[...], 3)
    work = jnp.concatenate([gram, eye], axis=1)
    index = lax.broadcasted_iota(jnp.int32, (cols, 1), 0)
    pivots = jnp.zeros(work.shape, F32)
    for start in range(0, cols, 8):
        wide = [jnp.broadcast_to(work[:, start + j : start + j + 1], work.shape) for j in range(8)]
        for j in range(8):
            k = start + j
            pivot = wide[j][k : k + 1, :]
            pivots = jnp.where(index == k, pivot, pivots)
            times = jnp.where(index > k, wide[j], 0.0) * (1.0 / pivot)
            for i in range(j + 1, 8):
                wide[i] = wide[i] - times * wide[i][k : k + 1, :]
            work = work - times * work[k : k + 1, :]
    work = work / jnp.sqrt(pivots)
    factor_ref[...] = jnp.transpose(jnp.where(row <= col, work[:, :cols], 0.0))
    solved = nn(work[:, cols:], final)
    left = split_dot(solved[:, :face], back_ref[...], 3)
    block_ref[:, :face] = left
    block_ref[:, face:] = solved[:, face:]


def sum_kernel(parts_ref, out_ref):
    total = jnp.sum(parts_ref[...], axis=0)
    for i in range(out_ref.shape[0]):
        out_ref[i] = total


def swap(parts, axes):
    return lax.all_to_all(parts, axes, 0, 0, tiled=True)


def summed(parts, copies):
    return call(sum_kernel, jax.ShapeDtypeStruct((copies,) + parts.shape[1:], F32))(parts)


def over_all(rows, n_red, n_z):
    parts = swap(rows.reshape(n_red, rows.shape[0] // n_red, LANE), RED)
    parts = swap(summed(parts, n_z), "zh")
    return swap(summed(parts, n_red), RED).reshape(rows.shape)


def up(count, unit):
    return -(-count // unit) * unit


def solution(mesh):
    n_sub, n_grp = mesh.shape["sub"], mesh.shape["grp"]
    n_y = min(4, n_sub)
    n_zl, n_c = 2, 2
    n_z = n_sub // n_y // n_zl
    n_x = n_grp // n_c
    devices = np.asarray(mesh.devices).reshape(n_y, n_z, n_zl, n_x, n_c)
    fine = Mesh(devices, ("y", "zh", "zl", "x", "c"))
    n_red = n_y * n_zl * n_x * n_c
    along = ("y", "zh", "zl")
    ahead = [(i, i + 1) for i in range(n_sub - 1)]
    behind = [(i + 1, i) for i in range(n_sub - 1)]

    def on_device(schur_inverse, schur, coarse_basis, corner_index, coarse_inverse, neighbor_map,
                  load, previous, mass):
        inverse_block, schur_block, basis = schur_inverse[0, 0], schur[0, 0], coarse_basis[0, 0]
        corners, nm = corner_index[0, 0], neighbor_map[0, 0]
        rhs, earlier, weights = load[0, 0].T, previous[0, 0], mass[0, 0]
        cols, rows = rhs.shape
        face = nm.shape[0]
        count = coarse_inverse.shape[0]
        total = rows * n_sub * n_grp
        own = corners.shape[0]
        position = lax.axis_index(along)
        nm_row = nm[None, :]
        side = jnp.arange(2 * face) < face
        mask = jnp.where(side, position > 0, position < n_sub - 1).astype(F32)[None, :]
        mask = jnp.broadcast_to(mask, (8, 2 * face))

        def shape(*dims):
            return jax.ShapeDtypeStruct(dims, F32)

        half = shape(cols + own + 8, face)
        sl, sr, cl = pl.pallas_call(
            start_kernel,
            out_shape=(half, half, shape(cols, own)),
            in_specs=[pl.BlockSpec(memory_space=pl.ANY)] * 5,
            scratch_shapes=[
                pltpu.VMEM((rows, rows), BF16),
                pltpu.VMEM((cols, rows), F32),
                pltpu.VMEM((own, rows), F32),
                pltpu.VMEM((1, face), jnp.int32),
                pltpu.VMEM((1, own), jnp.int32),
                pltpu.SemaphoreType.DMA((5,)),
            ],
            compiler_params=pltpu.CompilerParams(vmem_limit_bytes=60 * 1024 * 1024),
        )(inverse_block, rhs, basis, nm_row, corners[None, :])
        square = jax.ShapeDtypeStruct((rows, rows), BF16)

        def exchange(sl, sr):
            return lax.ppermute(sl, along, behind), lax.ppermute(sr, along, ahead)

        def step(k, sl, sr, near, mat):
            width = own + 16 * (k - 1)
            out = cols + width + 16
            return call(
                lambda *refs: step_kernel(
                    *refs, cols=cols, width=width, scale=0.25 if k % 2 == 1 else 1.0
                ),
                (shape(out, 2 * face), shape(out + 8, face), shape(out + 8, face)),
            )(sl, sr, *near, mask, mat)

        chain = [sl, sr]
        near = exchange(sl, sr)
        schur_p = call(matrix_kernel, square)(schur_block, nm_row)
        gram = call(lambda *refs: gram_kernel(*refs, total=total), shape(count, count))(
            earlier, weights[None, :]
        )
        near, gram = lax.optimization_barrier((near, gram))
        t, sl, sr = step(1, sl, sr, near, schur_p)
        chain += [t, sl, sr]
        near = exchange(sl, sr)
        inv_p = call(matrix_kernel, square)(inverse_block, nm_row)
        t, sl, sr = step(2, sl, sr, near, inv_p)
        chain += [t, sl, sr]
        near = exchange(sl, sr)
        size = up(4 * count + 9 * cols + 8, 8 * n_red)
        first = call(
            lambda *refs: moment_kernel(*refs, cols=cols, count=count), shape(size, LANE)
        )(chain[0], cl, gram, *chain[2:8])
        t, sl, sr = step(3, sl, sr, near, schur_p)
        chain += [t, sl, sr]
        first = call(
            lambda *refs: last_moment_kernel(*refs, cols=cols, count=count),
            shape(size, LANE),
        )(first, t, sl, sr)
        first = over_all(first, n_red, n_z)

        wide, part = shape(cols, 2 * face), shape(cols, face)
        sl0, sr0, t1, _, _, t2, sl2, sr2, t3, sl3, _ = chain
        sl, sr, w0 = call(
            lambda *refs: coarse_kernel(*refs, cols=cols, count=count), (part, part, wide)
        )(first, coarse_inverse, schur_p, t1, t3, sl3)
        z0, local, scal = call(
            lambda *refs: values_kernel(*refs, cols=cols, count=count),
            (wide, shape(4 * cols, LANE), shape(cols, LANE)),
        )(first, coarse_inverse, t2, sl3)
        near = exchange(sl, sr)
        n0, z1, ul, ur = call(dual_kernel, (wide, part, part, part))(
            sl, sr, *near, mask, z0, scal, inv_p
        )
        near = exchange(ul, ur)
        late, ul = lax.optimization_barrier((earlier, ul))
        prev_p, prev_t, mass_p = call(
            lambda *refs: basis_kernel(*refs, total=total),
            (
                jax.ShapeDtypeStruct(earlier.shape, BF16),
                jax.ShapeDtypeStruct(earlier.shape[::-1], BF16),
                shape(1, rows),
            ),
        )(late, nm_row, weights[None, :])
        near, prev_p = lax.optimization_barrier((near, prev_p))
        w1c, r1, base, gram, back = call(
            lambda *refs: base_kernel(*refs, cols=cols, count=count),
            (wide, part, shape(4 * cols, rows), shape(count, count),
             jax.ShapeDtypeStruct((face, face), BF16)),
        )(first, local, scal, nm_row, sl0, sr0, t1, sl2, sr2, w0)
        w1, sl, sr = call(precondition_kernel, (part, part, part))(
            ul, ur, *near, mask, w1c, schur_p
        )
        near = exchange(sl, sr)
        size = up(13 * cols, 8 * n_red)
        second, field = call(
            lambda *refs: early_kernel(*refs, cols=cols, count=count),
            (shape(size, LANE), shape(4 * cols, rows)),
        )(scal, z0, z1, ul, ur, r1, w0, w1, base, mass_p, prev_p)
        second, field, m = call(
            lambda *refs: combine_kernel(*refs, cols=cols, count=count),
            (shape(size, LANE), shape(4 * cols, rows), part),
        )(second, field, sl, sr, *near, mask, n0, inv_p, scal, r1, w0, w1, mass_p, prev_p)
        second = over_all(second, n_red, n_z)
        block, multi, coefficients, factor = call(
            lambda *refs: final_kernel(*refs, cols=cols, count=count),
            (shape(cols, rows), shape(cols, face), shape(cols, count), shape(cols, cols)),
        )(second, gram, scal, field, z0, z1, m, prev_t, back)
        return block.T[None, None], multi.T[None, None], coefficients.T, factor

    split = (along, ("x", "c"))
    return jax.shard_map(
        on_device,
        mesh=fine,
        in_specs=(
            P(*split, None, None),
            P(*split, None, None),
            P(*split, None, None),
            P(*split, None),
            P(),
            P(*split, None),
            P(*split, None, None),
            P(*split, None, None),
            P(*split, None),
        ),
        out_specs=(P(*split, None, None), P(*split, None, None), P(), P()),
        check_vma=False,
    )
```
